512 devices in a mesh: gx: 16 (over x_hi, y), gy: 8 (over z), gz: 4 (over x_lo, core).
Axes of the slice: x: 4 (x_hi: 2, x_lo: 2; x = x_hi * 2 + x_lo), y: 8, z: 8, core: 2. Of those that a mesh axis runs over, the one named last changes fastest.
Arguments:
- features: float32 [32, 16, 8, 8, 128], P('gx', 'gy', 'gz'), may hold values from -6 to 6
- offsets: float32 [32, 16, 8, 3, 8], P('gx', 'gy', 'gz'), may hold values from 0 to 1
- counts: int32 [32, 16, 8], P('gx', 'gy', 'gz'), may hold values from 0 to 8, as said below
- species: int32 [32, 16, 8, 8], P('gx', 'gy', 'gz'), may hold values from 0 to 7
- neighbours: int32 [32, 16, 8, 8, 32], P('gx', 'gy', 'gz'), may hold values from 0 to 215, as said below
- w_radial: float32 [8, 128], replicated, may hold values from -2 to 2
- w_vector: float32 [8, 128], replicated, may hold values from -2 to 2
- w_mix: float32 [128, 128], replicated, may hold values from -0.5 to 0.5
- w_out: float32 [128], replicated, may hold values from -0.5 to 0.5
- w_charge: float32 [128, 16], replicated, may hold values from -0.5 to 0.5
- species_shift: float32 [8], replicated, may hold values from -4 to 4
Outputs:
- atom_energy: float32 [32, 16, 8, 8], P('gx', 'gy', 'gz')
- forces: float32 [32, 16, 8, 3, 8], P('gx', 'gy', 'gz')
The draws below stay inside these ranges and needn't reach their ends.
Inputs may be any that keep to these rules, and one draw needn't show every extreme that they name: `counts`: at most 8 atoms in a cell and some cell holds exactly 8; the live atoms of a cell fill its first slots; the mean count differs strongly from domain to domain. `neighbours`: entries index the 27 cells around the atom's cell times 8 slots; an atom never lists its own slot; entries may name empty slots and may repeat.
All inputs are finite; a program needn't handle non-finite values.
Results may differ from the reference program's by a relative error of at most 0.0003.
Values sent between devices are 32-bit elements; how exact they have to be, the bound alone decides.
No kernel may reach another device: no remote copies, remote signals or barrier semaphores. Data moves between devices by JAX's collectives and lax.ppermute only.
A program may use at most 64 MiB of HBM per device.

```python
import math
import jax
import jax.numpy as jnp
from jax import lax

C = 128
Q = 16
KX = 16
KY = 8
KZ = 8
NB = 8
NS = 8
K = 32
P_SIZE = 8
CX = 2
CY = 2
CZ = 2
NX = 32
NY = 16
NZ = 8
N_GX = 16
N_GY = 8
N_GZ = 4


def draw_counts(key, part):
    key = jax.random.fold_in(key, 11)
    key_dense, key_level, key_fill = jax.random.split(key, 3)
    domains = (NX // CX, NY // CY, NZ // CZ)
    dense = jax.random.randint(key_dense, domains, 0, 8) == 0
    halfway = max(P_SIZE // 2, 1)
    level = jnp.where(dense, P_SIZE, jax.random.randint(key_level, domains, 1, halfway + 1))
    level = jnp.repeat(jnp.repeat(jnp.repeat(level, CX, 0), CY, 1), CZ, 2)
    drawn = jax.random.randint(key_fill, (NX, NY, NZ), 0, 2 * level + 1)
    filled = jnp.minimum(drawn, P_SIZE)
    return filled.at[0, 0, 0].set(P_SIZE).astype(jnp.int32)


def draw_neighbours(key, part):
    key = jax.random.fold_in(key, 23)
    shape = (NX, NY, NZ, P_SIZE, K)
    raw_index = jax.random.randint(key, shape, 0, 27 * P_SIZE - 1)
    own_index = 13 * P_SIZE + lax.broadcasted_iota(jnp.int32, shape, 3)
    return (raw_index + (raw_index >= own_index).astype(jnp.int32)).astype(jnp.int32)


def set_ends(values, rng, least, high):
    longest = values.shape.index(max(values.shape))
    spots = []
    for shift in (0, 1):
        where = [jax.random.randint(jax.random.fold_in(rng, axis), (), 0, length) for axis, length in enumerate(values.shape)]
        where[longest] = (where[longest] + shift) % values.shape[longest]
        spots.append(tuple(where))
    return values.at[spots[0]].set(least).at[spots[1]].set(high)


def block_levels(rng, extent, shards, low, high):
    gain = 1.0
    for position, blocks in shards:
        heights = jax.random.uniform(jax.random.fold_in(jax.random.fold_in(rng, 6), position), (blocks,), jnp.float32, low / len(shards), high / len(shards))
        gain = gain * jnp.repeat(jnp.exp(heights), extent[position] // blocks).reshape((-1,) + (1,) * (len(extent) - 1 - position))
    return gain


def noise(own_key, shape, deviation, reach, cuts=(), kind=jnp.bfloat16):
    loudness = block_levels(own_key, shape, cuts, -0.22, 0.18) if cuts else 1.0
    entries = jax.random.normal(own_key, shape, jnp.float32) * deviation * loudness
    return jnp.minimum(jnp.maximum(entries, -reach), reach).astype(kind)


def setup_inputs(seed: int = 0) -> dict:
    seeds = jax.random.split(jax.random.key(seed), 12)
    return {
        "features": noise(seeds[0], (NX, NY, NZ, P_SIZE, C), 1.0, 6.0, ((0, 16), (1, 8), (2, 4)), jnp.float32),
        "offsets": jnp.clip(1.0 * jax.random.uniform(seeds[1], (NX, NY, NZ, 3, P_SIZE), jnp.float32) ** block_levels(seeds[1], (NX, NY, NZ, 3, P_SIZE), ((0, 16), (1, 8), (2, 4)), -0.2, 0.2), 0.0, 1.0),
        "counts": draw_counts(jax.random.fold_in(seeds[11], 71), 0),
        "species": set_ends(jax.random.randint(seeds[3], (NX, NY, NZ, P_SIZE), 0, NS), jax.random.fold_in(seeds[3], 1), 0, NS - 1).astype(jnp.int32),
        "neighbours": draw_neighbours(jax.random.fold_in(seeds[11], 71), 0),
        "w_radial": noise(seeds[5], (NB, C), NB ** -0.5, 2.0, (), jnp.float32),
        "w_vector": noise(seeds[6], (NB, C), NB ** -0.5, 2.0, (), jnp.float32),
        "w_mix": noise(seeds[7], (C, C), C ** -0.5, 0.5, (), jnp.float32),
        "w_out": noise(seeds[8], (C,), C ** -0.5, 0.5, (), jnp.float32),
        "w_charge": noise(seeds[9], (C, Q), C ** -0.5, 0.5, (), jnp.float32),
        "species_shift": noise(seeds[10], (NS,), 1.0, 4.0, (), jnp.float32),
    }


HIGH = lax.Precision.HIGHEST

def wave_table(grid_x, grid_y, grid_z):
    number = jnp.arange(KX * KY * KZ, dtype=jnp.int32)
    index_x = (number // (KY * KZ) - KX // 2).astype(jnp.float32)
    index_y = (number // KZ % KY - KY // 2).astype(jnp.float32)
    index_z = (number % KZ - KZ // 2).astype(jnp.float32)
    waves = 2.0 * math.pi * jnp.stack([index_x / grid_x, index_y / grid_y, index_z / grid_z], 0)
    length_sq = lax.optimization_barrier(jnp.sum(waves * waves, 0))
    weights = jnp.exp(-0.5 * length_sq) / (length_sq + 1.0)
    return (waves, weights)

def short_range(pos_ext, feat_ext, occupied, neighbours, w_radial, w_vector, w_mix, w_out):
    extent_x, extent_y, extent_z, slots_cell, channels = feat_ext.shape
    listed = neighbours.shape[-1]
    stencil = neighbours // slots_cell
    within = neighbours % slots_cell
    step_x = stencil // 9
    step_y = stencil // 3 % 3
    step_z = stencil % 3
    cell_x = lax.broadcasted_iota(jnp.int32, neighbours.shape, 0)
    cell_y = lax.broadcasted_iota(jnp.int32, neighbours.shape, 1)
    cell_z = lax.broadcasted_iota(jnp.int32, neighbours.shape, 2)
    target = (((cell_x + step_x) * extent_y + cell_y + step_y) * extent_z + cell_z + step_z) * slots_cell + within
    target = target.reshape(-1, listed)
    others = feat_ext.reshape(-1, channels)[target]
    points = jnp.moveaxis(pos_ext, 3, 4).reshape(-1, 3)
    centre = jnp.moveaxis(pos_ext[1:-1, 1:-1, 1:-1], 3, 4).reshape(-1, 1, 3)
    crossing = jnp.stack([step_x - 1, step_y - 1, step_z - 1], -1).reshape(-1, listed, 3).astype(jnp.float32)
    vectors = crossing + points[target] - centre
    dist_sq = lax.optimization_barrier(jnp.sum(vectors * vectors, -1))
    envelope = (1.0 - dist_sq / 16.0) ** 2
    decays = 2.0 ** (jnp.arange(w_radial.shape[0], dtype=jnp.float32) - 4.0)
    basis = jnp.exp(-dist_sq[..., None] * decays)
    radial = jnp.einsum('akb,bc->akc', basis, w_radial, precision=HIGH) * envelope[..., None]
    angular = jnp.einsum('akb,bc->akc', basis, w_vector, precision=HIGH) * envelope[..., None]
    norm_scale = 1.0 / math.sqrt(listed)
    scalar = lax.optimization_barrier(jnp.sum(radial * others, 1)) * norm_scale
    vector = jnp.einsum('akd,akc->adc', vectors, angular * others, precision=HIGH) * norm_scale
    product = scalar + lax.optimization_barrier(jnp.sum(vector * vector, 1))
    mixed = jnp.dot(product, w_mix, precision=HIGH)
    own = feat_ext[1:-1, 1:-1, 1:-1].reshape(-1, channels)
    updated = own + jax.nn.silu(mixed)
    return jnp.dot(updated, w_out, precision=HIGH) * occupied.reshape(-1)

def structure_terms(centres, charges, waves):
    phase = jnp.dot(centres, waves, precision=HIGH)
    cosine = jnp.cos(phase)
    sine = jnp.sin(phase)
    part_cos = jnp.dot(charges.T, cosine, precision=HIGH)
    part_sin = jnp.dot(charges.T, sine, precision=HIGH)
    return (cosine, sine, part_cos, part_sin)

def ewald_terms(cosine, sine, charges, total_cos, total_sin, waves, weights, scale):
    field_cos = jnp.dot(charges, total_cos * weights, precision=HIGH)
    field_sin = jnp.dot(charges, total_sin * weights, precision=HIGH)
    long_range = 0.5 * scale * lax.optimization_barrier(jnp.sum(cosine * field_cos + sine * field_sin, 1))
    turning = scale * (cosine * field_sin - sine * field_cos)
    pull = jnp.dot(turning, waves.T, precision=HIGH)
    return (long_range, pull)

def fold_wrap(padded, axis_dim):
    size = padded.shape[axis_dim] - 2
    lower = lax.slice_in_dim(padded, 0, 1, axis=axis_dim)
    upper = lax.slice_in_dim(padded, size + 1, size + 2, axis=axis_dim)
    inner = lax.slice_in_dim(padded, 1, size + 1, axis=axis_dim)
    head = lax.slice_in_dim(inner, 0, 1, axis=axis_dim) + upper
    tail = lax.slice_in_dim(inner, size - 1, size, axis=axis_dim) + lower
    middle = lax.slice_in_dim(inner, 1, size - 1, axis=axis_dim)
    return jnp.concatenate([head, middle, tail], axis_dim)

def reference(features, offsets, counts, species, neighbours, w_radial, w_vector, w_mix, w_out, w_charge, species_shift):
    grid_x, grid_y, grid_z, slots_cell, channels = features.shape
    cells_x = grid_x // N_GX
    cells_y = grid_y // N_GY
    cells_z = grid_z // N_GZ
    blocks = N_GX * N_GY * N_GZ
    occupied = (lax.broadcasted_iota(jnp.int32, (grid_x, grid_y, grid_z, slots_cell), 3) < counts[..., None]).astype(jnp.float32)
    masked = features * occupied[..., None]
    wrap_pad = ((1, 1), (1, 1), (1, 1), (0, 0), (0, 0))
    padded_feat = jnp.pad(masked, wrap_pad, mode='wrap')
    padded_pos = jnp.pad(offsets, wrap_pad, mode='wrap')

    def corner_of(block):
        spot_x = block // (N_GY * N_GZ) * cells_x
        spot_y = block // N_GZ % N_GY * cells_y
        spot_z = block % N_GZ * cells_z
        return (spot_x.astype(jnp.int32), spot_y.astype(jnp.int32), spot_z.astype(jnp.int32))

    def one_block(block):
        spot_x, spot_y, spot_z = corner_of(block)
        zero = jnp.int32(0)
        feat_ext = lax.dynamic_slice(padded_feat, (spot_x, spot_y, spot_z, zero, zero), (cells_x + 2, cells_y + 2, cells_z + 2, slots_cell, channels))
        pos_ext = lax.dynamic_slice(padded_pos, (spot_x, spot_y, spot_z, zero, zero), (cells_x + 2, cells_y + 2, cells_z + 2, 3, slots_cell))
        occ_block = lax.dynamic_slice(occupied, (spot_x, spot_y, spot_z, zero), (cells_x, cells_y, cells_z, slots_cell))
        near_block = lax.dynamic_slice(neighbours, (spot_x, spot_y, spot_z, zero, zero), (cells_x, cells_y, cells_z, slots_cell, neighbours.shape[-1]))

        def local_total(moved):
            energies = short_range(moved, feat_ext, occ_block, near_block, w_radial, w_vector, w_mix, w_out)
            return (jnp.sum(energies), energies)
        _, backward, energies = jax.vjp(local_total, pos_ext, has_aux=True)
        return (energies.reshape(cells_x, cells_y, cells_z, slots_cell), backward(jnp.float32(1.0))[0])
    energy_blocks, grad_blocks = lax.map(one_block, jnp.arange(blocks, dtype=jnp.int32))
    short = energy_blocks.reshape(N_GX, N_GY, N_GZ, cells_x, cells_y, cells_z, slots_cell)
    short = jnp.transpose(short, (0, 3, 1, 4, 2, 5, 6)).reshape(grid_x, grid_y, grid_z, slots_cell)

    def add_block(block, total):
        spot_x, spot_y, spot_z = corner_of(block)
        zero = jnp.int32(0)
        start = (spot_x, spot_y, spot_z, zero, zero)
        shape = (cells_x + 2, cells_y + 2, cells_z + 2, 3, slots_cell)
        current = lax.dynamic_slice(total, start, shape)
        return lax.dynamic_update_slice(total, current + grad_blocks[block], start)
    grad_pad = jnp.zeros((grid_x + 2, grid_y + 2, grid_z + 2, 3, slots_cell), jnp.float32)
    grad_pad = lax.fori_loop(0, blocks, add_block, grad_pad)
    grad_short = fold_wrap(fold_wrap(fold_wrap(grad_pad, 0), 1), 2)
    waves, weights = wave_table(grid_x, grid_y, grid_z)
    scale = 1.0 / math.sqrt(grid_x * grid_y * grid_z * slots_cell * KX * KY * KZ)
    charges = jnp.dot(masked.reshape(-1, channels), w_charge, precision=HIGH)
    place_x = lax.broadcasted_iota(jnp.int32, (grid_x, grid_y, grid_z, slots_cell), 0)
    place_y = lax.broadcasted_iota(jnp.int32, (grid_x, grid_y, grid_z, slots_cell), 1)
    place_z = lax.broadcasted_iota(jnp.int32, (grid_x, grid_y, grid_z, slots_cell), 2)
    centres = jnp.stack([place_x, place_y, place_z], -1).astype(jnp.float32) + jnp.moveaxis(offsets, 3, 4)
    rows_block = cells_x * cells_y * cells_z * slots_cell
    centre_blocks = centres.reshape(blocks, rows_block, 3)
    charge_blocks = charges.reshape(blocks, rows_block, charges.shape[-1])

    def partial_sums(pieces):
        _, _, part_cos, part_sin = structure_terms(pieces[0], pieces[1], waves)
        return (part_cos, part_sin)
    cos_parts, sin_parts = lax.map(partial_sums, (centre_blocks, charge_blocks))
    total_cos = lax.optimization_barrier(jnp.sum(cos_parts, 0))
    total_sin = lax.optimization_barrier(jnp.sum(sin_parts, 0))

    def long_block(pieces):
        cosine, sine, _, _ = structure_terms(pieces[0], pieces[1], waves)
        return ewald_terms(cosine, sine, pieces[1], total_cos, total_sin, waves, weights, scale)
    long_parts, pull_parts = lax.map(long_block, (centre_blocks, charge_blocks))
    long_range = long_parts.reshape(grid_x, grid_y, grid_z, slots_cell)
    pull = jnp.moveaxis(pull_parts.reshape(grid_x, grid_y, grid_z, slots_cell, 3), 4, 3)
    table = (species[..., None] == jnp.arange(species_shift.shape[0], dtype=jnp.int32)).astype(jnp.float32)
    shifted = jnp.dot(table.reshape(-1, species_shift.shape[0]), species_shift, precision=HIGH).reshape(grid_x, grid_y, grid_z, slots_cell)
    atom_energy = short + long_range + shifted * occupied
    forces = -(grad_short + pull)
    return (atom_energy, forces)
```

```python
import math

import jax
import jax.numpy as jnp
from jax import lax
from jax.experimental import pallas as pl
from jax.experimental.pallas import tpu as pltpu
from jax.sharding import PartitionSpec as P

KX = 16
KY = 8
KZ = 8
MODES = KX * KY * KZ
HIGH = lax.Precision.HIGHEST
F32 = jnp.float32
BF16 = jnp.bfloat16
PARAMS = pltpu.CompilerParams(vmem_limit_bytes=48 * 1024 * 1024)


def iota(shape, dim):
    return lax.broadcasted_iota(jnp.int32, shape, dim)


def split(value):
    high = value.astype(BF16)
    low = (value - high.astype(F32)).astype(BF16)
    return high, low


def contract(left, right, dims, precision=None):
    return lax.dot_general(
        left, right, (dims, ((), ())), precision=precision, preferred_element_type=F32
    )


def swap_halves(value):
    return pltpu.roll(value, 64, value.ndim - 1)


def pack_kernel(feat_ref, pos_ref, count_ref, near_ref, charge_ref, slab_ref, rest_ref, message_ref):
    row = iota((64, 128), 0)
    lane = iota((8, 128), 1)
    count_col = jnp.zeros((64, 128), jnp.int32)
    count_row = jnp.zeros((8, 128), jnp.int32)
    for cell in range(8):
        count = count_ref[cell // 4][cell // 2 % 2 : cell // 2 % 2 + 1, cell % 2 : cell % 2 + 1]
        count_col = jnp.where(row // 8 == cell, count, count_col)
        count_row = jnp.where(lane // 8 == cell, count, count_row)
    occupied = (row % 8 < count_col).astype(F32)
    occupied_row = (lane % 8 < count_row).astype(F32)
    masked = feat_ref[...] * occupied
    charges = contract(
        charge_ref[...], jnp.concatenate([masked, masked], 0), (((1,), (1,))), HIGH
    )
    spots = pos_ref[...]
    sub = iota((8, 128), 0)
    tile = jnp.concatenate([spots, jnp.zeros((5, 64), F32)], 0)
    tile = jnp.concatenate([tile, jnp.zeros((8, 64), F32)], 1)
    tile = jnp.where(sub == 3, occupied_row, tile)
    cell_x, cell_y, cell_z = lane // 32 % 2, lane // 16 % 2, lane // 8 % 2
    corner_x = 2 * lax.axis_index("gx")
    corner_y = 2 * lax.axis_index("gy")
    corner_z = 2 * lax.axis_index("gz")
    corner = jnp.where(
        sub == 0, cell_x + corner_x, jnp.where(sub == 1, cell_y + corner_y, cell_z + corner_z)
    )
    places = tile + corner.astype(F32)
    lane_low = lane < 64
    message = jnp.concatenate(
        [jnp.where(lane_low, charges[0:8], charges[8:16]), places], 0
    )
    for member in range(message_ref.shape[0]):
        message_ref[member] = message
    turned = jnp.concatenate(
        [jnp.zeros((32, 128), F32), tile, jnp.zeros((88, 128), F32)], 0
    ).T
    near = near_ref[...]
    atom = iota((64, 32), 0)
    stencil = near >> 3
    slot = near & 7
    step_x = (stencil * 57) >> 9
    line = (stencil * 171) >> 9
    step_z = stencil - 3 * line
    step_y = line - 3 * step_x
    spot_x = step_x + 1 - ((atom >> 5) & 1)
    spot_y = step_y + 1 - ((atom >> 4) & 1)
    spot_z = step_z + 1 - ((atom >> 3) & 1)
    block = (spot_z >> 1) * 4 + (spot_y >> 1) * 2 + (spot_x >> 1)
    cell = (spot_x & 1) * 4 + (spot_y & 1) * 2 + (spot_z & 1)
    target = (block * 64 + cell * 8 + slot).astype(F32)
    slab_ref[0:64] = masked
    slab_ref[64:72] = tile
    slab_ref[72:104] = turned[0:32]
    slab_ref[72:104, 0:32] = target[0:32]
    rest_ref[...] = turned[32:64]
    rest_ref[:, 0:32] = target[32:64]


def wave_numbers(member, shape, dim):
    index = iota(shape, dim) % 32
    number_y = (index // 8 + (member % 2) * 4 - KY // 2).astype(F32)
    number_z = (index % 8 - KZ // 2).astype(F32)
    number_x = (member // 2 - KX // 2).astype(F32)
    return number_x, number_y, number_z


def sine_cosine(turns):
    part = turns - jnp.floor(turns + 0.5)
    angle = part * (2.0 * math.pi)
    square = angle * angle
    sine = jnp.full_like(square, 1.0 / math.factorial(19) * -1.0)
    for power in range(17, 0, -2):
        sign = 1.0 if power // 2 % 2 == 0 else -1.0
        sine = sine * square + sign / math.factorial(power)
    cosine = jnp.full_like(square, -1.0 / math.factorial(18))
    for power in range(16, -1, -2):
        sign = 1.0 if power // 2 % 2 == 0 else -1.0
        cosine = cosine * square + sign / math.factorial(power)
    return sine * angle, cosine


def waves_kernel(grid, atoms_ref, message_ref, phase_ref, charge_ref):
    member = lax.axis_index("gy") * 4 + lax.axis_index("gz")
    low = iota((8, 128), 1) < 64
    upper, lower, places = [], [], []
    for pair in range(16):
        first, second = atoms_ref[2 * pair], atoms_ref[2 * pair + 1]
        turned_first, turned_second = swap_halves(first), swap_halves(second)
        upper.append(jnp.where(low, first[0:8], turned_second[0:8]))
        lower.append(jnp.where(low, turned_first[0:8], second[0:8]))
        places.append(jnp.where(low, first[8:16], turned_second[8:16]))
    charges = jnp.concatenate(
        [jnp.concatenate(upper, 1), jnp.concatenate(lower, 1)], 0
    )
    places = jnp.concatenate(places, 1)
    number_x, number_y, number_z = wave_numbers(member, (32, 1), 0)
    turns = (
        number_x * (places[0:1] * (1.0 / grid[0]))
        + number_y * (places[1:2] * (1.0 / grid[1]))
        + number_z * (places[2:3] * (1.0 / grid[2]))
    )
    sine, cosine = sine_cosine(turns)
    phases = jnp.concatenate([cosine, sine], 0)
    phase_ref[...] = phases
    charge_ref[...] = charges
    charge_stack = jnp.concatenate(split(charges), 0)
    phase_stack = jnp.concatenate(split(phases), 0)
    sums = contract(charge_stack, phase_stack, (((1,), (1,))))
    partial = sums[0:16] + sums[16:32]
    for other in range(message_ref.shape[0]):
        message_ref[other] = partial


def field_kernel(grid, scale, sums_ref, phase_ref, charge_ref, kept_ref, came_ref, out_ref):
    at_y, at_z = lax.axis_index("gy"), lax.axis_index("gz")
    member = at_y * 4 + at_z
    total = sums_ref[0]
    for other in range(1, sums_ref.shape[0]):
        total = total + sums_ref[other]
    total = total + swap_halves(total)
    two_pi = 2.0 * math.pi
    number_x, number_y, number_z = wave_numbers(member, (16, 128), 1)
    wave_x, wave_y, wave_z = (
        number_x * (two_pi / grid[0]),
        number_y * (two_pi / grid[1]),
        number_z * (two_pi / grid[2]),
    )
    length_sq = wave_x * wave_x + wave_y * wave_y + wave_z * wave_z
    total = total * (jnp.exp(-0.5 * length_sq) / (length_sq + 1.0))
    high = total.astype(BF16).astype(F32)
    low = total - high
    left = jnp.concatenate([high, low, high, jnp.zeros((80, 128), F32)], 0).T[0:64, 0:64]
    charge_high, charge_low = split(charge_ref[...])
    right = jnp.concatenate(
        [charge_high, charge_high, charge_low, jnp.zeros_like(charge_low)], 0
    )
    fields = contract(left.astype(BF16), right, (((1,), (0,))))
    cosine, sine = phase_ref[0:32], phase_ref[32:64]
    field_cos, field_sin = fields[0:32], fields[32:64]
    energy = (0.5 * scale) * jnp.sum(cosine * field_cos + sine * field_sin, 0, keepdims=True)
    turning = scale * (cosine * field_sin - sine * field_cos)
    number_x, number_y, number_z = wave_numbers(member, (32, 1), 0)
    pull_x = (number_x * (two_pi / grid[0])) * jnp.sum(turning, 0, keepdims=True)
    pull_y = jnp.sum(turning * (number_y * (two_pi / grid[1])), 0, keepdims=True)
    pull_z = jnp.sum(turning * (number_z * (two_pi / grid[2])), 0, keepdims=True)
    rows = jnp.concatenate([energy, pull_x, pull_y, pull_z], 0)
    for target in range(32):
        out_ref[target] = rows[:, target // 2 * 128 : target // 2 * 128 + 128]
    half = iota((4, 128), 1) // 64
    for block in range(4):
        by, bz = block % 2, block // 2
        to_z = (at_z + bz) % 4
        to = ((at_y + by) % 8) * 4 + to_z
        folded = kept_ref[block] + came_ref[block]
        out_ref[to] = out_ref[to] + jnp.where(half == to_z % 2, folded, 0.0)


def short_kernel(
    own_ref, rest_ref, in_x_ref, in_y_ref, in_z_ref,
    radial_ref, vector_ref, mix_ref, out_weight_ref, kept_ref, sent_ref,
):
    bases = [
        (own_ref, 0), (in_x_ref, 0), (in_y_ref, 0), (in_y_ref, 72),
        (in_z_ref, 0), (in_z_ref, 72), (in_z_ref, 144), (in_z_ref, 216),
    ]
    feats = jnp.concatenate([ref[at : at + 64] for ref, at in bases], 0)
    low_lane = iota((8, 128), 1) < 64
    spots = []
    for pair in range(4):
        (ref_a, at_a), (ref_b, at_b) = bases[2 * pair], bases[2 * pair + 1]
        spots.append(
            jnp.where(
                low_lane,
                ref_a[at_a + 64 : at_a + 72],
                swap_halves(ref_b[at_b + 64 : at_b + 72]),
            )
        )
    spots = jnp.concatenate(spots, 1)
    tiles = [
        rest_ref[24:32], in_x_ref[96:104], in_y_ref[152:160], in_y_ref[168:176],
        in_z_ref[288:296], in_z_ref[296:304], in_z_ref[304:312], in_z_ref[312:320],
    ]
    centres = jnp.concatenate(tiles, 0)
    own = []
    for unit in range(8):
        ux, uy, uz = unit % 2, unit // 2 % 2, unit // 4
        ref, at = bases[unit]
        at = at + ((1 - ux) * 4 + (1 - uy) * 2 + (1 - uz)) * 8
        own.append(ref[at : at + 8])
    own = jnp.concatenate(own, 0)
    occupied = centres[:, 35:36]
    lane = iota((1, 512), 1)
    block = lane // 64
    cell = lane // 8 % 8
    spot = (
        spots[0:1] + ((block % 2) * 2 + cell // 4).astype(F32),
        spots[1:2] + ((block // 2 % 2) * 2 + cell // 2 % 2).astype(F32),
        spots[2:3] + ((block // 4) * 2 + cell % 2).astype(F32),
    )
    atom = iota((64, 1), 0)
    unit = atom // 8
    middle = (
        centres[:, 32:33] + (unit % 2 + 1).astype(F32),
        centres[:, 33:34] + (unit // 2 % 2 + 1).astype(F32),
        centres[:, 34:35] + (unit // 4 + 1).astype(F32),
    )
    delta = [spot[a] - middle[a] for a in range(3)]
    dist_sq = delta[0] * delta[0] + delta[1] * delta[1] + delta[2] * delta[2]
    near = 1.0 - dist_sq * (1.0 / 16.0)
    envelope = near * near
    lane_f = iota((64, 512), 1).astype(F32)
    times = jnp.zeros((64, 512), F32)
    for entry in range(32):
        times = times + jnp.where(centres[:, entry : entry + 1] == lane_f, 1.0, 0.0)
    bases_m = []
    power = None
    for b in range(8):
        if b % 4 == 0:
            power = jnp.exp(dist_sq * (-(2.0 ** (b - 4))))
        else:
            power = power * power
        bases_m.append(power * times)
    feat_high, feat_low = split(feats)
    feat_both = jnp.concatenate([feat_high, feat_low], 1)
    norm = 1.0 / math.sqrt(32.0)
    sums = [jnp.zeros((64, 128), F32) for _ in range(4)]
    for b in range(8):
        weight = bases_m[b] * envelope
        left = jnp.concatenate([weight] + [weight * delta[a] for a in range(3)], 0)
        left_high, left_low = split(left)
        first = contract(left_high, feat_both, (((1,), (0,))))
        second = contract(left_low, feat_high, (((1,), (0,))))
        made = first[:, 0:128] + first[:, 128:256] + second
        sums[0] = sums[0] + made[0:64] * radial_ref[b : b + 1]
        for a in range(3):
            sums[1 + a] = sums[1 + a] + made[64 * (1 + a) : 64 * (2 + a)] * vector_ref[b : b + 1]
    sums = [value * norm for value in sums]
    product = sums[0] + sums[1] * sums[1] + sums[2] * sums[2] + sums[3] * sums[3]
    mixed = contract(product, mix_ref[...], (((1,), (0,))), HIGH)
    gate = 1.0 / (1.0 + jnp.exp(-mixed))
    out_weight = out_weight_ref[...]
    energy = jnp.sum((own + mixed * gate) * out_weight, 1, keepdims=True) * occupied
    slope = gate * (1.0 + mixed * (1.0 - gate)) * (out_weight * occupied)
    grad = contract(slope, mix_ref[...], (((1,), (1,))), HIGH) * norm
    grads = [grad] + [2.0 * grad * sums[1 + a] for a in range(3)]
    right = jnp.concatenate([feat_high, feat_high, feat_low], 1)
    linear = [jnp.zeros((64, 512), F32) for _ in range(3)]
    plain = jnp.zeros((64, 512), F32)
    decayed = jnp.zeros((64, 512), F32)
    for b in range(8):
        left = jnp.concatenate(
            [grads[0] * radial_ref[b : b + 1]]
            + [grads[1 + a] * vector_ref[b : b + 1] for a in range(3)],
            0,
        )
        left_high, left_low = split(left)
        pulled = contract(
            jnp.concatenate([left_high, left_low, left_high], 1), right, (((1,), (1,)))
        )
        parts = [pulled[64 * (1 + a) : 64 * (2 + a)] for a in range(3)]
        full = pulled[0:64] + parts[0] * delta[0] + parts[1] * delta[1] + parts[2] * delta[2]
        weighted = bases_m[b] * full
        plain = plain + weighted
        decayed = decayed + weighted * (2.0 ** (b - 4))
        for a in range(3):
            linear[a] = linear[a] + bases_m[b] * parts[a]
    radial_slope = 2.0 * (near * (-0.125) * plain - envelope * decayed)
    lane_i = iota((64, 512), 1)
    row_i = iota((64, 512), 0)
    ux, uy, uz = row_i // 8 % 2, row_i // 16 % 2, row_i // 32
    self_at = (row_i // 8) * 64 + ((1 - ux) * 4 + (1 - uy) * 2 + (1 - uz)) * 8 + row_i % 8
    own_slot = lane_i == self_at
    rows = [jnp.sum(jnp.where(own_slot, energy, 0.0), 0, keepdims=True)]
    for a in range(3):
        push = envelope * linear[a] + delta[a] * radial_slope
        back = jnp.sum(push, 1, keepdims=True)
        rows.append(jnp.sum(push - jnp.where(own_slot, back, 0.0), 0, keepdims=True))
    rows = jnp.concatenate(rows, 0)
    low = iota((4, 128), 1) < 64
    for k in range(4):
        piece = rows[:, 128 * k : 128 * k + 128]
        turned = swap_halves(piece)
        kept_ref[k] = jnp.where(low, piece, turned)
        sent_ref[k] = jnp.where(low, turned, piece)


def sum_kernel(parts_ref, out_ref):
    total = parts_ref[0]
    for member in range(1, parts_ref.shape[0]):
        total = total + parts_ref[member]
    odd = lax.axis_index("gz") % 2
    total = jnp.where(odd == 1, swap_halves(total), total)
    out_ref[...] = total


def call(kernel, out, *operands):
    return pl.pallas_call(
        kernel,
        out_shape=[jax.ShapeDtypeStruct(shape, F32) for shape in out],
        compiler_params=PARAMS,
    )(*operands)


def moved(value, axis, steps):
    count = lax.axis_size(axis)
    return lax.ppermute(value, axis, [(i, (i + steps) % count) for i in range(count)])


def body(
    features, offsets, counts, species, neighbours,
    w_radial, w_vector, w_mix, w_out, w_charge, species_shift,
):
    cells_x, cells_y, cells_z, slots_cell, channels = features.shape
    block_shape = (cells_x, cells_y, cells_z, slots_cell)
    grid = (
        cells_x * lax.axis_size("gx"),
        cells_y * lax.axis_size("gy"),
        cells_z * lax.axis_size("gz"),
    )
    scale = 1.0 / math.sqrt(grid[0] * grid[1] * grid[2] * slots_cell * MODES)
    spots = jnp.transpose(offsets, (3, 0, 1, 2, 4)).reshape(3, 64)
    slab, rest, message = call(
        pack_kernel,
        [(104, 128), (32, 128), (32, 16, 128)],
        features.reshape(64, 128),
        spots,
        counts,
        neighbours.reshape(64, 32),
        w_charge.T,
    )
    in_x = moved(slab, "gx", -1)
    atoms = lax.all_to_all(message, ("gy", "gz"), 0, 0)
    in_y = moved(
        jnp.concatenate([slab[0:72], in_x[0:72], rest[0:16], in_x[72:88]], 0), "gy", -1
    )
    partial, phases, charges = call(
        lambda *refs: waves_kernel(grid, *refs),
        [(16, 16, 128), (64, 2048), (16, 2048)],
        atoms,
    )
    sums = lax.all_to_all(partial, "gx", 0, 0)
    in_z = moved(
        jnp.concatenate(
            [
                slab[0:72], in_x[0:72], in_y[0:144],
                rest[16:24], in_x[88:96], in_y[144:152], in_y[160:168],
            ],
            0,
        ),
        "gz",
        -1,
    )
    kept, sent = call(
        short_kernel,
        [(4, 4, 128), (4, 4, 128)],
        slab, rest, in_x, in_y, in_z, w_radial, w_vector, w_mix, w_out.reshape(1, 128),
    )
    came = moved(sent, "gx", 1)
    (parts,) = call(
        lambda *refs: field_kernel(grid, scale, *refs),
        [(32, 4, 128)],
        sums, phases, charges, kept, came,
    )
    (rows,) = call(sum_kernel, [(4, 128)], lax.all_to_all(parts, ("gy", "gz"), 0, 0))
    table = species[..., None] == jnp.arange(species_shift.shape[0], dtype=jnp.int32)
    shifted = jnp.sum(jnp.where(table, species_shift, 0.0), -1)
    occupied = iota(block_shape, 3) < counts[..., None]
    atom_energy = rows[0, 0:64].reshape(block_shape) + jnp.where(occupied, shifted, 0.0)
    forces = -rows[1:4, 0:64].reshape((3,) + block_shape)
    return (atom_energy, jnp.transpose(forces, (1, 2, 3, 0, 4)))


def solution(mesh):
    spread = P("gx", "gy", "gz")
    in_specs = (spread,) * 5 + (P(),) * 6
    return jax.shard_map(
        body, mesh=mesh, in_specs=in_specs, out_specs=(spread, spread), check_vma=False
    )
```

```python
import functools
import math

import jax
import jax.numpy as jnp
from jax import lax
from jax.experimental import pallas as pl
from jax.experimental.pallas import tpu as pltpu
from jax.sharding import PartitionSpec as P

KX = 16
KY = 8
KZ = 8
MODES = KX * KY * KZ
HIGH = lax.Precision.HIGHEST
F32 = jnp.float32
BF16 = jnp.bfloat16
STACK_MICROS = 50
WAVES_MICROS = 500
SHORT_MICROS = 1
PACK_ROOM = 60
LAST_ROOM = 48


def iota(shape, dim):
    return lax.broadcasted_iota(jnp.int32, shape, dim)


def split(value):
    high = value.astype(BF16)
    low = (value - high.astype(F32)).astype(BF16)
    return high, low


def contract(left, right, dims, precision=None):
    return lax.dot_general(
        left, right, (dims, ((), ())), precision=precision, preferred_element_type=F32
    )


def swap_halves(value):
    return pltpu.roll(value, 64, value.ndim - 1)


def position_rows(pos_ref, lane):
    pieces = [pos_ref[x, y, d] for x in range(2) for y in range(2) for d in range(3)]
    spread = (iota((8, 128), 1) % 8 == iota((8, 128), 0)).astype(F32)
    wide = contract(jnp.concatenate(pieces, 0), spread, (((1,), (0,))), HIGH)
    rows = []
    for d in range(3):
        row = jnp.zeros((1, 128), F32)
        for cell in range(8):
            at = (cell // 2) * 6 + d * 2 + cell % 2
            row = jnp.where(lane[0:1] // 8 == cell, wide[at : at + 1], row)
        rows.append(row)
    return jnp.concatenate(rows + [jnp.zeros((5, 128), F32)], 0)


def pack_kernel(
    feat_ref, pos_ref, count_ref, near_ref, charge_ref,
    to_x_ref, to_y_ref, to_xy_ref, rest_ref, message_ref,
):
    row = iota((64, 128), 0)
    lane = iota((8, 128), 1)
    count_col = jnp.zeros((64, 128), jnp.int32)
    count_row = jnp.zeros((8, 128), jnp.int32)
    for cell in range(8):
        count = count_ref[cell // 4][cell // 2 % 2 : cell // 2 % 2 + 1, cell % 2 : cell % 2 + 1]
        count_col = jnp.where(row // 8 == cell, count, count_col)
        count_row = jnp.where(lane // 8 == cell, count, count_row)
    occupied = (row % 8 < count_col).astype(F32)
    occupied_row = (lane % 8 < count_row).astype(F32)
    masked = feat_ref[...] * occupied
    charges = contract(
        charge_ref[...], jnp.concatenate([masked, masked], 0), (((1,), (1,))), HIGH
    )
    sub = iota((8, 128), 0)
    tile = position_rows(pos_ref, lane)
    tile = jnp.where(sub == 3, occupied_row, tile)
    cell_x, cell_y, cell_z = lane // 32 % 2, lane // 16 % 2, lane // 8 % 2
    corner_x = 2 * lax.axis_index("gx")
    corner_y = 2 * lax.axis_index("gy")
    corner_z = 2 * lax.axis_index("gz")
    corner = jnp.where(
        sub == 0, cell_x + corner_x, jnp.where(sub == 1, cell_y + corner_y, cell_z + corner_z)
    )
    places = tile + corner.astype(F32)
    lane_low = lane < 64
    message = jnp.concatenate(
        [jnp.where(lane_low, charges[0:8], charges[8:16]), places], 0
    )
    for member in range(message_ref.shape[0]):
        message_ref[member] = message
    turned = jnp.concatenate(
        [jnp.zeros((32, 128), F32), tile, jnp.zeros((88, 128), F32)], 0
    ).T
    near = near_ref[...]
    atom = iota((64, 32), 0)
    stencil = near >> 3
    slot = near & 7
    step_x = (stencil * 57) >> 9
    line = (stencil * 171) >> 9
    step_z = stencil - 3 * line
    step_y = line - 3 * step_x
    spot_x = step_x + 1 - ((atom >> 5) & 1)
    spot_y = step_y + 1 - ((atom >> 4) & 1)
    spot_z = step_z + 1 - ((atom >> 3) & 1)
    block = (spot_z >> 1) * 4 + (spot_y >> 1) * 2 + (spot_x >> 1)
    cell = (spot_x & 1) * 4 + (spot_y & 1) * 2 + (spot_z & 1)
    target = (block * 64 + cell * 8 + slot).astype(F32)
    for ref, first in ((to_xy_ref, 0), (to_x_ref, 16), (to_y_ref, 32)):
        ref[0:64] = masked
        ref[64:72] = tile
        ref[72:88] = turned[first : first + 16]
        ref[72:88, 0:32] = target[first : first + 16]
    rest_ref[...] = turned[48:64]
    rest_ref[:, 0:32] = target[48:64]


def stack_kernel(own_ref, rest_ref, in_x_ref, in_y_ref, in_xy_ref, out_ref):
    for block, ref in enumerate((own_ref, in_x_ref, in_y_ref, in_xy_ref)):
        out_ref[72 * block : 72 * block + 72] = ref[0:72]
    out_ref[288:296] = rest_ref[0:8]
    for block, ref in enumerate((in_x_ref, in_y_ref, in_xy_ref)):
        out_ref[296 + 8 * block : 304 + 8 * block] = ref[72:80]


def wave_numbers(member, shape, dim):
    index = iota(shape, dim) % 32
    number_y = (index // 8 + (member % 2) * 4 - KY // 2).astype(F32)
    number_z = (index % 8 - KZ // 2).astype(F32)
    number_x = (member // 2 - KX // 2).astype(F32)
    return number_x, number_y, number_z


def sine_cosine(turns):
    part = turns - jnp.floor(turns + 0.5)
    angle = part * (2.0 * math.pi)
    square = angle * angle
    sine = jnp.full_like(square, 1.0 / math.factorial(19) * -1.0)
    for power in range(17, 0, -2):
        sign = 1.0 if power // 2 % 2 == 0 else -1.0
        sine = sine * square + sign / math.factorial(power)
    cosine = jnp.full_like(square, -1.0 / math.factorial(18))
    for power in range(16, -1, -2):
        sign = 1.0 if power // 2 % 2 == 0 else -1.0
        cosine = cosine * square + sign / math.factorial(power)
    return sine * angle, cosine


def waves_kernel(grid, atoms_ref, partial_ref, phase_ref, charge_ref):
    member = lax.axis_index("gy") * 4 + lax.axis_index("gz")
    low = iota((8, 128), 1) < 64
    upper, lower, places = [], [], []
    for pair in range(16):
        first, second = atoms_ref[2 * pair], atoms_ref[2 * pair + 1]
        turned_first, turned_second = swap_halves(first), swap_halves(second)
        upper.append(jnp.where(low, first[0:8], turned_second[0:8]))
        lower.append(jnp.where(low, turned_first[0:8], second[0:8]))
        places.append(jnp.where(low, first[8:16], turned_second[8:16]))
    charges = jnp.concatenate(
        [jnp.concatenate(upper, 1), jnp.concatenate(lower, 1)], 0
    )
    places = jnp.concatenate(places, 1)
    number_x, number_y, number_z = wave_numbers(member, (32, 1), 0)
    turns = (
        number_x * (places[0:1] * (1.0 / grid[0]))
        + number_y * (places[1:2] * (1.0 / grid[1]))
        + number_z * (places[2:3] * (1.0 / grid[2]))
    )
    sine, cosine = sine_cosine(turns)
    phases = jnp.concatenate([cosine, sine], 0)
    phase_ref[...] = phases
    charge_ref[...] = charges
    charge_stack = jnp.concatenate(split(charges), 0)
    phase_stack = jnp.concatenate(split(phases), 0)
    sums = contract(charge_stack, phase_stack, (((1,), (1,))))
    partial = sums[0:16] + sums[16:32]
    partial = partial + swap_halves(partial)
    partial_ref[...] = jnp.where(low, partial[0:8], partial[8:16])


def join_kernel(partial_ref, kept_ref, sent_ref, message_ref):
    here = lax.axis_index("gx")
    count = message_ref.shape[0]
    partial = partial_ref[...]
    for other in range(count):
        message_ref[other, 0:8] = partial
        message_ref[other, 8:16] = jnp.zeros((8, 128), F32)
    message_ref[here, 8:16] = kept_ref[...]
    message_ref[(here + 1) % count, 8:16] = sent_ref[...]


def field_kernel(grid, scale, sums_ref, phase_ref, charge_ref, out_ref):
    at_y, at_z = lax.axis_index("gy"), lax.axis_index("gz")
    member = at_y * 4 + at_z
    total = sums_ref[0]
    for other in range(1, sums_ref.shape[0]):
        total = total + sums_ref[other]
    folded = total[8:16]
    turned = swap_halves(total)
    low_lane = iota((8, 128), 1) < 64
    total = jnp.concatenate(
        [
            jnp.where(low_lane, total[0:8], turned[0:8]),
            jnp.where(low_lane, turned[0:8], total[0:8]),
        ],
        0,
    )
    turned = turned[8:16]
    two_pi = 2.0 * math.pi
    number_x, number_y, number_z = wave_numbers(member, (16, 128), 1)
    wave_x, wave_y, wave_z = (
        number_x * (two_pi / grid[0]),
        number_y * (two_pi / grid[1]),
        number_z * (two_pi / grid[2]),
    )
    length_sq = wave_x * wave_x + wave_y * wave_y + wave_z * wave_z
    total = total * (jnp.exp(-0.5 * length_sq) / (length_sq + 1.0))
    high = total.astype(BF16).astype(F32)
    low = total - high
    left = jnp.concatenate([high, low, high, jnp.zeros((80, 128), F32)], 0).T[0:64, 0:64]
    charge_high, charge_low = split(charge_ref[...])
    right = jnp.concatenate(
        [charge_high, charge_high, charge_low, jnp.zeros_like(charge_low)], 0
    )
    fields = contract(left.astype(BF16), right, (((1,), (0,))))
    cosine, sine = phase_ref[0:32], phase_ref[32:64]
    field_cos, field_sin = fields[0:32], fields[32:64]
    energy = (0.5 * scale) * jnp.sum(cosine * field_cos + sine * field_sin, 0, keepdims=True)
    turning = scale * (cosine * field_sin - sine * field_cos)
    number_x, number_y, number_z = wave_numbers(member, (32, 1), 0)
    pull_x = (number_x * (two_pi / grid[0])) * jnp.sum(turning, 0, keepdims=True)
    pull_y = jnp.sum(turning * (number_y * (two_pi / grid[1])), 0, keepdims=True)
    pull_z = jnp.sum(turning * (number_z * (two_pi / grid[2])), 0, keepdims=True)
    rows = jnp.concatenate([energy, pull_x, pull_y, pull_z], 0)
    for target in range(32):
        out_ref[target] = rows[:, target // 2 * 128 : target // 2 * 128 + 128]
    half = iota((4, 128), 1) // 64
    for block in range(4):
        by, bz = block % 2, block // 2
        to_z = (at_z + bz) % 4
        to = ((at_y + by) % 8) * 4 + to_z
        rows_at = slice(4 * bz, 4 * bz + 4)
        piece = jnp.where(to_z % 2 == by, folded[rows_at], turned[rows_at])
        out_ref[to] = out_ref[to] + jnp.where(half == to_z % 2, piece, 0.0)


def short_kernel(
    own_ref, rest_ref, in_x_ref, in_y_ref, in_xy_ref, in_z_ref,
    radial_ref, vector_ref, mix_ref, out_weight_ref, species_ref, shift_ref, kept_ref, sent_ref,
):
    bases = [
        (own_ref, 0), (in_x_ref, 0), (in_y_ref, 0), (in_xy_ref, 0),
        (in_z_ref, 0), (in_z_ref, 72), (in_z_ref, 144), (in_z_ref, 216),
    ]
    feats = jnp.concatenate([ref[at : at + 64] for ref, at in bases], 0)
    low_lane = iota((8, 128), 1) < 64
    spots = []
    for pair in range(4):
        (ref_a, at_a), (ref_b, at_b) = bases[2 * pair], bases[2 * pair + 1]
        spots.append(
            jnp.where(
                low_lane,
                ref_a[at_a + 64 : at_a + 72],
                swap_halves(ref_b[at_b + 64 : at_b + 72]),
            )
        )
    spots = jnp.concatenate(spots, 1)
    tiles = [
        rest_ref[8:16], in_x_ref[80:88], in_y_ref[80:88], in_xy_ref[80:88],
        in_z_ref[288:296], in_z_ref[296:304], in_z_ref[304:312], in_z_ref[312:320],
    ]
    centres = jnp.concatenate(tiles, 0)
    own = []
    for unit in range(8):
        ux, uy, uz = unit % 2, unit // 2 % 2, unit // 4
        ref, at = bases[unit]
        at = at + ((1 - ux) * 4 + (1 - uy) * 2 + (1 - uz)) * 8
        own.append(ref[at : at + 8])
    own = jnp.concatenate(own, 0)
    occupied = centres[:, 35:36]
    lane = iota((1, 512), 1)
    block = lane // 64
    cell = lane // 8 % 8
    spot = (
        spots[0:1] + ((block % 2) * 2 + cell // 4).astype(F32),
        spots[1:2] + ((block // 2 % 2) * 2 + cell // 2 % 2).astype(F32),
        spots[2:3] + ((block // 4) * 2 + cell % 2).astype(F32),
    )
    atom = iota((64, 1), 0)
    unit = atom // 8
    middle = (
        centres[:, 32:33] + (unit % 2 + 1).astype(F32),
        centres[:, 33:34] + (unit // 2 % 2 + 1).astype(F32),
        centres[:, 34:35] + (unit // 4 + 1).astype(F32),
    )
    delta = [spot[a] - middle[a] for a in range(3)]
    dist_sq = delta[0] * delta[0] + delta[1] * delta[1] + delta[2] * delta[2]
    near = 1.0 - dist_sq * (1.0 / 16.0)
    envelope = near * near
    lane_f = iota((64, 512), 1).astype(F32)
    times = jnp.zeros((64, 512), F32)
    for entry in range(32):
        times = times + jnp.where(centres[:, entry : entry + 1] == lane_f, 1.0, 0.0)
    bases_m = []
    power = None
    for b in range(8):
        if b % 4 == 0:
            power = jnp.exp(dist_sq * (-(2.0 ** (b - 4))))
        else:
            power = power * power
        bases_m.append(power * times)
    feat_high, feat_low = split(feats)
    feat_both = jnp.concatenate([feat_high, feat_low], 1)
    norm = 1.0 / math.sqrt(32.0)
    sums = [jnp.zeros((64, 128), F32) for _ in range(4)]
    for b in range(8):
        weight = bases_m[b] * envelope
        left = jnp.concatenate([weight] + [weight * delta[a] for a in range(3)], 0)
        left_high, left_low = split(left)
        first = contract(left_high, feat_both, (((1,), (0,))))
        second = contract(left_low, feat_high, (((1,), (0,))))
        made = first[:, 0:128] + first[:, 128:256] + second
        sums[0] = sums[0] + made[0:64] * radial_ref[b : b + 1]
        for a in range(3):
            sums[1 + a] = sums[1 + a] + made[64 * (1 + a) : 64 * (2 + a)] * vector_ref[b : b + 1]
    sums = [value * norm for value in sums]
    product = sums[0] + sums[1] * sums[1] + sums[2] * sums[2] + sums[3] * sums[3]
    mixed = contract(product, mix_ref[...], (((1,), (0,))), HIGH)
    gate = 1.0 / (1.0 + jnp.exp(-mixed))
    out_weight = out_weight_ref[...]
    energy = jnp.sum((own + mixed * gate) * out_weight, 1, keepdims=True) * occupied
    slope = gate * (1.0 + mixed * (1.0 - gate)) * (out_weight * occupied)
    grad = contract(slope, mix_ref[...], (((1,), (1,))), HIGH) * norm
    grads = [grad] + [2.0 * grad * sums[1 + a] for a in range(3)]
    right = jnp.concatenate([feat_high, feat_high, feat_low], 1)
    linear = [jnp.zeros((64, 512), F32) for _ in range(3)]
    plain = jnp.zeros((64, 512), F32)
    decayed = jnp.zeros((64, 512), F32)
    for b in range(8):
        left = jnp.concatenate(
            [grads[0] * radial_ref[b : b + 1]]
            + [grads[1 + a] * vector_ref[b : b + 1] for a in range(3)],
            0,
        )
        left_high, left_low = split(left)
        pulled = contract(
            jnp.concatenate([left_high, left_low, left_high], 1), right, (((1,), (1,)))
        )
        parts = [pulled[64 * (1 + a) : 64 * (2 + a)] for a in range(3)]
        full = pulled[0:64] + parts[0] * delta[0] + parts[1] * delta[1] + parts[2] * delta[2]
        weighted = bases_m[b] * full
        plain = plain + weighted
        decayed = decayed + weighted * (2.0 ** (b - 4))
        for a in range(3):
            linear[a] = linear[a] + bases_m[b] * parts[a]
    radial_slope = 2.0 * (near * (-0.125) * plain - envelope * decayed)
    lane_i = iota((64, 512), 1)
    row_i = iota((64, 512), 0)
    ux, uy, uz = row_i // 8 % 2, row_i // 16 % 2, row_i // 32
    self_at = (row_i // 8) * 64 + ((1 - ux) * 4 + (1 - uy) * 2 + (1 - uz)) * 8 + row_i % 8
    own_slot = lane_i == self_at
    rows = [jnp.sum(jnp.where(own_slot, energy, 0.0), 0, keepdims=True)]
    for a in range(3):
        push = envelope * linear[a] + delta[a] * radial_slope
        back = jnp.sum(push, 1, keepdims=True)
        rows.append(jnp.sum(push - jnp.where(own_slot, back, 0.0), 0, keepdims=True))
    rows = jnp.concatenate(rows, 0)
    low = iota((4, 128), 1) < 64
    kinds = [species_ref[x, y] for x in range(2) for y in range(2)]
    spread = (iota((8, 128), 1) % 8 == iota((8, 128), 0)).astype(F32)
    kinds = contract(jnp.concatenate(kinds, 0).astype(F32), spread, (((1,), (0,))))
    shift = jnp.zeros((8, 128), F32)
    for name in range(shift_ref.shape[1]):
        shift = jnp.where(kinds == float(name), shift_ref[:, name : name + 1], shift)
    mine = iota((8, 128), 1) // 8 == iota((8, 128), 0)
    shift = jnp.sum(jnp.where(mine, shift, 0.0), 0, keepdims=True) * own_ref[67:68]
    shift = jnp.where(iota((4, 128), 0) == 0, shift, 0.0)
    for half in range(2):
        first, second = (rows[:, 128 * k : 128 * k + 128] for k in (2 * half, 2 * half + 1))
        at = slice(4 * half, 4 * half + 4)
        first = first + shift if half == 0 else first
        kept_ref[at] = jnp.where(low, first, swap_halves(second))
        sent_ref[at] = jnp.where(low, swap_halves(first), second)


def last_kernel(parts_ref, energy_ref, force_ref):
    total = parts_ref[0]
    for member in range(1, parts_ref.shape[0]):
        total = total + parts_ref[member]
    odd = lax.axis_index("gz") % 2
    total = jnp.where(odd == 1, swap_halves(total), total)
    for cell in range(8):
        x, y, z = cell // 4, cell // 2 % 2, cell % 2
        here = total if cell == 0 else pltpu.roll(total, 128 - 8 * cell, 1)
        energy_ref[x, y, z : z + 1] = here[0:1, 0:8]
        for d in range(3):
            force_ref[x, y, d, z : z + 1] = -here[1 + d : 2 + d, 0:8]


def call(kernel, out, *operands, micros=10, room=48):
    cost = pl.CostEstimate(flops=micros * 10**8, bytes_accessed=micros * 3 * 10**5, transcendentals=0)
    return pl.pallas_call(
        kernel,
        out_shape=[jax.ShapeDtypeStruct(shape, F32) for shape in out],
        compiler_params=pltpu.CompilerParams(vmem_limit_bytes=room * 1024 * 1024),
        cost_estimate=cost,
    )(*operands)


def moved(value, axes, *steps):
    counts = [lax.axis_size(axis) for axis in axes]
    pairs = []
    for source in range(math.prod(counts)):
        rest, target, stride = source, 0, 1
        for count, step in zip(counts[::-1], steps[::-1]):
            target += (rest + step) % count * stride
            rest, stride = rest // count, stride * count
        pairs.append((source, target))
    return lax.ppermute(value, axes, pairs)


def body(
    features, offsets, counts, species, neighbours,
    w_radial, w_vector, w_mix, w_out, w_charge, species_shift,
):
    cells_x, cells_y, cells_z, slots_cell, channels = features.shape
    grid = (
        cells_x * lax.axis_size("gx"),
        cells_y * lax.axis_size("gy"),
        cells_z * lax.axis_size("gz"),
    )
    scale = 1.0 / math.sqrt(grid[0] * grid[1] * grid[2] * slots_cell * MODES)
    to_x, to_y, to_xy, rest, message = call(
        pack_kernel,
        [(88, 128), (88, 128), (88, 128), (16, 128), (32, 16, 128)],
        features.reshape(64, 128),
        jnp.transpose(offsets, (0, 1, 3, 2, 4)),
        counts,
        neighbours.reshape(64, 32),
        w_charge.T,
        room=PACK_ROOM,
    )
    atoms = lax.all_to_all(message, ("gy", "gz"), 0, 0)
    in_x = moved(to_x, ("gx",), -1)
    in_y = moved(to_y, ("gy",), -1)
    in_xy = moved(to_xy, ("gx", "gy"), -1, -1)
    (to_z,) = call(
        stack_kernel, [(320, 128)], to_x, rest, in_x, in_y, in_xy, micros=STACK_MICROS
    )
    in_z = moved(to_z, ("gz",), -1)
    partial, phases, charges = call(
        functools.partial(waves_kernel, grid),
        [(8, 128), (64, 2048), (16, 2048)],
        atoms,
        micros=WAVES_MICROS,
    )
    kept, sent = call(
        short_kernel,
        [(8, 128), (8, 128)],
        to_x, rest, in_x, in_y, in_xy, in_z,
        w_radial, w_vector, w_mix, w_out.reshape(1, 128), species, species_shift.reshape(1, 8),
        micros=SHORT_MICROS,
    )
    (joined,) = call(join_kernel, [(16, 16, 128)], partial, kept, sent)
    sums = lax.all_to_all(joined, "gx", 0, 0)
    (parts,) = call(
        functools.partial(field_kernel, grid, scale), [(32, 4, 128)], sums, phases, charges
    )
    parts = lax.all_to_all(parts, ("gy", "gz"), 0, 0)
    atom_energy, forces = call(last_kernel, [(2, 2, 2, 8), (2, 2, 3, 2, 8)], parts, room=LAST_ROOM)
    return (atom_energy, jnp.transpose(forces, (0, 1, 3, 2, 4)))


def solution(mesh):
    spread = P("gx", "gy", "gz")
    in_specs = (spread,) * 5 + (P(),) * 6
    return jax.shard_map(
        body, mesh=mesh, in_specs=in_specs, out_specs=(spread, spread), check_vma=False
    )
```

```python
import functools
import math

import jax
import jax.numpy as jnp
from jax import lax
from jax.experimental import pallas as pl
from jax.experimental.pallas import tpu as pltpu
from jax.sharding import PartitionSpec as P

KX = 16
KY = 8
KZ = 8
MODES = KX * KY * KZ
HIGH = lax.Precision.HIGHEST
F32 = jnp.float32
BF16 = jnp.bfloat16
STACK_Y_MICROS = 50
STACK_Z_MICROS = 1
WAVES_MICROS = 500
SHORT_MICROS = 1
PACK_ROOM = 60
LAST_ROOM = 48


def iota(shape, dim):
    return lax.broadcasted_iota(jnp.int32, shape, dim)


def split(value):
    high = value.astype(BF16)
    low = (value - high.astype(F32)).astype(BF16)
    return high, low


def contract(left, right, dims, precision=None):
    return lax.dot_general(
        left, right, (dims, ((), ())), precision=precision, preferred_element_type=F32
    )


def split_left(value):
    high, low = split(value)
    return jnp.concatenate([high, low, high], 1)


def split_right(value, axis):
    high, low = split(value)
    return jnp.concatenate([high, high, low], axis)


def swap_halves(value):
    return pltpu.roll(value, 64, value.ndim - 1)


def position_rows(pos_ref, lane):
    pieces = [pos_ref[x, y, d] for x in range(2) for y in range(2) for d in range(3)]
    spread = (iota((8, 128), 1) % 8 == iota((8, 128), 0)).astype(F32)
    pieces = jnp.concatenate(pieces, 0)
    first, rest = split(pieces)
    last = (pieces - first.astype(F32) - rest.astype(F32)).astype(BF16)
    wide = contract(
        jnp.concatenate([first, rest, last], 1),
        jnp.concatenate([spread] * 3, 0).astype(BF16),
        (((1,), (0,))),
    )
    rows = []
    for d in range(3):
        row = jnp.zeros((1, 128), F32)
        for cell in range(8):
            at = (cell // 2) * 6 + d * 2 + cell % 2
            row = jnp.where(lane[0:1] // 8 == cell, wide[at : at + 1], row)
        rows.append(row)
    return jnp.concatenate(rows + [jnp.zeros((5, 128), F32)], 0)


def pack_kernel(
    feat_hbm, pos_hbm, count_hbm, near_hbm, charge_hbm, weight_hbm, shift_hbm,
    slab_ref, rest_ref, extra_ref, message_ref,
    feat_ref, pos_ref, count_ref, near_ref, charge_ref, weight_ref, shift_ref, arrived,
):
    copies = [
        pltpu.make_async_copy(source, target, arrived.at[at])
        for at, (source, target) in enumerate(
            (
                (feat_hbm, feat_ref), (pos_hbm, pos_ref), (count_hbm, count_ref),
                (near_hbm, near_ref), (charge_hbm, charge_ref), (weight_hbm, weight_ref),
                (shift_hbm, shift_ref),
            )
        )
    ]
    for copy in copies:
        copy.start()
    for copy in copies:
        copy.wait()
    extra_ref[...] = jnp.zeros((8, 128), F32)
    extra_ref[0:1] = weight_ref[...]
    extra_ref[1:2, 0:8] = shift_ref[...]
    row = iota((64, 128), 0)
    lane = iota((8, 128), 1)
    count_col = jnp.zeros((64, 128), jnp.int32)
    count_row = jnp.zeros((8, 128), jnp.int32)
    for cell in range(8):
        count = count_ref[cell // 4][cell // 2 % 2 : cell // 2 % 2 + 1, cell % 2 : cell % 2 + 1]
        count_col = jnp.where(row // 8 == cell, count, count_col)
        count_row = jnp.where(lane // 8 == cell, count, count_row)
    occupied = (row % 8 < count_col).astype(F32)
    occupied_row = (lane % 8 < count_row).astype(F32)
    masked = feat_ref[...] * occupied
    charges = contract(
        split_left(charge_ref[...]),
        split_right(jnp.concatenate([masked, masked], 0), 1),
        (((1,), (1,))),
    )
    sub = iota((8, 128), 0)
    tile = position_rows(pos_ref, lane)
    tile = jnp.where(sub == 3, occupied_row, tile)
    cell_x, cell_y, cell_z = lane // 32 % 2, lane // 16 % 2, lane // 8 % 2
    corner_x = 2 * lax.axis_index("gx")
    corner_y = 2 * lax.axis_index("gy")
    corner_z = 2 * lax.axis_index("gz")
    corner = jnp.where(
        sub == 0, cell_x + corner_x, jnp.where(sub == 1, cell_y + corner_y, cell_z + corner_z)
    )
    places = tile + corner.astype(F32)
    lane_low = lane < 64
    charges = jnp.where(lane_low, charges[0:8], charges[8:16])
    places = jnp.where(lane_low, places, swap_halves(pltpu.roll(places, 7, 0)))
    places = jnp.concatenate([places[0:1], places[2:3]], 0)
    pieces = [charges[2 * k : 2 * k + 2] for k in range(4)] + [places]
    for member in range(message_ref.shape[0]):
        for k in range(5):
            message_ref[member, k] = pieces[k]
    turned = jnp.concatenate(
        [jnp.zeros((32, 128), F32), tile, jnp.zeros((88, 128), F32)], 0
    ).T
    near = near_ref[...]
    atom = iota((64, 32), 0)
    stencil = near >> 3
    slot = near & 7
    step_x = (stencil * 57) >> 9
    line = (stencil * 171) >> 9
    step_z = stencil - 3 * line
    step_y = line - 3 * step_x
    spot_x = step_x + 1 - ((atom >> 5) & 1)
    spot_y = step_y + 1 - ((atom >> 4) & 1)
    spot_z = step_z + 1 - ((atom >> 3) & 1)
    block = (spot_z >> 1) * 4 + (spot_y >> 1) * 2 + (spot_x >> 1)
    cell = (spot_x & 1) * 4 + (spot_y & 1) * 2 + (spot_z & 1)
    target = (block * 64 + cell * 8 + slot).astype(F32)
    slab_ref[0:64] = masked
    slab_ref[64:72] = tile
    slab_ref[72:104] = turned[0:32]
    slab_ref[72:104, 0:32] = target[0:32]
    rest_ref[...] = turned[32:64]
    rest_ref[:, 0:32] = target[32:64]


def stack_y_kernel(own_ref, rest_ref, in_x_ref, out_ref):
    out_ref[0:72] = own_ref[0:72]
    out_ref[72:144] = in_x_ref[0:72]
    out_ref[144:160] = rest_ref[0:16]
    out_ref[160:176] = in_x_ref[72:88]


def stack_z_kernel(own_ref, rest_ref, in_x_ref, in_y_ref, out_ref):
    out_ref[0:72] = own_ref[0:72]
    out_ref[72:144] = in_x_ref[0:72]
    out_ref[144:288] = in_y_ref[0:144]
    out_ref[288:296] = rest_ref[16:24]
    out_ref[296:304] = in_x_ref[88:96]
    out_ref[304:312] = in_y_ref[144:152]
    out_ref[312:320] = in_y_ref[160:168]


def wave_numbers(member, shape, dim):
    index = iota(shape, dim) % 32
    number_y = (index // 8 + (member % 2) * 4 - KY // 2).astype(F32)
    number_z = (index % 8 - KZ // 2).astype(F32)
    number_x = (member // 2 - KX // 2).astype(F32)
    return number_x, number_y, number_z


def sine_cosine(turns):
    part = turns - jnp.floor(turns + 0.5)
    angle = part * (2.0 * math.pi)
    square = angle * angle
    sine = jnp.full_like(square, 1.0 / math.factorial(19) * -1.0)
    for power in range(17, 0, -2):
        sign = 1.0 if power // 2 % 2 == 0 else -1.0
        sine = sine * square + sign / math.factorial(power)
    cosine = jnp.full_like(square, -1.0 / math.factorial(18))
    for power in range(16, -1, -2):
        sign = 1.0 if power // 2 % 2 == 0 else -1.0
        cosine = cosine * square + sign / math.factorial(power)
    return sine * angle, cosine


def waves_kernel(grid, atoms_ref, partial_ref, phase_ref, charge_ref):
    member = lax.axis_index("gy") * 4 + lax.axis_index("gz")
    low = iota((8, 128), 1) < 64
    upper, lower, places = [], [], []
    for pair in range(16):
        first, second = atoms_ref[20 * pair : 20 * pair + 8], atoms_ref[20 * pair + 10 : 20 * pair + 18]
        upper.append(jnp.where(low, first, swap_halves(second)))
        lower.append(jnp.where(low, swap_halves(first), second))
        first, second = (
            atoms_ref[20 * pair + 8 : 20 * pair + 10],
            atoms_ref[20 * pair + 18 : 20 * pair + 20],
        )
        places.append(
            jnp.concatenate(
                [
                    jnp.where(low[0:2], first, swap_halves(second)),
                    jnp.where(low[0:2], swap_halves(first), second),
                ],
                0,
            )
        )
    charges = jnp.concatenate(
        [jnp.concatenate(upper, 1), jnp.concatenate(lower, 1)], 0
    )
    places = jnp.concatenate(places, 1)
    number_x, number_y, number_z = wave_numbers(member, (32, 1), 0)
    turns = (
        number_x * (places[0:1] * (1.0 / grid[0]))
        + number_y * (places[2:3] * (1.0 / grid[1]))
        + number_z * (places[1:2] * (1.0 / grid[2]))
    )
    sine, cosine = sine_cosine(turns)
    phases = jnp.concatenate([cosine, sine], 0)
    phase_ref[...] = phases
    charge_ref[...] = charges
    charge_stack = jnp.concatenate(split(charges), 0)
    phase_stack = jnp.concatenate(split(phases), 0)
    sums = contract(charge_stack, phase_stack, (((1,), (1,))))
    partial = sums[0:16] + sums[16:32]
    partial = partial + swap_halves(partial)
    partial_ref[...] = jnp.where(low, partial[0:8], partial[8:16])


def field_kernel(grid, scale, sums_ref, phase_ref, charge_ref, out_ref):
    at_y, at_z = lax.axis_index("gy"), lax.axis_index("gz")
    member = at_y * 4 + at_z
    total = sums_ref[0]
    for other in range(1, sums_ref.shape[0]):
        total = total + sums_ref[other]
    folded = total[8:16]
    turned = swap_halves(total)
    low_lane = iota((8, 128), 1) < 64
    total = jnp.concatenate(
        [
            jnp.where(low_lane, total[0:8], turned[0:8]),
            jnp.where(low_lane, turned[0:8], total[0:8]),
        ],
        0,
    )
    turned = turned[8:16]
    two_pi = 2.0 * math.pi
    number_x, number_y, number_z = wave_numbers(member, (16, 128), 1)
    wave_x, wave_y, wave_z = (
        number_x * (two_pi / grid[0]),
        number_y * (two_pi / grid[1]),
        number_z * (two_pi / grid[2]),
    )
    length_sq = wave_x * wave_x + wave_y * wave_y + wave_z * wave_z
    total = total * (jnp.exp(-0.5 * length_sq) / (length_sq + 1.0))
    high = total.astype(BF16).astype(F32)
    low = total - high
    left = jnp.concatenate([high, low, high, jnp.zeros((80, 128), F32)], 0).T[0:64, 0:64]
    charge_high, charge_low = split(charge_ref[...])
    right = jnp.concatenate(
        [charge_high, charge_high, charge_low, jnp.zeros_like(charge_low)], 0
    )
    fields = contract(left.astype(BF16), right, (((1,), (0,))))
    cosine, sine = phase_ref[0:32], phase_ref[32:64]
    field_cos, field_sin = fields[0:32], fields[32:64]
    energy = (0.5 * scale) * jnp.sum(cosine * field_cos + sine * field_sin, 0, keepdims=True)
    turning = scale * (cosine * field_sin - sine * field_cos)
    number_x, number_y, number_z = wave_numbers(member, (32, 1), 0)
    pull_x = (number_x * (two_pi / grid[0])) * jnp.sum(turning, 0, keepdims=True)
    pull_y = jnp.sum(turning * (number_y * (two_pi / grid[1])), 0, keepdims=True)
    pull_z = jnp.sum(turning * (number_z * (two_pi / grid[2])), 0, keepdims=True)
    rows = jnp.concatenate([energy, pull_x, pull_y, pull_z], 0)
    for target in range(32):
        out_ref[target] = rows[:, target // 2 * 128 : target // 2 * 128 + 128]
    half = iota((4, 128), 1) // 64
    for block in range(4):
        by, bz = block % 2, block // 2
        to_z = (at_z + bz) % 4
        to = ((at_y + by) % 8) * 4 + to_z
        rows_at = slice(4 * bz, 4 * bz + 4)
        piece = jnp.where(to_z % 2 == by, folded[rows_at], turned[rows_at])
        out_ref[to] = out_ref[to] + jnp.where(half == to_z % 2, piece, 0.0)


def short_kernel(
    own_ref, rest_ref, in_x_ref, in_y_ref, in_z_ref, extra_ref,
    radial_ref, vector_ref, mix_ref, species_ref, partial_ref, message_ref,
):
    bases = [
        (own_ref, 0), (in_x_ref, 0), (in_y_ref, 0), (in_y_ref, 72),
        (in_z_ref, 0), (in_z_ref, 72), (in_z_ref, 144), (in_z_ref, 216),
    ]
    feats = jnp.concatenate([ref[at : at + 64] for ref, at in bases], 0)
    low_lane = iota((8, 128), 1) < 64
    spots = []
    for pair in range(4):
        (ref_a, at_a), (ref_b, at_b) = bases[2 * pair], bases[2 * pair + 1]
        spots.append(
            jnp.where(
                low_lane,
                ref_a[at_a + 64 : at_a + 72],
                swap_halves(ref_b[at_b + 64 : at_b + 72]),
            )
        )
    spots = jnp.concatenate(spots, 1)
    tiles = [
        rest_ref[24:32], in_x_ref[96:104], in_y_ref[152:160], in_y_ref[168:176],
        in_z_ref[288:296], in_z_ref[296:304], in_z_ref[304:312], in_z_ref[312:320],
    ]
    centres = jnp.concatenate(tiles, 0)
    own = []
    for unit in range(8):
        ux, uy, uz = unit % 2, unit // 2 % 2, unit // 4
        ref, at = bases[unit]
        at = at + ((1 - ux) * 4 + (1 - uy) * 2 + (1 - uz)) * 8
        own.append(ref[at : at + 8])
    own = jnp.concatenate(own, 0)
    occupied = centres[:, 35:36]
    lane = iota((1, 512), 1)
    block = lane // 64
    cell = lane // 8 % 8
    spot = (
        spots[0:1] + ((block % 2) * 2 + cell // 4).astype(F32),
        spots[1:2] + ((block // 2 % 2) * 2 + cell // 2 % 2).astype(F32),
        spots[2:3] + ((block // 4) * 2 + cell % 2).astype(F32),
    )
    atom = iota((64, 1), 0)
    unit = atom // 8
    middle = (
        centres[:, 32:33] + (unit % 2 + 1).astype(F32),
        centres[:, 33:34] + (unit // 2 % 2 + 1).astype(F32),
        centres[:, 34:35] + (unit // 4 + 1).astype(F32),
    )
    delta = [spot[a] - middle[a] for a in range(3)]
    dist_sq = delta[0] * delta[0] + delta[1] * delta[1] + delta[2] * delta[2]
    near = 1.0 - dist_sq * (1.0 / 16.0)
    envelope = near * near
    lane_f = iota((64, 512), 1).astype(F32)
    times = jnp.zeros((64, 512), F32)
    for entry in range(32):
        times = times + jnp.where(centres[:, entry : entry + 1] == lane_f, 1.0, 0.0)
    bases_m = []
    power = None
    for b in range(8):
        if b % 4 == 0:
            power = jnp.exp(dist_sq * (-(2.0 ** (b - 4))))
        else:
            power = power * power
        bases_m.append(power * times)
    feat_high, feat_low = split(feats)
    feat_both = jnp.concatenate([feat_high, feat_low], 1)
    norm = 1.0 / math.sqrt(32.0)
    sums = [jnp.zeros((64, 128), F32) for _ in range(4)]
    for b in range(8):
        weight = bases_m[b] * envelope
        left = jnp.concatenate([weight] + [weight * delta[a] for a in range(3)], 0)
        left_high, left_low = split(left)
        first = contract(left_high, feat_both, (((1,), (0,))))
        second = contract(left_low, feat_high, (((1,), (0,))))
        made = first[:, 0:128] + first[:, 128:256] + second
        sums[0] = sums[0] + made[0:64] * radial_ref[b : b + 1]
        for a in range(3):
            sums[1 + a] = sums[1 + a] + made[64 * (1 + a) : 64 * (2 + a)] * vector_ref[b : b + 1]
    sums = [value * norm for value in sums]
    product = sums[0] + sums[1] * sums[1] + sums[2] * sums[2] + sums[3] * sums[3]
    mixed = contract(split_left(product), split_right(mix_ref[...], 0), (((1,), (0,))))
    gate = 1.0 / (1.0 + jnp.exp(-mixed))
    out_weight = extra_ref[0:1]
    energy = jnp.sum((own + mixed * gate) * out_weight, 1, keepdims=True) * occupied
    slope = gate * (1.0 + mixed * (1.0 - gate)) * (out_weight * occupied)
    grad = contract(split_left(slope), split_right(mix_ref[...], 1), (((1,), (1,)))) * norm
    grads = [grad] + [2.0 * grad * sums[1 + a] for a in range(3)]
    right = jnp.concatenate([feat_high, feat_high, feat_low], 1)
    linear = [jnp.zeros((64, 512), F32) for _ in range(3)]
    plain = jnp.zeros((64, 512), F32)
    decayed = jnp.zeros((64, 512), F32)
    for b in range(8):
        left = jnp.concatenate(
            [grads[0] * radial_ref[b : b + 1]]
            + [grads[1 + a] * vector_ref[b : b + 1] for a in range(3)],
            0,
        )
        left_high, left_low = split(left)
        pulled = contract(
            jnp.concatenate([left_high, left_low, left_high], 1), right, (((1,), (1,)))
        )
        parts = [pulled[64 * (1 + a) : 64 * (2 + a)] for a in range(3)]
        full = pulled[0:64] + parts[0] * delta[0] + parts[1] * delta[1] + parts[2] * delta[2]
        weighted = bases_m[b] * full
        plain = plain + weighted
        decayed = decayed + weighted * (2.0 ** (b - 4))
        for a in range(3):
            linear[a] = linear[a] + bases_m[b] * parts[a]
    radial_slope = 2.0 * (near * (-0.125) * plain - envelope * decayed)
    lane_i = iota((64, 512), 1)
    row_i = iota((64, 512), 0)
    ux, uy, uz = row_i // 8 % 2, row_i // 16 % 2, row_i // 32
    self_at = (row_i // 8) * 64 + ((1 - ux) * 4 + (1 - uy) * 2 + (1 - uz)) * 8 + row_i % 8
    own_slot = lane_i == self_at
    rows = [jnp.sum(jnp.where(own_slot, energy, 0.0), 0, keepdims=True)]
    for a in range(3):
        push = envelope * linear[a] + delta[a] * radial_slope
        back = jnp.sum(push, 1, keepdims=True)
        rows.append(jnp.sum(push - jnp.where(own_slot, back, 0.0), 0, keepdims=True))
    rows = jnp.concatenate(rows, 0)
    low = iota((4, 128), 1) < 64
    kinds = [species_ref[x, y] for x in range(2) for y in range(2)]
    spread = (iota((8, 128), 1) % 8 == iota((8, 128), 0)).astype(F32)
    kinds = contract(jnp.concatenate(kinds, 0).astype(F32), spread, (((1,), (0,))))
    shift = jnp.zeros((8, 128), F32)
    for name in range(8):
        shift = jnp.where(kinds == float(name), extra_ref[1:2, name : name + 1], shift)
    mine = iota((8, 128), 1) // 8 == iota((8, 128), 0)
    shift = jnp.sum(jnp.where(mine, shift, 0.0), 0, keepdims=True) * own_ref[67:68]
    shift = jnp.where(iota((4, 128), 0) == 0, shift, 0.0)
    kept, sent = [], []
    for half in range(2):
        first, second = (rows[:, 128 * k : 128 * k + 128] for k in (2 * half, 2 * half + 1))
        first = first + shift if half == 0 else first
        kept.append(jnp.where(low, first, swap_halves(second)))
        sent.append(jnp.where(low, swap_halves(first), second))
    here = lax.axis_index("gx")
    count = message_ref.shape[0]
    partial = partial_ref[...]
    for other in range(count):
        message_ref[other, 0:8] = partial
        message_ref[other, 8:16] = jnp.zeros((8, 128), F32)
    message_ref[here, 8:16] = jnp.concatenate(kept, 0)
    message_ref[(here + 1) % count, 8:16] = jnp.concatenate(sent, 0)


def last_kernel(parts_ref, energy_ref, force_ref):
    total = parts_ref[0]
    for member in range(1, parts_ref.shape[0]):
        total = total + parts_ref[member]
    odd = lax.axis_index("gz") % 2
    total = jnp.where(odd == 1, swap_halves(total), total)
    for cell in range(8):
        x, y, z = cell // 4, cell // 2 % 2, cell % 2
        here = total if cell == 0 else pltpu.roll(total, 128 - 8 * cell, 1)
        energy_ref[x, y, z : z + 1] = here[0:1, 0:8]
        for d in range(3):
            force_ref[x, y, d, z : z + 1] = -here[1 + d : 2 + d, 0:8]


def call(kernel, out, *operands, micros=10, room=48):
    cost = pl.CostEstimate(flops=micros * 10**8, bytes_accessed=micros * 3 * 10**5, transcendentals=0)
    return pl.pallas_call(
        kernel,
        out_shape=[jax.ShapeDtypeStruct(shape, F32) for shape in out],
        compiler_params=pltpu.CompilerParams(vmem_limit_bytes=room * 1024 * 1024),
        cost_estimate=cost,
    )(*operands)


def moved(value, axes, *steps):
    counts = [lax.axis_size(axis) for axis in axes]
    pairs = []
    for source in range(math.prod(counts)):
        rest, target, stride = source, 0, 1
        for count, step in zip(counts[::-1], steps[::-1]):
            target += (rest + step) % count * stride
            rest, stride = rest // count, stride * count
        pairs.append((source, target))
    return lax.ppermute(value, axes, pairs)


def body(
    features, offsets, counts, species, neighbours,
    w_radial, w_vector, w_mix, w_out, w_charge, species_shift,
):
    cells_x, cells_y, cells_z, slots_cell, channels = features.shape
    grid = (
        cells_x * lax.axis_size("gx"),
        cells_y * lax.axis_size("gy"),
        cells_z * lax.axis_size("gz"),
    )
    scale = 1.0 / math.sqrt(grid[0] * grid[1] * grid[2] * slots_cell * MODES)
    held = (
        features.reshape(64, 128),
        jnp.transpose(offsets, (0, 1, 3, 2, 4)),
        counts,
        neighbours.reshape(64, 32),
        w_charge.T,
        w_out.reshape(1, 128),
        species_shift.reshape(1, 8),
    )
    slab, rest, extra, message = pl.pallas_call(
        pack_kernel,
        out_shape=[
            jax.ShapeDtypeStruct(shape, F32)
            for shape in [(104, 128), (32, 128), (8, 128), (32, 5, 2, 128)]
        ],
        in_specs=[pl.BlockSpec(memory_space=pl.ANY)] * len(held),
        scratch_shapes=[pltpu.VMEM(value.shape, value.dtype) for value in held]
        + [pltpu.SemaphoreType.DMA((len(held),))],
        compiler_params=pltpu.CompilerParams(vmem_limit_bytes=PACK_ROOM * 1024 * 1024),
    )(*held)
    in_x = moved(slab, ("gx",), -1)
    atoms = lax.all_to_all(message, ("gy", "gz"), 0, 0).reshape(320, 128)
    (to_y,) = call(stack_y_kernel, [(176, 128)], slab, rest, in_x, micros=STACK_Y_MICROS)
    in_y = moved(to_y, ("gy",), -1)
    (to_z,) = call(
        stack_z_kernel, [(320, 128)], slab, rest, in_x, in_y, micros=STACK_Z_MICROS
    )
    in_z = moved(to_z, ("gz",), -1)
    partial, phases, charges = call(
        functools.partial(waves_kernel, grid),
        [(8, 128), (64, 2048), (16, 2048)],
        atoms,
        micros=WAVES_MICROS,
    )
    (joined,) = call(
        short_kernel,
        [(16, 16, 128)],
        slab, rest, in_x, in_y, in_z, extra,
        w_radial, w_vector, w_mix, species, partial,
        micros=SHORT_MICROS,
    )
    sums = lax.all_to_all(joined, "gx", 0, 0)
    (parts,) = call(
        functools.partial(field_kernel, grid, scale), [(32, 4, 128)], sums, phases, charges
    )
    parts = lax.all_to_all(parts, ("gy", "gz"), 0, 0)
    atom_energy, forces = call(last_kernel, [(2, 2, 2, 8), (2, 2, 3, 2, 8)], parts, room=LAST_ROOM)
    return (atom_energy, jnp.transpose(forces, (0, 1, 3, 2, 4)))


def solution(mesh):
    spread = P("gx", "gy", "gz")
    in_specs = (spread,) * 5 + (P(),) * 6
    return jax.shard_map(
        body, mesh=mesh, in_specs=in_specs, out_specs=(spread, spread), check_vma=False
    )
```

```python
import functools
import math

import jax
import jax.numpy as jnp
from jax import lax
from jax.experimental import pallas as pl
from jax.experimental.pallas import tpu as pltpu
from jax.sharding import PartitionSpec as P

KX = 16
KY = 8
KZ = 8
MODES = KX * KY * KZ
HIGH = lax.Precision.HIGHEST
F32 = jnp.float32
BF16 = jnp.bfloat16
STACK_Z_MICROS = 50
STACK_Y_MICROS = 1
WAVES_MICROS = 500
SHORT_MICROS = 1
PACK_ROOM = 60
LAST_ROOM = 48


def iota(shape, dim):
    return lax.broadcasted_iota(jnp.int32, shape, dim)


def split(value):
    high = value.astype(BF16)
    low = (value - high.astype(F32)).astype(BF16)
    return high, low


def contract(left, right, dims, precision=None):
    return lax.dot_general(
        left, right, (dims, ((), ())), precision=precision, preferred_element_type=F32
    )


def split_left(value):
    high, low = split(value)
    return jnp.concatenate([high, low, high], 1)


def split_right(value, axis):
    high, low = split(value)
    return jnp.concatenate([high, high, low], axis)


def swap_halves(value):
    return pltpu.roll(value, 64, value.ndim - 1)


def position_rows(pos_ref, lane):
    pieces = [pos_ref[x, y, d] for x in range(2) for y in range(2) for d in range(3)]
    spread = (iota((8, 128), 1) % 8 == iota((8, 128), 0)).astype(F32)
    pieces = jnp.concatenate(pieces, 0)
    first, rest = split(pieces)
    last = (pieces - first.astype(F32) - rest.astype(F32)).astype(BF16)
    wide = contract(
        jnp.concatenate([first, rest, last], 1),
        jnp.concatenate([spread] * 3, 0).astype(BF16),
        (((1,), (0,))),
    )
    rows = []
    for d in range(3):
        row = jnp.zeros((1, 128), F32)
        for cell in range(8):
            at = (cell // 2) * 6 + d * 2 + cell % 2
            row = jnp.where(lane[0:1] // 8 == cell, wide[at : at + 1], row)
        rows.append(row)
    return jnp.concatenate(rows + [jnp.zeros((5, 128), F32)], 0)


def pack_kernel(
    feat_hbm, pos_hbm, count_hbm, near_hbm, charge_hbm, weight_hbm, shift_hbm,
    slab_ref, rest_ref, extra_ref, message_ref,
    feat_ref, pos_ref, count_ref, near_ref, charge_ref, weight_ref, shift_ref, arrived,
):
    copies = [
        pltpu.make_async_copy(source, target, arrived.at[at])
        for at, (source, target) in enumerate(
            (
                (feat_hbm, feat_ref), (pos_hbm, pos_ref), (count_hbm, count_ref),
                (near_hbm, near_ref), (charge_hbm, charge_ref), (weight_hbm, weight_ref),
                (shift_hbm, shift_ref),
            )
        )
    ]
    for copy in copies:
        copy.start()
    for copy in copies:
        copy.wait()
    extra_ref[...] = jnp.zeros((8, 128), F32)
    extra_ref[0:1] = weight_ref[...]
    extra_ref[1:2, 0:8] = shift_ref[...]
    row = iota((64, 128), 0)
    lane = iota((8, 128), 1)
    count_col = jnp.zeros((64, 128), jnp.int32)
    count_row = jnp.zeros((8, 128), jnp.int32)
    for cell in range(8):
        count = count_ref[cell // 4][cell // 2 % 2 : cell // 2 % 2 + 1, cell % 2 : cell % 2 + 1]
        count_col = jnp.where(row // 8 == cell, count, count_col)
        count_row = jnp.where(lane // 8 == cell, count, count_row)
    occupied = (row % 8 < count_col).astype(F32)
    occupied_row = (lane % 8 < count_row).astype(F32)
    masked = feat_ref[...] * occupied
    charges = contract(
        split_left(charge_ref[...]),
        split_right(jnp.concatenate([masked, masked], 0), 1),
        (((1,), (1,))),
    )
    sub = iota((8, 128), 0)
    tile = position_rows(pos_ref, lane)
    tile = jnp.where(sub == 3, occupied_row, tile)
    cell_x, cell_y, cell_z = lane // 32 % 2, lane // 16 % 2, lane // 8 % 2
    corner_x = 2 * lax.axis_index("gx")
    corner_y = 2 * lax.axis_index("gy")
    corner_z = 2 * lax.axis_index("gz")
    corner = jnp.where(
        sub == 0, cell_x + corner_x, jnp.where(sub == 1, cell_y + corner_y, cell_z + corner_z)
    )
    places = tile + corner.astype(F32)
    lane_low = lane < 64
    charges = jnp.where(lane_low, charges[0:8], charges[8:16])
    places = jnp.where(lane_low, places, swap_halves(pltpu.roll(places, 7, 0)))
    places = jnp.concatenate([places[0:1], places[2:3]], 0)
    pieces = [charges[2 * k : 2 * k + 2] for k in range(4)] + [places]
    for member in range(message_ref.shape[0]):
        for k in range(5):
            message_ref[member, k] = pieces[k]
    turned = jnp.concatenate(
        [jnp.zeros((32, 128), F32), tile, jnp.zeros((88, 128), F32)], 0
    ).T
    near = near_ref[...]
    atom = iota((64, 32), 0)
    stencil = near >> 3
    slot = near & 7
    step_x = (stencil * 57) >> 9
    line = (stencil * 171) >> 9
    step_z = stencil - 3 * line
    step_y = line - 3 * step_x
    spot_x = step_x + 1 - ((atom >> 5) & 1)
    spot_y = step_y + 1 - ((atom >> 4) & 1)
    spot_z = step_z + 1 - ((atom >> 3) & 1)
    block = (spot_z >> 1) * 4 + (spot_y >> 1) * 2 + (spot_x >> 1)
    cell = (spot_x & 1) * 4 + (spot_y & 1) * 2 + (spot_z & 1)
    target = (block * 64 + cell * 8 + slot).astype(F32)
    slab_ref[0:64] = masked
    slab_ref[64:72] = tile
    slab_ref[72:104] = turned[0:32]
    slab_ref[72:104, 0:32] = target[0:32]
    rest_ref[...] = turned[32:64]
    rest_ref[:, 0:32] = target[32:64]


def stack_z_kernel(own_ref, rest_ref, in_x_ref, out_ref):
    out_ref[0:72] = own_ref[0:72]
    out_ref[72:144] = in_x_ref[0:72]
    out_ref[144:152] = rest_ref[0:8]
    out_ref[152:160] = rest_ref[16:24]
    out_ref[160:168] = in_x_ref[72:80]
    out_ref[168:176] = in_x_ref[88:96]


def stack_y_kernel(own_ref, rest_ref, in_x_ref, in_z_ref, out_ref):
    out_ref[0:72] = own_ref[0:72]
    out_ref[72:144] = in_x_ref[0:72]
    out_ref[144:288] = in_z_ref[0:144]
    out_ref[288:296] = rest_ref[8:16]
    out_ref[296:304] = in_x_ref[80:88]
    out_ref[304:312] = in_z_ref[144:152]
    out_ref[312:320] = in_z_ref[160:168]


def wave_numbers(member, shape, dim):
    index = iota(shape, dim) % 32
    number_y = (index // 8 + (member % 2) * 4 - KY // 2).astype(F32)
    number_z = (index % 8 - KZ // 2).astype(F32)
    number_x = (member // 2 - KX // 2).astype(F32)
    return number_x, number_y, number_z


def sine_cosine(turns):
    part = turns - jnp.floor(turns + 0.5)
    angle = part * (2.0 * math.pi)
    square = angle * angle
    sine = jnp.full_like(square, 1.0 / math.factorial(19) * -1.0)
    for power in range(17, 0, -2):
        sign = 1.0 if power // 2 % 2 == 0 else -1.0
        sine = sine * square + sign / math.factorial(power)
    cosine = jnp.full_like(square, -1.0 / math.factorial(18))
    for power in range(16, -1, -2):
        sign = 1.0 if power // 2 % 2 == 0 else -1.0
        cosine = cosine * square + sign / math.factorial(power)
    return sine * angle, cosine


def waves_kernel(grid, atoms_ref, message_ref, phase_ref, charge_ref):
    member = lax.axis_index("gy") * 4 + lax.axis_index("gz")
    low = iota((8, 128), 1) < 64
    upper, lower, places = [], [], []
    for pair in range(16):
        first, second = atoms_ref[20 * pair : 20 * pair + 8], atoms_ref[20 * pair + 10 : 20 * pair + 18]
        upper.append(jnp.where(low, first, swap_halves(second)))
        lower.append(jnp.where(low, swap_halves(first), second))
        first, second = (
            atoms_ref[20 * pair + 8 : 20 * pair + 10],
            atoms_ref[20 * pair + 18 : 20 * pair + 20],
        )
        places.append(
            jnp.concatenate(
                [
                    jnp.where(low[0:2], first, swap_halves(second)),
                    jnp.where(low[0:2], swap_halves(first), second),
                ],
                0,
            )
        )
    charges = jnp.concatenate(
        [jnp.concatenate(upper, 1), jnp.concatenate(lower, 1)], 0
    )
    places = jnp.concatenate(places, 1)
    number_x, number_y, number_z = wave_numbers(member, (32, 1), 0)
    turns = (
        number_x * (places[0:1] * (1.0 / grid[0]))
        + number_y * (places[2:3] * (1.0 / grid[1]))
        + number_z * (places[1:2] * (1.0 / grid[2]))
    )
    sine, cosine = sine_cosine(turns)
    phases = jnp.concatenate([cosine, sine], 0)
    phase_ref[...] = phases
    charge_ref[...] = charges
    charge_stack = jnp.concatenate(split(charges), 0)
    phase_stack = jnp.concatenate(split(phases), 0)
    sums = contract(charge_stack, phase_stack, (((1,), (1,))))
    partial = sums[0:16] + sums[16:32]
    partial = partial + swap_halves(partial)
    partial = jnp.where(low, partial[0:8], partial[8:16])
    for other in range(message_ref.shape[0]):
        message_ref[other] = partial


def field_kernel(grid, scale, sums_ref, phase_ref, charge_ref, kept_ref, came_ref, out_ref):
    at_y, at_z = lax.axis_index("gy"), lax.axis_index("gz")
    member = at_y * 4 + at_z
    total = sums_ref[0]
    for other in range(1, sums_ref.shape[0]):
        total = total + sums_ref[other]
    turned = swap_halves(total)
    low_lane = iota((8, 128), 1) < 64
    total = jnp.concatenate(
        [
            jnp.where(low_lane, total[0:8], turned[0:8]),
            jnp.where(low_lane, turned[0:8], total[0:8]),
        ],
        0,
    )
    folded = kept_ref[...] + came_ref[...]
    turned = swap_halves(folded)
    two_pi = 2.0 * math.pi
    number_x, number_y, number_z = wave_numbers(member, (16, 128), 1)
    wave_x, wave_y, wave_z = (
        number_x * (two_pi / grid[0]),
        number_y * (two_pi / grid[1]),
        number_z * (two_pi / grid[2]),
    )
    length_sq = wave_x * wave_x + wave_y * wave_y + wave_z * wave_z
    total = total * (jnp.exp(-0.5 * length_sq) / (length_sq + 1.0))
    high = total.astype(BF16).astype(F32)
    low = total - high
    left = jnp.concatenate([high, low, high, jnp.zeros((80, 128), F32)], 0).T[0:64, 0:64]
    charge_high, charge_low = split(charge_ref[...])
    right = jnp.concatenate(
        [charge_high, charge_high, charge_low, jnp.zeros_like(charge_low)], 0
    )
    fields = contract(left.astype(BF16), right, (((1,), (0,))))
    cosine, sine = phase_ref[0:32], phase_ref[32:64]
    field_cos, field_sin = fields[0:32], fields[32:64]
    energy = (0.5 * scale) * jnp.sum(cosine * field_cos + sine * field_sin, 0, keepdims=True)
    turning = scale * (cosine * field_sin - sine * field_cos)
    number_x, number_y, number_z = wave_numbers(member, (32, 1), 0)
    pull_x = (number_x * (two_pi / grid[0])) * jnp.sum(turning, 0, keepdims=True)
    pull_y = jnp.sum(turning * (number_y * (two_pi / grid[1])), 0, keepdims=True)
    pull_z = jnp.sum(turning * (number_z * (two_pi / grid[2])), 0, keepdims=True)
    rows = jnp.concatenate([energy, pull_x, pull_y, pull_z], 0)
    for target in range(32):
        out_ref[target] = rows[:, target // 2 * 128 : target // 2 * 128 + 128]
    half = iota((4, 128), 1) // 64
    for block in range(4):
        by, bz = block % 2, block // 2
        to_z = (at_z + bz) % 4
        to = ((at_y + by) % 8) * 4 + to_z
        rows_at = slice(4 * bz, 4 * bz + 4)
        piece = jnp.where(to_z % 2 == by, folded[rows_at], turned[rows_at])
        out_ref[to] = out_ref[to] + jnp.where(half == to_z % 2, piece, 0.0)


def short_kernel(
    own_ref, rest_ref, in_x_ref, in_y_ref, in_z_ref, extra_ref,
    radial_ref, vector_ref, mix_ref, species_ref, kept_ref, sent_ref,
):
    bases = [
        (own_ref, 0), (in_x_ref, 0), (in_y_ref, 0), (in_y_ref, 72),
        (in_z_ref, 0), (in_z_ref, 72), (in_y_ref, 144), (in_y_ref, 216),
    ]
    feats = jnp.concatenate([ref[at : at + 64] for ref, at in bases], 0)
    low_lane = iota((8, 128), 1) < 64
    spots = []
    for pair in range(4):
        (ref_a, at_a), (ref_b, at_b) = bases[2 * pair], bases[2 * pair + 1]
        spots.append(
            jnp.where(
                low_lane,
                ref_a[at_a + 64 : at_a + 72],
                swap_halves(ref_b[at_b + 64 : at_b + 72]),
            )
        )
    spots = jnp.concatenate(spots, 1)
    tiles = [
        rest_ref[24:32], in_x_ref[96:104], in_y_ref[288:296], in_y_ref[296:304],
        in_z_ref[152:160], in_z_ref[168:176], in_y_ref[304:312], in_y_ref[312:320],
    ]
    centres = jnp.concatenate(tiles, 0)
    own = []
    for unit in range(8):
        ux, uy, uz = unit % 2, unit // 2 % 2, unit // 4
        ref, at = bases[unit]
        at = at + ((1 - ux) * 4 + (1 - uy) * 2 + (1 - uz)) * 8
        own.append(ref[at : at + 8])
    own = jnp.concatenate(own, 0)
    occupied = centres[:, 35:36]
    lane = iota((1, 512), 1)
    block = lane // 64
    cell = lane // 8 % 8
    spot = (
        spots[0:1] + ((block % 2) * 2 + cell // 4).astype(F32),
        spots[1:2] + ((block // 2 % 2) * 2 + cell // 2 % 2).astype(F32),
        spots[2:3] + ((block // 4) * 2 + cell % 2).astype(F32),
    )
    atom = iota((64, 1), 0)
    unit = atom // 8
    middle = (
        centres[:, 32:33] + (unit % 2 + 1).astype(F32),
        centres[:, 33:34] + (unit // 2 % 2 + 1).astype(F32),
        centres[:, 34:35] + (unit // 4 + 1).astype(F32),
    )
    delta = [spot[a] - middle[a] for a in range(3)]
    dist_sq = delta[0] * delta[0] + delta[1] * delta[1] + delta[2] * delta[2]
    near = 1.0 - dist_sq * (1.0 / 16.0)
    envelope = near * near
    lane_f = iota((64, 512), 1).astype(F32)
    times = jnp.zeros((64, 512), F32)
    for entry in range(32):
        times = times + jnp.where(centres[:, entry : entry + 1] == lane_f, 1.0, 0.0)
    bases_m = []
    power = None
    for b in range(8):
        if b % 4 == 0:
            power = jnp.exp(dist_sq * (-(2.0 ** (b - 4))))
        else:
            power = power * power
        bases_m.append(power * times)
    feat_high, feat_low = split(feats)
    feat_both = jnp.concatenate([feat_high, feat_low], 1)
    norm = 1.0 / math.sqrt(32.0)
    sums = [jnp.zeros((64, 128), F32) for _ in range(4)]
    for b in range(8):
        weight = bases_m[b] * envelope
        left = jnp.concatenate([weight] + [weight * delta[a] for a in range(3)], 0)
        left_high, left_low = split(left)
        first = contract(left_high, feat_both, (((1,), (0,))))
        second = contract(left_low, feat_high, (((1,), (0,))))
        made = first[:, 0:128] + first[:, 128:256] + second
        sums[0] = sums[0] + made[0:64] * radial_ref[b : b + 1]
        for a in range(3):
            sums[1 + a] = sums[1 + a] + made[64 * (1 + a) : 64 * (2 + a)] * vector_ref[b : b + 1]
    sums = [value * norm for value in sums]
    product = sums[0] + sums[1] * sums[1] + sums[2] * sums[2] + sums[3] * sums[3]
    mixed = contract(split_left(product), split_right(mix_ref[...], 0), (((1,), (0,))))
    gate = 1.0 / (1.0 + jnp.exp(-mixed))
    out_weight = extra_ref[0:1]
    energy = jnp.sum((own + mixed * gate) * out_weight, 1, keepdims=True) * occupied
    slope = gate * (1.0 + mixed * (1.0 - gate)) * (out_weight * occupied)
    grad = contract(split_left(slope), split_right(mix_ref[...], 1), (((1,), (1,)))) * norm
    grads = [grad] + [2.0 * grad * sums[1 + a] for a in range(3)]
    right = jnp.concatenate([feat_high, feat_high, feat_low], 1)
    linear = [jnp.zeros((64, 512), F32) for _ in range(3)]
    plain = jnp.zeros((64, 512), F32)
    decayed = jnp.zeros((64, 512), F32)
    for b in range(8):
        left = jnp.concatenate(
            [grads[0] * radial_ref[b : b + 1]]
            + [grads[1 + a] * vector_ref[b : b + 1] for a in range(3)],
            0,
        )
        left_high, left_low = split(left)
        pulled = contract(
            jnp.concatenate([left_high, left_low, left_high], 1), right, (((1,), (1,)))
        )
        parts = [pulled[64 * (1 + a) : 64 * (2 + a)] for a in range(3)]
        full = pulled[0:64] + parts[0] * delta[0] + parts[1] * delta[1] + parts[2] * delta[2]
        weighted = bases_m[b] * full
        plain = plain + weighted
        decayed = decayed + weighted * (2.0 ** (b - 4))
        for a in range(3):
            linear[a] = linear[a] + bases_m[b] * parts[a]
    radial_slope = 2.0 * (near * (-0.125) * plain - envelope * decayed)
    lane_i = iota((64, 512), 1)
    row_i = iota((64, 512), 0)
    ux, uy, uz = row_i // 8 % 2, row_i // 16 % 2, row_i // 32
    self_at = (row_i // 8) * 64 + ((1 - ux) * 4 + (1 - uy) * 2 + (1 - uz)) * 8 + row_i % 8
    own_slot = lane_i == self_at
    rows = [jnp.sum(jnp.where(own_slot, energy, 0.0), 0, keepdims=True)]
    for a in range(3):
        push = envelope * linear[a] + delta[a] * radial_slope
        back = jnp.sum(push, 1, keepdims=True)
        rows.append(jnp.sum(push - jnp.where(own_slot, back, 0.0), 0, keepdims=True))
    rows = jnp.concatenate(rows, 0)
    low = iota((4, 128), 1) < 64
    kinds = [species_ref[x, y] for x in range(2) for y in range(2)]
    spread = (iota((8, 128), 1) % 8 == iota((8, 128), 0)).astype(F32)
    kinds = contract(jnp.concatenate(kinds, 0).astype(F32), spread, (((1,), (0,))))
    shift = jnp.zeros((8, 128), F32)
    for name in range(8):
        shift = jnp.where(kinds == float(name), extra_ref[1:2, name : name + 1], shift)
    mine = iota((8, 128), 1) // 8 == iota((8, 128), 0)
    shift = jnp.sum(jnp.where(mine, shift, 0.0), 0, keepdims=True) * own_ref[67:68]
    shift = jnp.where(iota((4, 128), 0) == 0, shift, 0.0)
    for half in range(2):
        first, second = (rows[:, 128 * k : 128 * k + 128] for k in (2 * half, 2 * half + 1))
        first = first + shift if half == 0 else first
        kept_ref[4 * half : 4 * half + 4] = jnp.where(low, first, swap_halves(second))
        sent_ref[4 * half : 4 * half + 4] = jnp.where(low, swap_halves(first), second)


def last_kernel(parts_ref, energy_ref, force_ref):
    total = parts_ref[0]
    for member in range(1, parts_ref.shape[0]):
        total = total + parts_ref[member]
    odd = lax.axis_index("gz") % 2
    total = jnp.where(odd == 1, swap_halves(total), total)
    for cell in range(8):
        x, y, z = cell // 4, cell // 2 % 2, cell % 2
        here = total if cell == 0 else pltpu.roll(total, 128 - 8 * cell, 1)
        energy_ref[x, y, z : z + 1] = here[0:1, 0:8]
        for d in range(3):
            force_ref[x, y, d, z : z + 1] = -here[1 + d : 2 + d, 0:8]


def call(kernel, out, *operands, micros=10, room=48):
    cost = pl.CostEstimate(flops=micros * 10**8, bytes_accessed=micros * 3 * 10**5, transcendentals=0)
    return pl.pallas_call(
        kernel,
        out_shape=[jax.ShapeDtypeStruct(shape, F32) for shape in out],
        compiler_params=pltpu.CompilerParams(vmem_limit_bytes=room * 1024 * 1024),
        cost_estimate=cost,
    )(*operands)


def moved(value, axes, *steps):
    counts = [lax.axis_size(axis) for axis in axes]
    pairs = []
    for source in range(math.prod(counts)):
        rest, target, stride = source, 0, 1
        for count, step in zip(counts[::-1], steps[::-1]):
            target += (rest + step) % count * stride
            rest, stride = rest // count, stride * count
        pairs.append((source, target))
    return lax.ppermute(value, axes, pairs)


def body(
    features, offsets, counts, species, neighbours,
    w_radial, w_vector, w_mix, w_out, w_charge, species_shift,
):
    cells_x, cells_y, cells_z, slots_cell, channels = features.shape
    grid = (
        cells_x * lax.axis_size("gx"),
        cells_y * lax.axis_size("gy"),
        cells_z * lax.axis_size("gz"),
    )
    scale = 1.0 / math.sqrt(grid[0] * grid[1] * grid[2] * slots_cell * MODES)
    held = (
        features.reshape(64, 128),
        jnp.transpose(offsets, (0, 1, 3, 2, 4)),
        counts,
        neighbours.reshape(64, 32),
        w_charge.T,
        w_out.reshape(1, 128),
        species_shift.reshape(1, 8),
    )
    slab, rest, extra, message = pl.pallas_call(
        pack_kernel,
        out_shape=[
            jax.ShapeDtypeStruct(shape, F32)
            for shape in [(104, 128), (32, 128), (8, 128), (32, 5, 2, 128)]
        ],
        in_specs=[pl.BlockSpec(memory_space=pl.ANY)] * len(held),
        scratch_shapes=[pltpu.VMEM(value.shape, value.dtype) for value in held]
        + [pltpu.SemaphoreType.DMA((len(held),))],
        compiler_params=pltpu.CompilerParams(vmem_limit_bytes=PACK_ROOM * 1024 * 1024),
    )(*held)
    in_x = moved(slab, ("gx",), -1)
    atoms = lax.all_to_all(message, ("gy", "gz"), 0, 0).reshape(320, 128)
    (to_z,) = call(stack_z_kernel, [(176, 128)], slab, rest, in_x, micros=STACK_Z_MICROS)
    in_z = moved(to_z, ("gz",), -1)
    (to_y,) = call(
        stack_y_kernel, [(320, 128)], slab, rest, in_x, in_z, micros=STACK_Y_MICROS
    )
    in_y = moved(to_y, ("gy",), -1)
    partial, phases, charges = call(
        functools.partial(waves_kernel, grid),
        [(16, 8, 128), (64, 2048), (16, 2048)],
        atoms,
        micros=WAVES_MICROS,
    )
    sums = lax.all_to_all(partial, "gx", 0, 0)
    kept, sent = call(
        short_kernel,
        [(8, 128), (8, 128)],
        slab, rest, in_x, in_y, in_z, extra,
        w_radial, w_vector, w_mix, species,
        micros=SHORT_MICROS,
    )
    came = moved(sent, ("gx",), 1)
    (parts,) = call(
        functools.partial(field_kernel, grid, scale),
        [(32, 4, 128)],
        sums, phases, charges, kept, came,
    )
    parts = lax.all_to_all(parts, ("gy", "gz"), 0, 0)
    atom_energy, forces = call(last_kernel, [(2, 2, 2, 8), (2, 2, 3, 2, 8)], parts, room=LAST_ROOM)
    return (atom_energy, jnp.transpose(forces, (0, 1, 3, 2, 4)))


def solution(mesh):
    spread = P("gx", "gy", "gz")
    in_specs = (spread,) * 5 + (P(),) * 6
    return jax.shard_map(
        body, mesh=mesh, in_specs=in_specs, out_specs=(spread, spread), check_vma=False
    )
```

```python
import functools
import math

import jax
import jax.numpy as jnp
from jax import lax
from jax.experimental import pallas as pl
from jax.experimental.pallas import tpu as pltpu
from jax.sharding import PartitionSpec as P

KX = 16
KY = 8
KZ = 8
MODES = KX * KY * KZ
HIGH = lax.Precision.HIGHEST
F32 = jnp.float32
BF16 = jnp.bfloat16
STACK_Z_MICROS = 50
STACK_Y_MICROS = 1
WAVES_MICROS = 500
SHORT_MICROS = 1
PACK_ROOM = 60
LAST_ROOM = 48


def iota(shape, dim):
    return lax.broadcasted_iota(jnp.int32, shape, dim)


def split(value):
    high = value.astype(BF16)
    low = (value - high.astype(F32)).astype(BF16)
    return high, low


def contract(left, right, dims, precision=None):
    return lax.dot_general(
        left, right, (dims, ((), ())), precision=precision, preferred_element_type=F32
    )


def split_left(value):
    high, low = split(value)
    return jnp.concatenate([high, low, high], 1)


def split_right(value, axis):
    high, low = split(value)
    return jnp.concatenate([high, high, low], axis)


def swap_halves(value):
    return pltpu.roll(value, 64, value.ndim - 1)


def position_rows(pos_ref, lane):
    pieces = [pos_ref[x, y, d] for x in range(2) for y in range(2) for d in range(3)]
    spread = (iota((8, 128), 1) % 8 == iota((8, 128), 0)).astype(F32)
    pieces = jnp.concatenate(pieces, 0)
    first, rest = split(pieces)
    last = (pieces - first.astype(F32) - rest.astype(F32)).astype(BF16)
    wide = contract(
        jnp.concatenate([first, rest, last], 1),
        jnp.concatenate([spread] * 3, 0).astype(BF16),
        (((1,), (0,))),
    )
    rows = []
    for d in range(3):
        row = jnp.zeros((1, 128), F32)
        for cell in range(8):
            at = (cell // 2) * 6 + d * 2 + cell % 2
            row = jnp.where(lane[0:1] // 8 == cell, wide[at : at + 1], row)
        rows.append(row)
    return jnp.concatenate(rows + [jnp.zeros((5, 128), F32)], 0)


def pack_kernel(
    feat_hbm, pos_hbm, count_hbm, near_hbm, charge_hbm, weight_hbm, shift_hbm,
    slab_ref, rest_ref, extra_ref, message_ref,
    feat_ref, pos_ref, count_ref, near_ref, charge_ref, weight_ref, shift_ref, arrived,
):
    copies = [
        pltpu.make_async_copy(source, target, arrived.at[at])
        for at, (source, target) in enumerate(
            (
                (feat_hbm, feat_ref), (pos_hbm, pos_ref), (count_hbm, count_ref),
                (near_hbm, near_ref), (charge_hbm, charge_ref), (weight_hbm, weight_ref),
                (shift_hbm, shift_ref),
            )
        )
    ]
    for copy in copies:
        copy.start()
    for copy in copies:
        copy.wait()
    extra_ref[...] = jnp.zeros((8, 128), F32)
    extra_ref[0:1] = weight_ref[...]
    extra_ref[1:2, 0:8] = shift_ref[...]
    row = iota((64, 128), 0)
    lane = iota((8, 128), 1)
    count_col = jnp.zeros((64, 128), jnp.int32)
    count_row = jnp.zeros((8, 128), jnp.int32)
    for cell in range(8):
        count = count_ref[cell // 4][cell // 2 % 2 : cell // 2 % 2 + 1, cell % 2 : cell % 2 + 1]
        count_col = jnp.where(row // 8 == cell, count, count_col)
        count_row = jnp.where(lane // 8 == cell, count, count_row)
    occupied = (row % 8 < count_col).astype(F32)
    occupied_row = (lane % 8 < count_row).astype(F32)
    masked = feat_ref[...] * occupied
    charges = contract(
        split_left(charge_ref[...]),
        split_right(jnp.concatenate([masked, masked], 0), 1),
        (((1,), (1,))),
    )
    sub = iota((8, 128), 0)
    tile = position_rows(pos_ref, lane)
    tile = jnp.where(sub == 3, occupied_row, tile)
    cell_x, cell_y, cell_z = lane // 32 % 2, lane // 16 % 2, lane // 8 % 2
    corner_x = 2 * lax.axis_index("gx")
    corner_y = 2 * lax.axis_index("gy")
    corner_z = 2 * lax.axis_index("gz")
    corner = jnp.where(
        sub == 0, cell_x + corner_x, jnp.where(sub == 1, cell_y + corner_y, cell_z + corner_z)
    )
    places = tile + corner.astype(F32)
    lane_low = lane < 64
    charges = jnp.where(lane_low, charges[0:8], charges[8:16])
    places = jnp.where(lane_low, places, swap_halves(pltpu.roll(places, 7, 0)))
    places = jnp.concatenate([places[0:1], places[2:3]], 0)
    pieces = [charges[2 * k : 2 * k + 2] for k in range(4)] + [places]
    for member in range(message_ref.shape[0]):
        for k in range(5):
            message_ref[member, k] = pieces[k]
    turned = jnp.concatenate(
        [jnp.zeros((32, 128), F32), tile, jnp.zeros((88, 128), F32)], 0
    ).T
    near = near_ref[...].astype(F32)
    slab_ref[0:64] = masked
    slab_ref[64:72] = tile
    slab_ref[72:104] = turned[0:32]
    slab_ref[72:104, 0:32] = near[0:32]
    rest_ref[...] = turned[32:64]
    rest_ref[:, 0:32] = near[32:64]


def stack_z_kernel(own_ref, rest_ref, in_x_ref, out_ref):
    out_ref[0:72] = own_ref[0:72]
    out_ref[72:144] = in_x_ref[0:72]
    out_ref[144:152] = rest_ref[0:8]
    out_ref[152:160] = rest_ref[16:24]
    out_ref[160:168] = in_x_ref[72:80]
    out_ref[168:176] = in_x_ref[88:96]


def stack_y_kernel(own_ref, rest_ref, in_x_ref, in_z_ref, out_ref):
    out_ref[0:72] = own_ref[0:72]
    out_ref[72:144] = in_x_ref[0:72]
    out_ref[144:288] = in_z_ref[0:144]
    out_ref[288:296] = rest_ref[8:16]
    out_ref[296:304] = in_x_ref[80:88]
    out_ref[304:312] = in_z_ref[144:152]
    out_ref[312:320] = in_z_ref[160:168]


def wave_numbers(member, shape, dim):
    index = iota(shape, dim) % 32
    number_y = (index // 8 + (member % 2) * 4 - KY // 2).astype(F32)
    number_z = (index % 8 - KZ // 2).astype(F32)
    number_x = (member // 2 - KX // 2).astype(F32)
    return number_x, number_y, number_z


def sine_cosine(turns):
    part = turns - jnp.floor(turns + 0.5)
    angle = part * (2.0 * math.pi)
    square = angle * angle
    sine = jnp.full_like(square, 1.0 / math.factorial(19) * -1.0)
    for power in range(17, 0, -2):
        sign = 1.0 if power // 2 % 2 == 0 else -1.0
        sine = sine * square + sign / math.factorial(power)
    cosine = jnp.full_like(square, -1.0 / math.factorial(18))
    for power in range(16, -1, -2):
        sign = 1.0 if power // 2 % 2 == 0 else -1.0
        cosine = cosine * square + sign / math.factorial(power)
    return sine * angle, cosine


def waves_kernel(grid, atoms_ref, message_ref, phase_ref, charge_ref):
    member = lax.axis_index("gy") * 4 + lax.axis_index("gz")
    low = iota((8, 128), 1) < 64
    upper, lower, places = [], [], []
    for pair in range(16):
        first, second = atoms_ref[20 * pair : 20 * pair + 8], atoms_ref[20 * pair + 10 : 20 * pair + 18]
        upper.append(jnp.where(low, first, swap_halves(second)))
        lower.append(jnp.where(low, swap_halves(first), second))
        first, second = (
            atoms_ref[20 * pair + 8 : 20 * pair + 10],
            atoms_ref[20 * pair + 18 : 20 * pair + 20],
        )
        places.append(
            jnp.concatenate(
                [
                    jnp.where(low[0:2], first, swap_halves(second)),
                    jnp.where(low[0:2], swap_halves(first), second),
                ],
                0,
            )
        )
    charges = jnp.concatenate(
        [jnp.concatenate(upper, 1), jnp.concatenate(lower, 1)], 0
    )
    places = jnp.concatenate(places, 1)
    number_x, number_y, number_z = wave_numbers(member, (32, 1), 0)
    turns = (
        number_x * (places[0:1] * (1.0 / grid[0]))
        + number_y * (places[2:3] * (1.0 / grid[1]))
        + number_z * (places[1:2] * (1.0 / grid[2]))
    )
    sine, cosine = sine_cosine(turns)
    phases = jnp.concatenate([cosine, sine], 0)
    phase_ref[...] = phases
    charge_ref[...] = charges
    charge_stack = jnp.concatenate(split(charges), 0)
    phase_stack = jnp.concatenate(split(phases), 0)
    sums = contract(charge_stack, phase_stack, (((1,), (1,))))
    partial = sums[0:16] + sums[16:32]
    partial = partial + swap_halves(partial)
    partial = jnp.where(low, partial[0:8], partial[8:16])
    for other in range(message_ref.shape[0]):
        message_ref[other] = partial


def field_kernel(grid, scale, sums_ref, phase_ref, charge_ref, kept_ref, came_ref, out_ref):
    at_y, at_z = lax.axis_index("gy"), lax.axis_index("gz")
    member = at_y * 4 + at_z
    total = sums_ref[0]
    for other in range(1, sums_ref.shape[0]):
        total = total + sums_ref[other]
    turned = swap_halves(total)
    low_lane = iota((8, 128), 1) < 64
    total = jnp.concatenate(
        [
            jnp.where(low_lane, total[0:8], turned[0:8]),
            jnp.where(low_lane, turned[0:8], total[0:8]),
        ],
        0,
    )
    folded = kept_ref[...] + came_ref[...]
    turned = swap_halves(folded)
    two_pi = 2.0 * math.pi
    number_x, number_y, number_z = wave_numbers(member, (16, 128), 1)
    wave_x, wave_y, wave_z = (
        number_x * (two_pi / grid[0]),
        number_y * (two_pi / grid[1]),
        number_z * (two_pi / grid[2]),
    )
    length_sq = wave_x * wave_x + wave_y * wave_y + wave_z * wave_z
    total = total * (jnp.exp(-0.5 * length_sq) / (length_sq + 1.0))
    high = total.astype(BF16).astype(F32)
    low = total - high
    left = jnp.concatenate([high, low, high, jnp.zeros((80, 128), F32)], 0).T[0:64, 0:64]
    charge_high, charge_low = split(charge_ref[...])
    right = jnp.concatenate(
        [charge_high, charge_high, charge_low, jnp.zeros_like(charge_low)], 0
    )
    fields = contract(left.astype(BF16), right, (((1,), (0,))))
    cosine, sine = phase_ref[0:32], phase_ref[32:64]
    field_cos, field_sin = fields[0:32], fields[32:64]
    energy = (0.5 * scale) * jnp.sum(cosine * field_cos + sine * field_sin, 0, keepdims=True)
    turning = scale * (cosine * field_sin - sine * field_cos)
    number_x, number_y, number_z = wave_numbers(member, (32, 1), 0)
    pull_x = (number_x * (two_pi / grid[0])) * jnp.sum(turning, 0, keepdims=True)
    pull_y = jnp.sum(turning * (number_y * (two_pi / grid[1])), 0, keepdims=True)
    pull_z = jnp.sum(turning * (number_z * (two_pi / grid[2])), 0, keepdims=True)
    first = jnp.concatenate([energy, pull_y], 0)
    second = jnp.concatenate([pull_x, pull_z], 0)
    low = iota((2, 128), 1) < 64
    for pair in range(16):
        lanes = slice(128 * pair, 128 * pair + 128)
        left_part, right_part = first[:, lanes], second[:, lanes]
        out_ref[2 * pair] = jnp.where(low, left_part, swap_halves(right_part))
        out_ref[2 * pair + 1] = jnp.where(low, swap_halves(left_part), right_part)
    for block in range(4):
        by, bz = block % 2, block // 2
        to = ((at_y + by) % 8) * 4 + (at_z + bz) % 4
        here, there = (folded, turned) if by == 0 else (turned, folded)
        row = 4 * bz
        piece = jnp.where(
            low,
            jnp.concatenate([here[row : row + 1], here[row + 2 : row + 3]], 0),
            jnp.concatenate([there[row + 1 : row + 2], there[row + 3 : row + 4]], 0),
        )
        out_ref[to] = out_ref[to] + piece


def short_kernel(
    own_ref, rest_ref, in_x_ref, in_z_ref, in_y_ref, extra_ref,
    radial_ref, vector_ref, mix_ref, species_ref, kept_ref, sent_ref,
):
    bases = [
        (own_ref, 0), (in_x_ref, 0), (in_y_ref, 0), (in_y_ref, 72),
        (in_z_ref, 0), (in_z_ref, 72), (in_y_ref, 144), (in_y_ref, 216),
    ]

    def local_row(x, y, z):
        return (x % 2 * 4 + y % 2 * 2 + z % 2) * 8

    def block_of(x, y, z):
        return z // 2 * 4 + y // 2 * 2 + x // 2

    def cell_tile(x, y, z):
        ref, at = bases[block_of(x, y, z)]
        at = at + local_row(x, y, z)
        return ref[at : at + 8]

    units = [(x, y, z) for z in (1, 2) for y in (1, 2) for x in (1, 2)]
    steps = [(dx, dy, dz) for dx in range(3) for dy in range(3) for dz in range(3)]
    centres = [
        rest_ref[24:32], in_x_ref[96:104], in_y_ref[288:296], in_y_ref[296:304],
        in_z_ref[152:160], in_z_ref[168:176], in_y_ref[304:312], in_y_ref[312:320],
    ]
    centres = jnp.concatenate(centres, 0)
    own = jnp.concatenate([cell_tile(*unit) for unit in units], 0)
    occupied = centres[:, 35:36]
    group = iota((8, 128), 1) // 8
    group_long = iota((64, 128), 1) // 8
    rows = [ref[at + 64 : at + 72] for ref, at in bases]
    columns = jnp.concatenate(rows + [jnp.zeros((64, 128), F32)], 0).T[0:64]
    copies = []
    for block in range(8):
        wide = jnp.where(group_long == block, columns, 0.0)
        for shift in (8, 16, 32, 64):
            wide = wide + pltpu.roll(wide, shift, 1)
        copies.append(wide)
    tiles = []
    for dx, dy, dz in steps:
        tile = jnp.zeros((8, 128), F32)
        for unit, (x, y, z) in enumerate(units):
            tx, ty, tz = x - 1 + dx, y - 1 + dy, z - 1 + dz
            row = local_row(tx, ty, tz)
            tile = jnp.where(group == unit, copies[block_of(tx, ty, tz)][row : row + 8], tile)
        tiles.append(tile)
    spots = jnp.concatenate(tiles + [jnp.zeros((40, 128), F32)], 0).T
    stencil = iota((1, 256), 1) // 8
    crossing = (stencil // 9 - 1, stencil // 3 % 3 - 1, stencil % 3 - 1)
    delta = []
    for a in range(3):
        spread = jnp.concatenate(
            [
                jnp.broadcast_to(spots[8 * unit + a : 8 * unit + a + 1], (8, 256))
                for unit in range(8)
            ],
            0,
        )
        delta.append(crossing[a].astype(F32) + spread - centres[:, 32 + a : 33 + a])
    dist_sq = delta[0] * delta[0] + delta[1] * delta[1] + delta[2] * delta[2]
    near = 1.0 - dist_sq * (1.0 / 16.0)
    envelope = near * near
    lane_f = iota((64, 256), 1).astype(F32)
    times = jnp.zeros((64, 256), F32)
    for entry in range(32):
        times = times + jnp.where(centres[:, entry : entry + 1] == lane_f, 1.0, 0.0)
    bases_m = []
    power = None
    for b in range(8):
        if b % 4 == 0:
            power = jnp.exp(dist_sq * (-(2.0 ** (b - 4))))
        else:
            power = power * power
        bases_m.append(power * times)
    norm = 1.0 / math.sqrt(32.0)
    windows = []
    sums = [[], [], [], []]
    for unit, (x, y, z) in enumerate(units):
        window = jnp.concatenate(
            [cell_tile(x - 1 + dx, y - 1 + dy, z - 1 + dz) for dx, dy, dz in steps]
            + [jnp.zeros((40, 128), F32)],
            0,
        )
        high, low = split(window)
        windows.append((high, low))
        at = slice(8 * unit, 8 * unit + 8)
        left = []
        for b in range(8):
            weight = bases_m[b][at] * envelope[at]
            left += [weight] + [weight * delta[a][at] for a in range(3)]
        left_high, left_low = split(jnp.concatenate(left, 0))
        made = contract(
            jnp.concatenate([left_high, left_low], 0),
            jnp.concatenate([high, low], 1),
            (((1,), (0,))),
        )
        made = made[0:256, 0:128] + made[0:256, 128:256] + made[256:512, 0:128]
        for part in range(4):
            weights = radial_ref if part == 0 else vector_ref
            total = made[8 * part : 8 * part + 8] * weights[0:1]
            for b in range(1, 8):
                row = 8 * (4 * b + part)
                total = total + made[row : row + 8] * weights[b : b + 1]
            sums[part].append(total)
    sums = [jnp.concatenate(part, 0) * norm for part in sums]
    product = sums[0] + sums[1] * sums[1] + sums[2] * sums[2] + sums[3] * sums[3]
    mixed = contract(split_left(product), split_right(mix_ref[...], 0), (((1,), (0,))))
    gate = 1.0 / (1.0 + jnp.exp(-mixed))
    out_weight = extra_ref[0:1]
    energy = jnp.sum((own + mixed * gate) * out_weight, 1, keepdims=True) * occupied
    slope = gate * (1.0 + mixed * (1.0 - gate)) * (out_weight * occupied)
    grad = contract(split_left(slope), split_right(mix_ref[...], 1), (((1,), (1,)))) * norm
    grads = [grad] + [2.0 * grad * sums[1 + a] for a in range(3)]
    sub = iota((8, 256), 0)
    column = iota((8, 128), 1)
    pushes, ends = [], {}
    for unit, spot in enumerate(units):
        at = slice(8 * unit, 8 * unit + 8)
        left = []
        for b in range(8):
            left.append(grads[0][at] * radial_ref[b : b + 1])
            left += [grads[1 + a][at] * vector_ref[b : b + 1] for a in range(3)]
        high, low = windows[unit]
        pulled = contract(
            split_left(jnp.concatenate(left, 0)),
            jnp.concatenate([high, high, low], 1),
            (((1,), (1,))),
        )
        linear = [jnp.zeros((8, 256), F32) for _ in range(3)]
        plain = jnp.zeros((8, 256), F32)
        decayed = jnp.zeros((8, 256), F32)
        here = [delta[a][at] for a in range(3)]
        for b in range(8):
            parts = [pulled[32 * b + 8 * part : 32 * b + 8 * part + 8] for part in range(4)]
            full = parts[0] + parts[1] * here[0] + parts[2] * here[1] + parts[3] * here[2]
            basis = bases_m[b][at]
            weighted = basis * full
            plain = plain + weighted
            decayed = decayed + weighted * (2.0 ** (b - 4))
            for a in range(3):
                linear[a] = linear[a] + basis * parts[1 + a]
        radial_slope = 2.0 * (near[at] * (-0.125) * plain - envelope[at] * decayed)
        gathered = jnp.zeros((8, 256), F32)
        end = jnp.where(column == 0, energy[at], 0.0)
        for a in range(3):
            push = envelope[at] * linear[a] + here[a] * radial_slope
            gathered = jnp.where(sub == 1 + a, jnp.sum(push, 0, keepdims=True), gathered)
            end = jnp.where(column == 1 + a, -jnp.sum(push, 1, keepdims=True), end)
        pushes.append(gathered)
        ends[spot] = end
    pushes = jnp.concatenate(pushes + [jnp.zeros((64, 256), F32)], 0).T
    folded = []
    for block in range(8):
        for local in range(8):
            x = block % 2 * 2 + local // 4
            y = block // 2 % 2 * 2 + local // 2 % 2
            z = block // 4 * 2 + local % 2
            total = ends.get((x, y, z), jnp.zeros((8, 128), F32))
            for unit, (ux, uy, uz) in enumerate(units):
                step = (x - ux + 1, y - uy + 1, z - uz + 1)
                if step in steps:
                    row = 8 * steps.index(step)
                    total = total + jnp.where(group == unit, pushes[row : row + 8], 0.0)
            folded.append(total)
    folded = jnp.concatenate(folded, 0).T
    rows = folded[0:8]
    for unit in range(1, 8):
        rows = rows + folded[8 * unit : 8 * unit + 8]
    rows = rows[0:4]
    kinds = [species_ref[x, y] for x in range(2) for y in range(2)]
    spread = (iota((8, 128), 1) % 8 == iota((8, 128), 0)).astype(F32)
    kinds = contract(jnp.concatenate(kinds, 0).astype(F32), spread, (((1,), (0,))))
    shift = jnp.zeros((8, 128), F32)
    for name in range(8):
        shift = jnp.where(kinds == float(name), extra_ref[1:2, name : name + 1], shift)
    mine = iota((8, 128), 1) // 8 == iota((8, 128), 0)
    shift = jnp.sum(jnp.where(mine, shift, 0.0), 0, keepdims=True) * own_ref[67:68]
    shift = jnp.where(iota((4, 128), 0) == 0, shift, 0.0)
    low = iota((4, 128), 1) < 64
    for half in range(2):
        first, second = (rows[:, 128 * k : 128 * k + 128] for k in (2 * half, 2 * half + 1))
        first = first + shift if half == 0 else first
        kept_ref[4 * half : 4 * half + 4] = jnp.where(low, first, swap_halves(second))
        sent_ref[4 * half : 4 * half + 4] = jnp.where(low, swap_halves(first), second)


def last_kernel(parts_ref, energy_ref, force_ref):
    total = parts_ref[0:8]
    for at in range(8, 64, 8):
        total = total + parts_ref[at : at + 8]
    total = total + pltpu.roll(total, 4, 0)
    total = total + pltpu.roll(total, 2, 0)
    turned = swap_halves(total)
    total = jnp.concatenate([total[0:1], turned[0:1], total[1:2], turned[1:2]], 0)
    for cell in range(8):
        x, y, z = cell // 4, cell // 2 % 2, cell % 2
        here = total if cell == 0 else pltpu.roll(total, 128 - 8 * cell, 1)
        energy_ref[x, y, z : z + 1] = here[0:1, 0:8]
        for d in range(3):
            force_ref[x, y, d, z : z + 1] = -here[1 + d : 2 + d, 0:8]


def call(kernel, out, *operands, micros=10, room=48):
    cost = pl.CostEstimate(flops=micros * 10**8, bytes_accessed=micros * 3 * 10**5, transcendentals=0)
    return pl.pallas_call(
        kernel,
        out_shape=[jax.ShapeDtypeStruct(shape, F32) for shape in out],
        compiler_params=pltpu.CompilerParams(vmem_limit_bytes=room * 1024 * 1024),
        cost_estimate=cost,
    )(*operands)


def moved(value, axes, *steps):
    counts = [lax.axis_size(axis) for axis in axes]
    pairs = []
    for source in range(math.prod(counts)):
        rest, target, stride = source, 0, 1
        for count, step in zip(counts[::-1], steps[::-1]):
            target += (rest + step) % count * stride
            rest, stride = rest // count, stride * count
        pairs.append((source, target))
    return lax.ppermute(value, axes, pairs)


def body(
    features, offsets, counts, species, neighbours,
    w_radial, w_vector, w_mix, w_out, w_charge, species_shift,
):
    cells_x, cells_y, cells_z, slots_cell, channels = features.shape
    grid = (
        cells_x * lax.axis_size("gx"),
        cells_y * lax.axis_size("gy"),
        cells_z * lax.axis_size("gz"),
    )
    scale = 1.0 / math.sqrt(grid[0] * grid[1] * grid[2] * slots_cell * MODES)
    held = (
        features.reshape(64, 128),
        jnp.transpose(offsets, (0, 1, 3, 2, 4)),
        counts,
        neighbours.reshape(64, 32),
        w_charge.T,
        w_out.reshape(1, 128),
        species_shift.reshape(1, 8),
    )
    slab, rest, extra, message = pl.pallas_call(
        pack_kernel,
        out_shape=[
            jax.ShapeDtypeStruct(shape, F32)
            for shape in [(104, 128), (32, 128), (8, 128), (32, 5, 2, 128)]
        ],
        in_specs=[pl.BlockSpec(memory_space=pl.ANY)] * len(held),
        scratch_shapes=[pltpu.VMEM(value.shape, value.dtype) for value in held]
        + [pltpu.SemaphoreType.DMA((len(held),))],
        compiler_params=pltpu.CompilerParams(vmem_limit_bytes=PACK_ROOM * 1024 * 1024),
    )(*held)
    in_x = moved(slab, ("gx",), -1)
    atoms = lax.all_to_all(message, ("gy", "gz"), 0, 0).reshape(320, 128)
    (to_z,) = call(stack_z_kernel, [(176, 128)], slab, rest, in_x, micros=STACK_Z_MICROS)
    in_z = moved(to_z, ("gz",), -1)
    (to_y,) = call(
        stack_y_kernel, [(320, 128)], slab, rest, in_x, in_z, micros=STACK_Y_MICROS
    )
    in_y = moved(to_y, ("gy",), -1)
    partial, phases, charges = call(
        functools.partial(waves_kernel, grid),
        [(16, 8, 128), (64, 2048), (16, 2048)],
        atoms,
        micros=WAVES_MICROS,
    )
    sums = lax.all_to_all(partial, "gx", 0, 0)
    kept, sent = call(
        short_kernel,
        [(8, 128), (8, 128)],
        slab, rest, in_x, in_z, in_y, extra,
        w_radial, w_vector, w_mix, species,
        micros=SHORT_MICROS,
    )
    came = moved(sent, ("gx",), 1)
    (parts,) = call(
        functools.partial(field_kernel, grid, scale),
        [(32, 2, 128)],
        sums, phases, charges, kept, came,
    )
    parts = lax.all_to_all(parts, ("gy", "gz"), 0, 0).reshape(64, 128)
    atom_energy, forces = call(last_kernel, [(2, 2, 2, 8), (2, 2, 3, 2, 8)], parts, room=LAST_ROOM)
    return (atom_energy, jnp.transpose(forces, (0, 1, 3, 2, 4)))


def solution(mesh):
    spread = P("gx", "gy", "gz")
    in_specs = (spread,) * 5 + (P(),) * 6
    return jax.shard_map(
        body, mesh=mesh, in_specs=in_specs, out_specs=(spread, spread), check_vma=False
    )
```

```python
import functools
import math

import jax
import jax.numpy as jnp
from jax import lax
from jax.experimental import pallas as pl
from jax.experimental.pallas import tpu as pltpu
from jax.sharding import PartitionSpec as P

KX = 16
KY = 8
KZ = 8
MODES = KX * KY * KZ
HIGH = lax.Precision.HIGHEST
F32 = jnp.float32
BF16 = jnp.bfloat16
STACK_Z_MICROS = 50
STACK_Y_MICROS = 1
WAVES_MICROS = 500
FIELD_MICROS = 50
SHORT_MICROS = 1
PACK_ROOM = 60
LAST_ROOM = 48


def iota(shape, dim):
    return lax.broadcasted_iota(jnp.int32, shape, dim)


def split(value):
    high = value.astype(BF16)
    low = (value - high.astype(F32)).astype(BF16)
    return high, low


def contract(left, right, dims, precision=None):
    return lax.dot_general(
        left, right, (dims, ((), ())), precision=precision, preferred_element_type=F32
    )


def split_left(value):
    high, low = split(value)
    return jnp.concatenate([high, low, high], 1)


def split_right(value, axis):
    high, low = split(value)
    return jnp.concatenate([high, high, low], axis)


def swap_halves(value):
    return pltpu.roll(value, 64, value.ndim - 1)


def position_rows(pos_ref, lane):
    pieces = [pos_ref[x, y, d] for x in range(2) for y in range(2) for d in range(3)]
    spread = (iota((8, 128), 1) % 8 == iota((8, 128), 0)).astype(F32)
    pieces = jnp.concatenate(pieces, 0)
    first, rest = split(pieces)
    last = (pieces - first.astype(F32) - rest.astype(F32)).astype(BF16)
    wide = contract(
        jnp.concatenate([first, rest, last], 1),
        jnp.concatenate([spread] * 3, 0).astype(BF16),
        (((1,), (0,))),
    )
    rows = []
    for d in range(3):
        row = jnp.zeros((1, 128), F32)
        for cell in range(8):
            at = (cell // 2) * 6 + d * 2 + cell % 2
            row = jnp.where(lane[0:1] // 8 == cell, wide[at : at + 1], row)
        rows.append(row)
    return jnp.concatenate(rows + [jnp.zeros((5, 128), F32)], 0)


def pack_kernel(
    feat_hbm, pos_hbm, count_hbm, near_hbm, charge_hbm, weight_hbm, shift_hbm,
    slab_ref, rest_ref, extra_ref, message_ref,
    feat_ref, pos_ref, count_ref, near_ref, charge_ref, weight_ref, shift_ref, arrived,
):
    copies = [
        pltpu.make_async_copy(source, target, arrived.at[at])
        for at, (source, target) in enumerate(
            (
                (feat_hbm, feat_ref), (pos_hbm, pos_ref), (count_hbm, count_ref),
                (near_hbm, near_ref), (charge_hbm, charge_ref), (weight_hbm, weight_ref),
                (shift_hbm, shift_ref),
            )
        )
    ]
    for copy in copies:
        copy.start()
    for copy in copies:
        copy.wait()
    extra_ref[...] = jnp.zeros((8, 128), F32)
    extra_ref[0:1] = weight_ref[...]
    extra_ref[1:2, 0:8] = shift_ref[...]
    row = iota((64, 128), 0)
    lane = iota((8, 128), 1)
    count_col = jnp.zeros((64, 128), jnp.int32)
    count_row = jnp.zeros((8, 128), jnp.int32)
    for cell in range(8):
        count = count_ref[cell // 4][cell // 2 % 2 : cell // 2 % 2 + 1, cell % 2 : cell % 2 + 1]
        count_col = jnp.where(row // 8 == cell, count, count_col)
        count_row = jnp.where(lane // 8 == cell, count, count_row)
    occupied = (row % 8 < count_col).astype(F32)
    occupied_row = (lane % 8 < count_row).astype(F32)
    masked = feat_ref[...] * occupied
    charges = contract(
        split_left(charge_ref[...]),
        split_right(jnp.concatenate([masked, masked], 0), 1),
        (((1,), (1,))),
    )
    sub = iota((8, 128), 0)
    tile = position_rows(pos_ref, lane)
    tile = jnp.where(sub == 3, occupied_row, tile)
    cell_x, cell_y, cell_z = lane // 32 % 2, lane // 16 % 2, lane // 8 % 2
    corner_x = 2 * lax.axis_index("gx")
    corner_y = 2 * lax.axis_index("gy")
    corner_z = 2 * lax.axis_index("gz")
    corner = jnp.where(
        sub == 0, cell_x + corner_x, jnp.where(sub == 1, cell_y + corner_y, cell_z + corner_z)
    )
    places = tile + corner.astype(F32)
    lane_low = lane < 64
    charges = jnp.where(lane_low, charges[0:8], charges[8:16])
    places = jnp.where(lane_low, places, swap_halves(pltpu.roll(places, 7, 0)))
    places = jnp.concatenate([places[0:1], places[2:3]], 0)
    pieces = [charges[2 * k : 2 * k + 2] for k in range(4)] + [places]
    for member in range(message_ref.shape[0]):
        for k in range(5):
            message_ref[member, k] = pieces[k]
    turned = jnp.concatenate(
        [jnp.zeros((32, 128), F32), tile, jnp.zeros((88, 128), F32)], 0
    ).T
    near = near_ref[...].astype(F32)
    slab_ref[0:64] = masked
    slab_ref[64:72] = tile
    slab_ref[72:104] = turned[0:32]
    slab_ref[72:104, 0:32] = near[0:32]
    rest_ref[...] = turned[32:64]
    rest_ref[:, 0:32] = near[32:64]


def stack_z_kernel(own_ref, rest_ref, in_x_ref, out_ref):
    out_ref[0:72] = own_ref[0:72]
    out_ref[72:144] = in_x_ref[0:72]
    out_ref[144:152] = rest_ref[0:8]
    out_ref[152:160] = rest_ref[16:24]
    out_ref[160:168] = in_x_ref[72:80]
    out_ref[168:176] = in_x_ref[88:96]


def stack_y_kernel(own_ref, rest_ref, in_x_ref, in_z_ref, out_ref):
    out_ref[0:72] = own_ref[0:72]
    out_ref[72:144] = in_x_ref[0:72]
    out_ref[144:288] = in_z_ref[0:144]
    out_ref[288:296] = rest_ref[8:16]
    out_ref[296:304] = in_x_ref[80:88]
    out_ref[304:312] = in_z_ref[144:152]
    out_ref[312:320] = in_z_ref[160:168]


def wave_numbers(member, shape, dim):
    index = iota(shape, dim) % 32
    number_y = (index // 8 + (member % 2) * 4 - KY // 2).astype(F32)
    number_z = (index % 8 - KZ // 2).astype(F32)
    number_x = (member // 2 - KX // 2).astype(F32)
    return number_x, number_y, number_z


def sine_cosine(turns):
    part = turns - jnp.floor(turns + 0.5)
    angle = part * (2.0 * math.pi)
    square = angle * angle
    sine = jnp.full_like(square, 1.0 / math.factorial(19) * -1.0)
    for power in range(17, 0, -2):
        sign = 1.0 if power // 2 % 2 == 0 else -1.0
        sine = sine * square + sign / math.factorial(power)
    cosine = jnp.full_like(square, -1.0 / math.factorial(18))
    for power in range(16, -1, -2):
        sign = 1.0 if power // 2 % 2 == 0 else -1.0
        cosine = cosine * square + sign / math.factorial(power)
    return sine * angle, cosine


def waves_kernel(grid, atoms_ref, message_ref, phase_ref, charge_ref):
    member = lax.axis_index("gy") * 4 + lax.axis_index("gz")
    low = iota((8, 128), 1) < 64
    upper, lower, places = [], [], []
    for pair in range(16):
        first, second = atoms_ref[20 * pair : 20 * pair + 8], atoms_ref[20 * pair + 10 : 20 * pair + 18]
        upper.append(jnp.where(low, first, swap_halves(second)))
        lower.append(jnp.where(low, swap_halves(first), second))
        first, second = (
            atoms_ref[20 * pair + 8 : 20 * pair + 10],
            atoms_ref[20 * pair + 18 : 20 * pair + 20],
        )
        places.append(
            jnp.concatenate(
                [
                    jnp.where(low[0:2], first, swap_halves(second)),
                    jnp.where(low[0:2], swap_halves(first), second),
                ],
                0,
            )
        )
    charges = jnp.concatenate(
        [jnp.concatenate(upper, 1), jnp.concatenate(lower, 1)], 0
    )
    places = jnp.concatenate(places, 1)
    number_x, number_y, number_z = wave_numbers(member, (32, 1), 0)
    turns = (
        number_x * (places[0:1] * (1.0 / grid[0]))
        + number_y * (places[2:3] * (1.0 / grid[1]))
        + number_z * (places[1:2] * (1.0 / grid[2]))
    )
    sine, cosine = sine_cosine(turns)
    phases = jnp.concatenate([cosine, sine], 0)
    phase_ref[...] = phases
    charge_ref[...] = charges
    charge_stack = jnp.concatenate(split(charges), 0)
    phase_stack = jnp.concatenate(split(phases), 0)
    sums = contract(charge_stack, phase_stack, (((1,), (1,))))
    partial = sums[0:16] + sums[16:32]
    partial = partial + swap_halves(partial)
    partial = jnp.where(low, partial[0:8], partial[8:16])
    for other in range(message_ref.shape[0]):
        message_ref[other] = partial


def field_kernel(grid, scale, sums_ref, phase_ref, charge_ref, out_ref):
    at_y, at_z = lax.axis_index("gy"), lax.axis_index("gz")
    member = at_y * 4 + at_z
    total = sums_ref[0]
    for other in range(1, sums_ref.shape[0]):
        total = total + sums_ref[other]
    turned = swap_halves(total)
    low_lane = iota((8, 128), 1) < 64
    total = jnp.concatenate(
        [
            jnp.where(low_lane, total[0:8], turned[0:8]),
            jnp.where(low_lane, turned[0:8], total[0:8]),
        ],
        0,
    )
    two_pi = 2.0 * math.pi
    number_x, number_y, number_z = wave_numbers(member, (16, 128), 1)
    wave_x, wave_y, wave_z = (
        number_x * (two_pi / grid[0]),
        number_y * (two_pi / grid[1]),
        number_z * (two_pi / grid[2]),
    )
    length_sq = wave_x * wave_x + wave_y * wave_y + wave_z * wave_z
    total = total * (jnp.exp(-0.5 * length_sq) / (length_sq + 1.0))
    high = total.astype(BF16).astype(F32)
    low = total - high
    left = jnp.concatenate([high, low, high, jnp.zeros((80, 128), F32)], 0).T[0:64, 0:64]
    charge_high, charge_low = split(charge_ref[...])
    right = jnp.concatenate(
        [charge_high, charge_high, charge_low, jnp.zeros_like(charge_low)], 0
    )
    fields = contract(left.astype(BF16), right, (((1,), (0,))))
    cosine, sine = phase_ref[0:32], phase_ref[32:64]
    field_cos, field_sin = fields[0:32], fields[32:64]
    energy = (0.5 * scale) * jnp.sum(cosine * field_cos + sine * field_sin, 0, keepdims=True)
    turning = scale * (cosine * field_sin - sine * field_cos)
    number_x, number_y, number_z = wave_numbers(member, (32, 1), 0)
    pull_x = (number_x * (two_pi / grid[0])) * jnp.sum(turning, 0, keepdims=True)
    pull_y = jnp.sum(turning * (number_y * (two_pi / grid[1])), 0, keepdims=True)
    pull_z = jnp.sum(turning * (number_z * (two_pi / grid[2])), 0, keepdims=True)
    first = jnp.concatenate([energy, pull_y], 0)
    second = jnp.concatenate([pull_x, pull_z], 0)
    low = iota((2, 128), 1) < 64
    for pair in range(16):
        lanes = slice(128 * pair, 128 * pair + 128)
        left_part, right_part = first[:, lanes], second[:, lanes]
        out_ref[2 * pair] = jnp.where(low, left_part, swap_halves(right_part))
        out_ref[2 * pair + 1] = jnp.where(low, swap_halves(left_part), right_part)


def fold_kernel(parts_ref, kept_ref, came_ref, out_ref):
    at_y, at_z = lax.axis_index("gy"), lax.axis_index("gz")
    folded = kept_ref[...] + came_ref[...]
    turned = swap_halves(folded)
    low = iota((2, 128), 1) < 64
    out_ref[...] = parts_ref[...]
    for block in range(4):
        by, bz = block % 2, block // 2
        to = ((at_y + by) % 8) * 4 + (at_z + bz) % 4
        here, there = (folded, turned) if by == 0 else (turned, folded)
        row = 4 * bz
        piece = jnp.where(
            low,
            jnp.concatenate([here[row : row + 1], here[row + 2 : row + 3]], 0),
            jnp.concatenate([there[row + 1 : row + 2], there[row + 3 : row + 4]], 0),
        )
        out_ref[to] = out_ref[to] + piece


def short_kernel(
    own_ref, rest_ref, in_x_ref, in_z_ref, in_y_ref, extra_ref,
    radial_ref, vector_ref, mix_ref, species_ref, kept_ref, sent_ref,
):
    bases = [
        (own_ref, 0), (in_x_ref, 0), (in_y_ref, 0), (in_y_ref, 72),
        (in_z_ref, 0), (in_z_ref, 72), (in_y_ref, 144), (in_y_ref, 216),
    ]

    def local_row(x, y, z):
        return (x % 2 * 4 + y % 2 * 2 + z % 2) * 8

    def block_of(x, y, z):
        return z // 2 * 4 + y // 2 * 2 + x // 2

    def cell_tile(x, y, z):
        ref, at = bases[block_of(x, y, z)]
        at = at + local_row(x, y, z)
        return ref[at : at + 8]

    units = [(x, y, z) for z in (1, 2) for y in (1, 2) for x in (1, 2)]
    steps = [(dx, dy, dz) for dx in range(3) for dy in range(3) for dz in range(3)]
    centres = [
        rest_ref[24:32], in_x_ref[96:104], in_y_ref[288:296], in_y_ref[296:304],
        in_z_ref[152:160], in_z_ref[168:176], in_y_ref[304:312], in_y_ref[312:320],
    ]
    centres = jnp.concatenate(centres, 0)
    own = jnp.concatenate([cell_tile(*unit) for unit in units], 0)
    occupied = centres[:, 35:36]
    group = iota((8, 128), 1) // 8
    group_long = iota((64, 128), 1) // 8
    rows = [ref[at + 64 : at + 72] for ref, at in bases]
    columns = jnp.concatenate(rows + [jnp.zeros((64, 128), F32)], 0).T[0:64]
    copies = []
    for block in range(8):
        wide = jnp.where(group_long == block, columns, 0.0)
        for shift in (8, 16, 32, 64):
            wide = wide + pltpu.roll(wide, shift, 1)
        copies.append(wide)
    tiles = []
    for dx, dy, dz in steps:
        tile = jnp.zeros((8, 128), F32)
        for unit, (x, y, z) in enumerate(units):
            tx, ty, tz = x - 1 + dx, y - 1 + dy, z - 1 + dz
            row = local_row(tx, ty, tz)
            tile = jnp.where(group == unit, copies[block_of(tx, ty, tz)][row : row + 8], tile)
        tiles.append(tile)
    spots = jnp.concatenate(tiles + [jnp.zeros((40, 128), F32)], 0).T
    stencil = iota((1, 256), 1) // 8
    crossing = (stencil // 9 - 1, stencil // 3 % 3 - 1, stencil % 3 - 1)
    delta = []
    for a in range(3):
        spread = jnp.concatenate(
            [
                jnp.broadcast_to(spots[8 * unit + a : 8 * unit + a + 1], (8, 256))
                for unit in range(8)
            ],
            0,
        )
        delta.append(crossing[a].astype(F32) + spread - centres[:, 32 + a : 33 + a])
    dist_sq = delta[0] * delta[0] + delta[1] * delta[1] + delta[2] * delta[2]
    near = 1.0 - dist_sq * (1.0 / 16.0)
    envelope = near * near
    lane_f = iota((64, 256), 1).astype(F32)
    times = jnp.zeros((64, 256), F32)
    for entry in range(32):
        times = times + jnp.where(centres[:, entry : entry + 1] == lane_f, 1.0, 0.0)
    bases_m = []
    power = None
    for b in range(8):
        if b % 4 == 0:
            power = jnp.exp(dist_sq * (-(2.0 ** (b - 4))))
        else:
            power = power * power
        bases_m.append(power * times)
    norm = 1.0 / math.sqrt(32.0)
    windows = []
    sums = [[], [], [], []]
    for unit, (x, y, z) in enumerate(units):
        window = jnp.concatenate(
            [cell_tile(x - 1 + dx, y - 1 + dy, z - 1 + dz) for dx, dy, dz in steps]
            + [jnp.zeros((40, 128), F32)],
            0,
        )
        high, low = split(window)
        windows.append((high, low))
        at = slice(8 * unit, 8 * unit + 8)
        left = []
        for b in range(8):
            weight = bases_m[b][at] * envelope[at]
            left += [weight] + [weight * delta[a][at] for a in range(3)]
        left_high, left_low = split(jnp.concatenate(left, 0))
        made = contract(
            jnp.concatenate([left_high, left_low], 0),
            jnp.concatenate([high, low], 1),
            (((1,), (0,))),
        )
        made = made[0:256, 0:128] + made[0:256, 128:256] + made[256:512, 0:128]
        for part in range(4):
            weights = radial_ref if part == 0 else vector_ref
            total = made[8 * part : 8 * part + 8] * weights[0:1]
            for b in range(1, 8):
                row = 8 * (4 * b + part)
                total = total + made[row : row + 8] * weights[b : b + 1]
            sums[part].append(total)
    sums = [jnp.concatenate(part, 0) * norm for part in sums]
    product = sums[0] + sums[1] * sums[1] + sums[2] * sums[2] + sums[3] * sums[3]
    mixed = contract(split_left(product), split_right(mix_ref[...], 0), (((1,), (0,))))
    gate = 1.0 / (1.0 + jnp.exp(-mixed))
    out_weight = extra_ref[0:1]
    energy = jnp.sum((own + mixed * gate) * out_weight, 1, keepdims=True) * occupied
    slope = gate * (1.0 + mixed * (1.0 - gate)) * (out_weight * occupied)
    grad = contract(split_left(slope), split_right(mix_ref[...], 1), (((1,), (1,)))) * norm
    grads = [grad] + [2.0 * grad * sums[1 + a] for a in range(3)]
    sub = iota((8, 256), 0)
    column = iota((8, 128), 1)
    pushes, ends = [], {}
    for unit, spot in enumerate(units):
        at = slice(8 * unit, 8 * unit + 8)
        left = []
        for b in range(8):
            left.append(grads[0][at] * radial_ref[b : b + 1])
            left += [grads[1 + a][at] * vector_ref[b : b + 1] for a in range(3)]
        high, low = windows[unit]
        pulled = contract(
            split_left(jnp.concatenate(left, 0)),
            jnp.concatenate([high, high, low], 1),
            (((1,), (1,))),
        )
        linear = [jnp.zeros((8, 256), F32) for _ in range(3)]
        plain = jnp.zeros((8, 256), F32)
        decayed = jnp.zeros((8, 256), F32)
        here = [delta[a][at] for a in range(3)]
        for b in range(8):
            parts = [pulled[32 * b + 8 * part : 32 * b + 8 * part + 8] for part in range(4)]
            full = parts[0] + parts[1] * here[0] + parts[2] * here[1] + parts[3] * here[2]
            basis = bases_m[b][at]
            weighted = basis * full
            plain = plain + weighted
            decayed = decayed + weighted * (2.0 ** (b - 4))
            for a in range(3):
                linear[a] = linear[a] + basis * parts[1 + a]
        radial_slope = 2.0 * (near[at] * (-0.125) * plain - envelope[at] * decayed)
        gathered = jnp.zeros((8, 256), F32)
        end = jnp.where(column == 0, energy[at], 0.0)
        for a in range(3):
            push = envelope[at] * linear[a] + here[a] * radial_slope
            gathered = jnp.where(sub == 1 + a, jnp.sum(push, 0, keepdims=True), gathered)
            end = jnp.where(column == 1 + a, -jnp.sum(push, 1, keepdims=True), end)
        pushes.append(gathered)
        ends[spot] = end
    pushes = jnp.concatenate(pushes + [jnp.zeros((64, 256), F32)], 0).T
    folded = []
    for block in range(8):
        for local in range(8):
            x = block % 2 * 2 + local // 4
            y = block // 2 % 2 * 2 + local // 2 % 2
            z = block // 4 * 2 + local % 2
            total = ends.get((x, y, z), jnp.zeros((8, 128), F32))
            for unit, (ux, uy, uz) in enumerate(units):
                step = (x - ux + 1, y - uy + 1, z - uz + 1)
                if step in steps:
                    row = 8 * steps.index(step)
                    total = total + jnp.where(group == unit, pushes[row : row + 8], 0.0)
            folded.append(total)
    folded = jnp.concatenate(folded, 0).T
    rows = folded[0:8]
    for unit in range(1, 8):
        rows = rows + folded[8 * unit : 8 * unit + 8]
    rows = rows[0:4]
    kinds = [species_ref[x, y] for x in range(2) for y in range(2)]
    spread = (iota((8, 128), 1) % 8 == iota((8, 128), 0)).astype(F32)
    kinds = contract(jnp.concatenate(kinds, 0).astype(F32), spread, (((1,), (0,))))
    shift = jnp.zeros((8, 128), F32)
    for name in range(8):
        shift = jnp.where(kinds == float(name), extra_ref[1:2, name : name + 1], shift)
    mine = iota((8, 128), 1) // 8 == iota((8, 128), 0)
    shift = jnp.sum(jnp.where(mine, shift, 0.0), 0, keepdims=True) * own_ref[67:68]
    shift = jnp.where(iota((4, 128), 0) == 0, shift, 0.0)
    low = iota((4, 128), 1) < 64
    for half in range(2):
        first, second = (rows[:, 128 * k : 128 * k + 128] for k in (2 * half, 2 * half + 1))
        first = first + shift if half == 0 else first
        kept_ref[4 * half : 4 * half + 4] = jnp.where(low, first, swap_halves(second))
        sent_ref[4 * half : 4 * half + 4] = jnp.where(low, swap_halves(first), second)


def last_kernel(parts_ref, energy_ref, force_ref):
    total = parts_ref[0:8]
    for at in range(8, 64, 8):
        total = total + parts_ref[at : at + 8]
    total = total + pltpu.roll(total, 4, 0)
    total = total + pltpu.roll(total, 2, 0)
    turned = swap_halves(total)
    total = jnp.concatenate([total[0:1], turned[0:1], total[1:2], turned[1:2]], 0)
    for cell in range(8):
        x, y, z = cell // 4, cell // 2 % 2, cell % 2
        here = total if cell == 0 else pltpu.roll(total, 128 - 8 * cell, 1)
        energy_ref[x, y, z : z + 1] = here[0:1, 0:8]
        for d in range(3):
            force_ref[x, y, d, z : z + 1] = -here[1 + d : 2 + d, 0:8]


def call(kernel, out, *operands, micros=10, room=48):
    cost = pl.CostEstimate(flops=micros * 10**8, bytes_accessed=micros * 3 * 10**5, transcendentals=0)
    return pl.pallas_call(
        kernel,
        out_shape=[jax.ShapeDtypeStruct(shape, F32) for shape in out],
        compiler_params=pltpu.CompilerParams(vmem_limit_bytes=room * 1024 * 1024),
        cost_estimate=cost,
    )(*operands)


def moved(value, axes, *steps):
    counts = [lax.axis_size(axis) for axis in axes]
    pairs = []
    for source in range(math.prod(counts)):
        rest, target, stride = source, 0, 1
        for count, step in zip(counts[::-1], steps[::-1]):
            target += (rest + step) % count * stride
            rest, stride = rest // count, stride * count
        pairs.append((source, target))
    return lax.ppermute(value, axes, pairs)


def body(
    features, offsets, counts, species, neighbours,
    w_radial, w_vector, w_mix, w_out, w_charge, species_shift,
):
    cells_x, cells_y, cells_z, slots_cell, channels = features.shape
    grid = (
        cells_x * lax.axis_size("gx"),
        cells_y * lax.axis_size("gy"),
        cells_z * lax.axis_size("gz"),
    )
    scale = 1.0 / math.sqrt(grid[0] * grid[1] * grid[2] * slots_cell * MODES)
    held = (
        features.reshape(64, 128),
        jnp.transpose(offsets, (0, 1, 3, 2, 4)),
        counts,
        neighbours.reshape(64, 32),
        w_charge.T,
        w_out.reshape(1, 128),
        species_shift.reshape(1, 8),
    )
    slab, rest, extra, message = pl.pallas_call(
        pack_kernel,
        out_shape=[
            jax.ShapeDtypeStruct(shape, F32)
            for shape in [(104, 128), (32, 128), (8, 128), (32, 5, 2, 128)]
        ],
        in_specs=[pl.BlockSpec(memory_space=pl.ANY)] * len(held),
        scratch_shapes=[pltpu.VMEM(value.shape, value.dtype) for value in held]
        + [pltpu.SemaphoreType.DMA((len(held),))],
        compiler_params=pltpu.CompilerParams(vmem_limit_bytes=PACK_ROOM * 1024 * 1024),
    )(*held)
    in_x = moved(slab, ("gx",), -1)
    atoms = lax.all_to_all(message, ("gy", "gz"), 0, 0).reshape(320, 128)
    (to_z,) = call(stack_z_kernel, [(176, 128)], slab, rest, in_x, micros=STACK_Z_MICROS)
    in_z = moved(to_z, ("gz",), -1)
    (to_y,) = call(
        stack_y_kernel, [(320, 128)], slab, rest, in_x, in_z, micros=STACK_Y_MICROS
    )
    in_y = moved(to_y, ("gy",), -1)
    partial, phases, charges = call(
        functools.partial(waves_kernel, grid),
        [(16, 8, 128), (64, 2048), (16, 2048)],
        atoms,
        micros=WAVES_MICROS,
    )
    sums = lax.all_to_all(partial, "gx", 0, 0)
    kept, sent = call(
        short_kernel,
        [(8, 128), (8, 128)],
        slab, rest, in_x, in_z, in_y, extra,
        w_radial, w_vector, w_mix, species,
        micros=SHORT_MICROS,
    )
    came = moved(sent, ("gx",), 1)
    (parts,) = call(
        functools.partial(field_kernel, grid, scale),
        [(32, 2, 128)],
        sums, phases, charges,
        micros=FIELD_MICROS,
    )
    (parts,) = call(fold_kernel, [(32, 2, 128)], parts, kept, came)
    parts = lax.all_to_all(parts, ("gy", "gz"), 0, 0).reshape(64, 128)
    atom_energy, forces = call(last_kernel, [(2, 2, 2, 8), (2, 2, 3, 2, 8)], parts, room=LAST_ROOM)
    return (atom_energy, jnp.transpose(forces, (0, 1, 3, 2, 4)))


def solution(mesh):
    spread = P("gx", "gy", "gz")
    in_specs = (spread,) * 5 + (P(),) * 6
    return jax.shard_map(
        body, mesh=mesh, in_specs=in_specs, out_specs=(spread, spread), check_vma=False
    )
```

```python
import functools
import math

import jax
import jax.numpy as jnp
from jax import lax
from jax.experimental import pallas as pl
from jax.experimental.pallas import tpu as pltpu
from jax.sharding import PartitionSpec as P

KX = 16
KY = 8
KZ = 8
MODES = KX * KY * KZ
HIGH = lax.Precision.HIGHEST
F32 = jnp.float32
BF16 = jnp.bfloat16
STACK_Z_MICROS = 50
STACK_Y_MICROS = 1
WAVES_MICROS = 500
FIELD_MICROS = 50
SHORT_MICROS = 1
PACK_ROOM = 60
LAST_ROOM = 48


def iota(shape, dim):
    return lax.broadcasted_iota(jnp.int32, shape, dim)


def split(value):
    high = value.astype(BF16)
    low = (value - high.astype(F32)).astype(BF16)
    return high, low


def contract(left, right, dims, precision=None):
    return lax.dot_general(
        left, right, (dims, ((), ())), precision=precision, preferred_element_type=F32
    )


def split_left(value):
    high, low = split(value)
    return jnp.concatenate([high, low, high], 1)


def split_right(value, axis):
    high, low = split(value)
    return jnp.concatenate([high, high, low], axis)


def swap_halves(value):
    return pltpu.roll(value, 64, value.ndim - 1)


def position_rows(pos_ref, lane):
    pieces = [pos_ref[x, y, d] for x in range(2) for y in range(2) for d in range(3)]
    spread = (iota((8, 128), 1) % 8 == iota((8, 128), 0)).astype(F32)
    pieces = jnp.concatenate(pieces, 0)
    first, rest = split(pieces)
    last = (pieces - first.astype(F32) - rest.astype(F32)).astype(BF16)
    wide = contract(
        jnp.concatenate([first, rest, last], 1),
        jnp.concatenate([spread] * 3, 0).astype(BF16),
        (((1,), (0,))),
    )
    rows = []
    for d in range(3):
        row = jnp.zeros((1, 128), F32)
        for cell in range(8):
            at = (cell // 2) * 6 + d * 2 + cell % 2
            row = jnp.where(lane[0:1] // 8 == cell, wide[at : at + 1], row)
        rows.append(row)
    return jnp.concatenate(rows + [jnp.zeros((5, 128), F32)], 0)


def pack_kernel(
    feat_hbm, pos_hbm, count_hbm, near_hbm, charge_hbm, weight_hbm, shift_hbm,
    slab_ref, rest_ref, extra_ref, message_ref,
    feat_ref, pos_ref, count_ref, near_ref, charge_ref, weight_ref, shift_ref, arrived,
):
    copies = [
        pltpu.make_async_copy(source, target, arrived.at[at])
        for at, (source, target) in enumerate(
            (
                (feat_hbm, feat_ref), (pos_hbm, pos_ref), (count_hbm, count_ref),
                (near_hbm, near_ref), (charge_hbm, charge_ref), (weight_hbm, weight_ref),
                (shift_hbm, shift_ref),
            )
        )
    ]
    for copy in copies:
        copy.start()
    for copy in copies:
        copy.wait()
    extra_ref[...] = jnp.zeros((8, 128), F32)
    extra_ref[0:1] = weight_ref[...]
    extra_ref[1:2, 0:8] = shift_ref[...]
    row = iota((64, 128), 0)
    lane = iota((8, 128), 1)
    count_col = jnp.zeros((64, 128), jnp.int32)
    count_row = jnp.zeros((8, 128), jnp.int32)
    for cell in range(8):
        count = count_ref[cell // 4][cell // 2 % 2 : cell // 2 % 2 + 1, cell % 2 : cell % 2 + 1]
        count_col = jnp.where(row // 8 == cell, count, count_col)
        count_row = jnp.where(lane // 8 == cell, count, count_row)
    occupied = (row % 8 < count_col).astype(F32)
    occupied_row = (lane % 8 < count_row).astype(F32)
    masked = feat_ref[...] * occupied
    charges = contract(
        split_left(charge_ref[...]),
        split_right(jnp.concatenate([masked, masked], 0), 1),
        (((1,), (1,))),
    )
    sub = iota((8, 128), 0)
    tile = position_rows(pos_ref, lane)
    tile = jnp.where(sub == 3, occupied_row, tile)
    cell_x, cell_y, cell_z = lane // 32 % 2, lane // 16 % 2, lane // 8 % 2
    corner_x = 2 * lax.axis_index("gx")
    corner_y = 2 * lax.axis_index("gy")
    corner_z = 2 * lax.axis_index("gz")
    corner = jnp.where(
        sub == 0, cell_x + corner_x, jnp.where(sub == 1, cell_y + corner_y, cell_z + corner_z)
    )
    places = tile + corner.astype(F32)
    lane_low = lane < 64
    charges = jnp.where(lane_low, charges[0:8], charges[8:16])
    places = jnp.where(lane_low, places, swap_halves(pltpu.roll(places, 7, 0)))
    places = jnp.concatenate([places[0:1], places[2:3]], 0)
    pieces = [charges[2 * k : 2 * k + 2] for k in range(4)] + [places]
    for member in range(message_ref.shape[0]):
        for k in range(5):
            message_ref[member, k] = pieces[k]
    turned = jnp.concatenate(
        [jnp.zeros((32, 128), F32), tile, jnp.zeros((88, 128), F32)], 0
    ).T
    near = near_ref[...].astype(F32)
    slab_ref[0:64] = masked
    slab_ref[64:72] = tile
    slab_ref[72:104] = turned[0:32]
    slab_ref[72:104, 0:32] = near[0:32]
    rest_ref[...] = turned[32:64]
    rest_ref[:, 0:32] = near[32:64]


def stack_z_kernel(own_ref, rest_ref, in_x_ref, out_ref):
    out_ref[0:72] = own_ref[0:72]
    out_ref[72:144] = in_x_ref[0:72]
    out_ref[144:152] = rest_ref[0:8]
    out_ref[152:160] = rest_ref[16:24]
    out_ref[160:168] = in_x_ref[72:80]
    out_ref[168:176] = in_x_ref[88:96]


def stack_y_kernel(own_ref, rest_ref, in_x_ref, in_z_ref, out_ref):
    out_ref[0:72] = own_ref[0:72]
    out_ref[72:144] = in_x_ref[0:72]
    out_ref[144:288] = in_z_ref[0:144]
    out_ref[288:296] = rest_ref[8:16]
    out_ref[296:304] = in_x_ref[80:88]
    out_ref[304:312] = in_z_ref[144:152]
    out_ref[312:320] = in_z_ref[160:168]


def wave_numbers(member, shape, dim):
    index = iota(shape, dim) % 32
    number_y = (index // 8 + (member % 2) * 4 - KY // 2).astype(F32)
    number_z = (index % 8 - KZ // 2).astype(F32)
    number_x = (member // 2 - KX // 2).astype(F32)
    return number_x, number_y, number_z


def sine_cosine(turns):
    part = turns - jnp.floor(turns + 0.5)
    angle = part * (2.0 * math.pi)
    square = angle * angle
    sine = jnp.full_like(square, 1.0 / math.factorial(19) * -1.0)
    for power in range(17, 0, -2):
        sign = 1.0 if power // 2 % 2 == 0 else -1.0
        sine = sine * square + sign / math.factorial(power)
    cosine = jnp.full_like(square, -1.0 / math.factorial(18))
    for power in range(16, -1, -2):
        sign = 1.0 if power // 2 % 2 == 0 else -1.0
        cosine = cosine * square + sign / math.factorial(power)
    return sine * angle, cosine


def waves_kernel(grid, atoms_ref, message_ref, phase_ref, charge_ref):
    member = lax.axis_index("gy") * 4 + lax.axis_index("gz")
    low = iota((8, 128), 1) < 64
    upper, lower, places = [], [], []
    for pair in range(16):
        first, second = atoms_ref[20 * pair : 20 * pair + 8], atoms_ref[20 * pair + 10 : 20 * pair + 18]
        upper.append(jnp.where(low, first, swap_halves(second)))
        lower.append(jnp.where(low, swap_halves(first), second))
        first, second = (
            atoms_ref[20 * pair + 8 : 20 * pair + 10],
            atoms_ref[20 * pair + 18 : 20 * pair + 20],
        )
        places.append(
            jnp.concatenate(
                [
                    jnp.where(low[0:2], first, swap_halves(second)),
                    jnp.where(low[0:2], swap_halves(first), second),
                ],
                0,
            )
        )
    charges = jnp.concatenate(
        [jnp.concatenate(upper, 1), jnp.concatenate(lower, 1)], 0
    )
    places = jnp.concatenate(places, 1)
    row = iota((16, 1), 0)
    along_z = jnp.where(row < 8, (row - KZ // 2).astype(F32), 0.0)
    along_y = (row - 8 + (member % 2) * 4 - KY // 2).astype(F32)
    along_y = jnp.where((row >= 8) & (row < 12), along_y, 0.0)
    along_x = jnp.where(row == 12, (member // 2 - KX // 2).astype(F32), 0.0)
    turns = (
        along_x * (places[0:1] * (1.0 / grid[0]))
        + along_y * (places[2:3] * (1.0 / grid[1]))
        + along_z * (places[1:2] * (1.0 / grid[2]))
    )
    sine, cosine = sine_cosine(turns)
    sine_z, cosine_z = sine[0:8], cosine[0:8]
    sine_x, cosine_x = sine[12:13], cosine[12:13]
    flat_sine = sine_x * cosine[8:12] + cosine_x * sine[8:12]
    flat_cosine = cosine_x * cosine[8:12] - sine_x * sine[8:12]
    sines, cosines = [], []
    for k in range(4):
        sine_xy, cosine_xy = flat_sine[k : k + 1], flat_cosine[k : k + 1]
        sines.append(sine_xy * cosine_z + cosine_xy * sine_z)
        cosines.append(cosine_xy * cosine_z - sine_xy * sine_z)
    sine, cosine = jnp.concatenate(sines, 0), jnp.concatenate(cosines, 0)
    phases = jnp.concatenate([cosine, sine], 0)
    phase_ref[...] = phases
    charge_ref[...] = charges
    charge_stack = jnp.concatenate(split(charges), 0)
    phase_stack = jnp.concatenate(split(phases), 0)
    sums = contract(charge_stack, phase_stack, (((1,), (1,))))
    partial = sums[0:16] + sums[16:32]
    partial = partial + swap_halves(partial)
    partial = jnp.where(low, partial[0:8], partial[8:16])
    for other in range(message_ref.shape[0]):
        message_ref[other] = partial


def field_kernel(grid, scale, sums_ref, phase_ref, charge_ref, out_ref):
    at_y, at_z = lax.axis_index("gy"), lax.axis_index("gz")
    member = at_y * 4 + at_z
    total = sums_ref[0]
    for other in range(1, sums_ref.shape[0]):
        total = total + sums_ref[other]
    turned = swap_halves(total)
    low_lane = iota((8, 128), 1) < 64
    total = jnp.concatenate(
        [
            jnp.where(low_lane, total[0:8], turned[0:8]),
            jnp.where(low_lane, turned[0:8], total[0:8]),
        ],
        0,
    )
    two_pi = 2.0 * math.pi
    number_x, number_y, number_z = wave_numbers(member, (16, 128), 1)
    wave_x, wave_y, wave_z = (
        number_x * (two_pi / grid[0]),
        number_y * (two_pi / grid[1]),
        number_z * (two_pi / grid[2]),
    )
    length_sq = wave_x * wave_x + wave_y * wave_y + wave_z * wave_z
    total = total * (jnp.exp(-0.5 * length_sq) / (length_sq + 1.0))
    high = total.astype(BF16).astype(F32)
    low = total - high
    left = jnp.concatenate([high, low, high, jnp.zeros((80, 128), F32)], 0).T[0:64, 0:64]
    charge_high, charge_low = split(charge_ref[...])
    right = jnp.concatenate(
        [charge_high, charge_high, charge_low, jnp.zeros_like(charge_low)], 0
    )
    fields = contract(left.astype(BF16), right, (((1,), (0,))))
    cosine, sine = phase_ref[0:32], phase_ref[32:64]
    field_cos, field_sin = fields[0:32], fields[32:64]
    energy = (0.5 * scale) * jnp.sum(cosine * field_cos + sine * field_sin, 0, keepdims=True)
    turning = scale * (cosine * field_sin - sine * field_cos)
    number_x, number_y, number_z = wave_numbers(member, (32, 1), 0)
    pull_x = (number_x * (two_pi / grid[0])) * jnp.sum(turning, 0, keepdims=True)
    pull_y = jnp.sum(turning * (number_y * (two_pi / grid[1])), 0, keepdims=True)
    pull_z = jnp.sum(turning * (number_z * (two_pi / grid[2])), 0, keepdims=True)
    first = jnp.concatenate([energy, pull_y], 0)
    second = jnp.concatenate([pull_x, pull_z], 0)
    low = iota((2, 128), 1) < 64
    for pair in range(16):
        lanes = slice(128 * pair, 128 * pair + 128)
        left_part, right_part = first[:, lanes], second[:, lanes]
        out_ref[2 * pair] = jnp.where(low, left_part, swap_halves(right_part))
        out_ref[2 * pair + 1] = jnp.where(low, swap_halves(left_part), right_part)


def fold_kernel(parts_ref, kept_ref, came_ref, out_ref):
    at_y, at_z = lax.axis_index("gy"), lax.axis_index("gz")
    folded = kept_ref[...] + came_ref[...]
    turned = swap_halves(folded)
    low = iota((2, 128), 1) < 64
    out_ref[...] = parts_ref[...]
    for block in range(4):
        by, bz = block % 2, block // 2
        to = ((at_y + by) % 8) * 4 + (at_z + bz) % 4
        here, there = (folded, turned) if by == 0 else (turned, folded)
        row = 4 * bz
        piece = jnp.where(
            low,
            jnp.concatenate([here[row : row + 1], here[row + 2 : row + 3]], 0),
            jnp.concatenate([there[row + 1 : row + 2], there[row + 3 : row + 4]], 0),
        )
        out_ref[to] = out_ref[to] + piece


def short_kernel(
    own_ref, rest_ref, in_x_ref, in_z_ref, in_y_ref, extra_ref,
    radial_ref, vector_ref, mix_ref, species_ref, kept_ref, sent_ref,
):
    bases = [
        (own_ref, 0), (in_x_ref, 0), (in_y_ref, 0), (in_y_ref, 72),
        (in_z_ref, 0), (in_z_ref, 72), (in_y_ref, 144), (in_y_ref, 216),
    ]

    def local_row(x, y, z):
        return (x % 2 * 4 + y % 2 * 2 + z % 2) * 8

    def block_of(x, y, z):
        return z // 2 * 4 + y // 2 * 2 + x // 2

    def cell_tile(x, y, z):
        ref, at = bases[block_of(x, y, z)]
        at = at + local_row(x, y, z)
        return ref[at : at + 8]

    units = [(x, y, z) for z in (1, 2) for y in (1, 2) for x in (1, 2)]
    steps = [(dx, dy, dz) for dx in range(3) for dy in range(3) for dz in range(3)]
    centres = [
        rest_ref[24:32], in_x_ref[96:104], in_y_ref[288:296], in_y_ref[296:304],
        in_z_ref[152:160], in_z_ref[168:176], in_y_ref[304:312], in_y_ref[312:320],
    ]
    centres = jnp.concatenate(centres, 0)
    own = jnp.concatenate([cell_tile(*unit) for unit in units], 0)
    occupied = centres[:, 35:36]
    group = iota((8, 128), 1) // 8
    group_long = iota((64, 128), 1) // 8
    rows = [ref[at + 64 : at + 72] for ref, at in bases]
    columns = jnp.concatenate(rows + [jnp.zeros((64, 128), F32)], 0).T[0:64]
    copies = []
    for block in range(8):
        wide = jnp.where(group_long == block, columns, 0.0)
        for shift in (8, 16, 32, 64):
            wide = wide + pltpu.roll(wide, shift, 1)
        copies.append(wide)
    tiles = []
    for dx, dy, dz in steps:
        tile = jnp.zeros((8, 128), F32)
        for unit, (x, y, z) in enumerate(units):
            tx, ty, tz = x - 1 + dx, y - 1 + dy, z - 1 + dz
            row = local_row(tx, ty, tz)
            tile = jnp.where(group == unit, copies[block_of(tx, ty, tz)][row : row + 8], tile)
        tiles.append(tile)
    spots = jnp.concatenate(tiles + [jnp.zeros((40, 128), F32)], 0).T
    stencil = iota((1, 256), 1) // 8
    crossing = (stencil // 9 - 1, stencil // 3 % 3 - 1, stencil % 3 - 1)
    delta = []
    for a in range(3):
        spread = jnp.concatenate(
            [
                jnp.broadcast_to(spots[8 * unit + a : 8 * unit + a + 1], (8, 256))
                for unit in range(8)
            ],
            0,
        )
        delta.append(crossing[a].astype(F32) + spread - centres[:, 32 + a : 33 + a])
    dist_sq = delta[0] * delta[0] + delta[1] * delta[1] + delta[2] * delta[2]
    near = 1.0 - dist_sq * (1.0 / 16.0)
    envelope = near * near
    lane_f = iota((64, 256), 1).astype(F32)
    times = jnp.zeros((64, 256), F32)
    for entry in range(32):
        times = times + jnp.where(centres[:, entry : entry + 1] == lane_f, 1.0, 0.0)
    bases_m = []
    power = None
    for b in range(8):
        if b % 4 == 0:
            power = jnp.exp(dist_sq * (-(2.0 ** (b - 4))))
        else:
            power = power * power
        bases_m.append(power * times)
    norm = 1.0 / math.sqrt(32.0)
    windows = []
    sums = [[], [], [], []]
    for unit, (x, y, z) in enumerate(units):
        window = jnp.concatenate(
            [cell_tile(x - 1 + dx, y - 1 + dy, z - 1 + dz) for dx, dy, dz in steps]
            + [jnp.zeros((40, 128), F32)],
            0,
        )
        high, low = split(window)
        windows.append((high, low))
        at = slice(8 * unit, 8 * unit + 8)
        left = []
        for b in range(8):
            weight = bases_m[b][at] * envelope[at]
            left += [weight] + [weight * delta[a][at] for a in range(3)]
        left_high, left_low = split(jnp.concatenate(left, 0))
        made = contract(
            jnp.concatenate([left_high, left_low], 0),
            jnp.concatenate([high, low], 1),
            (((1,), (0,))),
        )
        made = made[0:256, 0:128] + made[0:256, 128:256] + made[256:512, 0:128]
        for part in range(4):
            weights = radial_ref if part == 0 else vector_ref
            total = made[8 * part : 8 * part + 8] * weights[0:1]
            for b in range(1, 8):
                row = 8 * (4 * b + part)
                total = total + made[row : row + 8] * weights[b : b + 1]
            sums[part].append(total)
    sums = [jnp.concatenate(part, 0) * norm for part in sums]
    product = sums[0] + sums[1] * sums[1] + sums[2] * sums[2] + sums[3] * sums[3]
    mixed = contract(split_left(product), split_right(mix_ref[...], 0), (((1,), (0,))))
    gate = 1.0 / (1.0 + jnp.exp(-mixed))
    out_weight = extra_ref[0:1]
    energy = jnp.sum((own + mixed * gate) * out_weight, 1, keepdims=True) * occupied
    slope = gate * (1.0 + mixed * (1.0 - gate)) * (out_weight * occupied)
    grad = contract(split_left(slope), split_right(mix_ref[...], 1), (((1,), (1,)))) * norm
    grads = [grad] + [2.0 * grad * sums[1 + a] for a in range(3)]
    sub = iota((8, 256), 0)
    column = iota((8, 128), 1)
    pushes, ends = [], {}
    for unit, spot in enumerate(units):
        at = slice(8 * unit, 8 * unit + 8)
        left = []
        for b in range(8):
            left.append(grads[0][at] * radial_ref[b : b + 1])
            left += [grads[1 + a][at] * vector_ref[b : b + 1] for a in range(3)]
        high, low = windows[unit]
        pulled = contract(
            split_left(jnp.concatenate(left, 0)),
            jnp.concatenate([high, high, low], 1),
            (((1,), (1,))),
        )
        linear = [jnp.zeros((8, 256), F32) for _ in range(3)]
        plain = jnp.zeros((8, 256), F32)
        decayed = jnp.zeros((8, 256), F32)
        here = [delta[a][at] for a in range(3)]
        for b in range(8):
            parts = [pulled[32 * b + 8 * part : 32 * b + 8 * part + 8] for part in range(4)]
            full = parts[0] + parts[1] * here[0] + parts[2] * here[1] + parts[3] * here[2]
            basis = bases_m[b][at]
            weighted = basis * full
            plain = plain + weighted
            decayed = decayed + weighted * (2.0 ** (b - 4))
            for a in range(3):
                linear[a] = linear[a] + basis * parts[1 + a]
        radial_slope = 2.0 * (near[at] * (-0.125) * plain - envelope[at] * decayed)
        gathered = jnp.zeros((8, 256), F32)
        end = jnp.where(column == 0, energy[at], 0.0)
        for a in range(3):
            push = envelope[at] * linear[a] + here[a] * radial_slope
            gathered = jnp.where(sub == 1 + a, jnp.sum(push, 0, keepdims=True), gathered)
            end = jnp.where(column == 1 + a, -jnp.sum(push, 1, keepdims=True), end)
        pushes.append(gathered)
        ends[spot] = end
    pushes = jnp.concatenate(pushes + [jnp.zeros((64, 256), F32)], 0).T
    folded = []
    for block in range(8):
        for local in range(8):
            x = block % 2 * 2 + local // 4
            y = block // 2 % 2 * 2 + local // 2 % 2
            z = block // 4 * 2 + local % 2
            total = ends.get((x, y, z), jnp.zeros((8, 128), F32))
            for unit, (ux, uy, uz) in enumerate(units):
                step = (x - ux + 1, y - uy + 1, z - uz + 1)
                if step in steps:
                    row = 8 * steps.index(step)
                    total = total + jnp.where(group == unit, pushes[row : row + 8], 0.0)
            folded.append(total)
    folded = jnp.concatenate(folded, 0).T
    rows = folded[0:8]
    for unit in range(1, 8):
        rows = rows + folded[8 * unit : 8 * unit + 8]
    rows = rows[0:4]
    kinds = [species_ref[x, y] for x in range(2) for y in range(2)]
    spread = (iota((8, 128), 1) % 8 == iota((8, 128), 0)).astype(F32)
    kinds = contract(jnp.concatenate(kinds, 0).astype(F32), spread, (((1,), (0,))))
    shift = jnp.zeros((8, 128), F32)
    for name in range(8):
        shift = jnp.where(kinds == float(name), extra_ref[1:2, name : name + 1], shift)
    mine = iota((8, 128), 1) // 8 == iota((8, 128), 0)
    shift = jnp.sum(jnp.where(mine, shift, 0.0), 0, keepdims=True) * own_ref[67:68]
    shift = jnp.where(iota((4, 128), 0) == 0, shift, 0.0)
    low = iota((4, 128), 1) < 64
    for half in range(2):
        first, second = (rows[:, 128 * k : 128 * k + 128] for k in (2 * half, 2 * half + 1))
        first = first + shift if half == 0 else first
        kept_ref[4 * half : 4 * half + 4] = jnp.where(low, first, swap_halves(second))
        sent_ref[4 * half : 4 * half + 4] = jnp.where(low, swap_halves(first), second)


def last_kernel(parts_ref, energy_ref, force_ref):
    total = parts_ref[0:8]
    for at in range(8, 64, 8):
        total = total + parts_ref[at : at + 8]
    total = total + pltpu.roll(total, 4, 0)
    total = total + pltpu.roll(total, 2, 0)
    turned = swap_halves(total)
    total = jnp.concatenate([total[0:1], turned[0:1], total[1:2], turned[1:2]], 0)
    for cell in range(8):
        x, y, z = cell // 4, cell // 2 % 2, cell % 2
        here = total if cell == 0 else pltpu.roll(total, 128 - 8 * cell, 1)
        energy_ref[x, y, z : z + 1] = here[0:1, 0:8]
        for d in range(3):
            force_ref[x, y, d, z : z + 1] = -here[1 + d : 2 + d, 0:8]


def call(kernel, out, *operands, micros=10, room=48):
    cost = pl.CostEstimate(flops=micros * 10**8, bytes_accessed=micros * 3 * 10**5, transcendentals=0)
    return pl.pallas_call(
        kernel,
        out_shape=[jax.ShapeDtypeStruct(shape, F32) for shape in out],
        compiler_params=pltpu.CompilerParams(vmem_limit_bytes=room * 1024 * 1024),
        cost_estimate=cost,
    )(*operands)


def moved(value, axes, *steps):
    counts = [lax.axis_size(axis) for axis in axes]
    pairs = []
    for source in range(math.prod(counts)):
        rest, target, stride = source, 0, 1
        for count, step in zip(counts[::-1], steps[::-1]):
            target += (rest + step) % count * stride
            rest, stride = rest // count, stride * count
        pairs.append((source, target))
    return lax.ppermute(value, axes, pairs)


def body(
    features, offsets, counts, species, neighbours,
    w_radial, w_vector, w_mix, w_out, w_charge, species_shift,
):
    cells_x, cells_y, cells_z, slots_cell, channels = features.shape
    grid = (
        cells_x * lax.axis_size("gx"),
        cells_y * lax.axis_size("gy"),
        cells_z * lax.axis_size("gz"),
    )
    scale = 1.0 / math.sqrt(grid[0] * grid[1] * grid[2] * slots_cell * MODES)
    held = (
        features.reshape(64, 128),
        jnp.transpose(offsets, (0, 1, 3, 2, 4)),
        counts,
        neighbours.reshape(64, 32),
        w_charge.T,
        w_out.reshape(1, 128),
        species_shift.reshape(1, 8),
    )
    slab, rest, extra, message = pl.pallas_call(
        pack_kernel,
        out_shape=[
            jax.ShapeDtypeStruct(shape, F32)
            for shape in [(104, 128), (32, 128), (8, 128), (32, 5, 2, 128)]
        ],
        in_specs=[pl.BlockSpec(memory_space=pl.ANY)] * len(held),
        scratch_shapes=[pltpu.VMEM(value.shape, value.dtype) for value in held]
        + [pltpu.SemaphoreType.DMA((len(held),))],
        compiler_params=pltpu.CompilerParams(vmem_limit_bytes=PACK_ROOM * 1024 * 1024),
    )(*held)
    in_x = moved(slab, ("gx",), -1)
    atoms = lax.all_to_all(message, ("gy", "gz"), 0, 0).reshape(320, 128)
    (to_z,) = call(stack_z_kernel, [(176, 128)], slab, rest, in_x, micros=STACK_Z_MICROS)
    in_z = moved(to_z, ("gz",), -1)
    (to_y,) = call(
        stack_y_kernel, [(320, 128)], slab, rest, in_x, in_z, micros=STACK_Y_MICROS
    )
    in_y = moved(to_y, ("gy",), -1)
    partial, phases, charges = call(
        functools.partial(waves_kernel, grid),
        [(16, 8, 128), (64, 2048), (16, 2048)],
        atoms,
        micros=WAVES_MICROS,
    )
    sums = lax.all_to_all(partial, "gx", 0, 0)
    kept, sent = call(
        short_kernel,
        [(8, 128), (8, 128)],
        slab, rest, in_x, in_z, in_y, extra,
        w_radial, w_vector, w_mix, species,
        micros=SHORT_MICROS,
    )
    came = moved(sent, ("gx",), 1)
    (parts,) = call(
        functools.partial(field_kernel, grid, scale),
        [(32, 2, 128)],
        sums, phases, charges,
        micros=FIELD_MICROS,
    )
    (parts,) = call(fold_kernel, [(32, 2, 128)], parts, kept, came)
    parts = lax.all_to_all(parts, ("gy", "gz"), 0, 0).reshape(64, 128)
    atom_energy, forces = call(last_kernel, [(2, 2, 2, 8), (2, 2, 3, 2, 8)], parts, room=LAST_ROOM)
    return (atom_energy, jnp.transpose(forces, (0, 1, 3, 2, 4)))


def solution(mesh):
    spread = P("gx", "gy", "gz")
    in_specs = (spread,) * 5 + (P(),) * 6
    return jax.shard_map(
        body, mesh=mesh, in_specs=in_specs, out_specs=(spread, spread), check_vma=False
    )
```

```python
import functools
import math

import jax
import jax.numpy as jnp
from jax import lax
from jax.experimental import pallas as pl
from jax.experimental.pallas import tpu as pltpu
from jax.sharding import PartitionSpec as P

KX = 16
KY = 8
KZ = 8
MODES = KX * KY * KZ
HIGH = lax.Precision.HIGHEST
F32 = jnp.float32
BF16 = jnp.bfloat16
STACK_Z_MICROS = 50
STACK_Y_MICROS = 1
WAVES_MICROS = 500
FIELD_MICROS = 50
SHORT_MICROS = 1
PACK_ROOM = 55
LAST_ROOM = 48


def iota(shape, dim):
    return lax.broadcasted_iota(jnp.int32, shape, dim)


def split(value):
    high = value.astype(BF16)
    low = (value - high.astype(F32)).astype(BF16)
    return high, low


def contract(left, right, dims, precision=None):
    return lax.dot_general(
        left, right, (dims, ((), ())), precision=precision, preferred_element_type=F32
    )


def split_left(value):
    high, low = split(value)
    return jnp.concatenate([high, low, high], 1)


def split_right(value, axis):
    high, low = split(value)
    return jnp.concatenate([high, high, low], axis)


def swap_halves(value):
    return pltpu.roll(value, 64, value.ndim - 1)


def position_rows(pos_ref, lane):
    pieces = [pos_ref[x, y, d] for x in range(2) for y in range(2) for d in range(3)]
    spread = (iota((8, 128), 1) % 8 == iota((8, 128), 0)).astype(F32)
    pieces = jnp.concatenate(pieces, 0)
    first, rest = split(pieces)
    last = (pieces - first.astype(F32) - rest.astype(F32)).astype(BF16)
    wide = contract(
        jnp.concatenate([first, rest, last], 1),
        jnp.concatenate([spread] * 3, 0).astype(BF16),
        (((1,), (0,))),
    )
    rows = []
    for d in range(3):
        row = jnp.zeros((1, 128), F32)
        for cell in range(8):
            at = (cell // 2) * 6 + d * 2 + cell % 2
            row = jnp.where(lane[0:1] // 8 == cell, wide[at : at + 1], row)
        rows.append(row)
    return jnp.concatenate(rows + [jnp.zeros((5, 128), F32)], 0)


def pack_kernel(
    feat_hbm, pos_hbm, count_hbm, near_hbm, charge_hbm, weight_hbm, shift_hbm,
    slab_ref, rest_ref, extra_ref, message_ref,
    feat_ref, pos_ref, count_ref, near_ref, charge_ref, weight_ref, shift_ref, arrived,
):
    copies = [
        pltpu.make_async_copy(source, target, arrived.at[at])
        for at, (source, target) in enumerate(
            (
                (feat_hbm, feat_ref), (pos_hbm, pos_ref), (count_hbm, count_ref),
                (near_hbm, near_ref), (charge_hbm, charge_ref), (weight_hbm, weight_ref),
                (shift_hbm, shift_ref),
            )
        )
    ]
    for copy in copies:
        copy.start()
    for copy in copies:
        copy.wait()
    extra_ref[...] = jnp.zeros((8, 128), F32)
    extra_ref[0:1] = weight_ref[...]
    extra_ref[1:2, 0:8] = shift_ref[...]
    row = iota((64, 128), 0)
    lane = iota((8, 128), 1)
    count_col = jnp.zeros((64, 128), jnp.int32)
    count_row = jnp.zeros((8, 128), jnp.int32)
    for cell in range(8):
        count = count_ref[cell // 4][cell // 2 % 2 : cell // 2 % 2 + 1, cell % 2 : cell % 2 + 1]
        count_col = jnp.where(row // 8 == cell, count, count_col)
        count_row = jnp.where(lane // 8 == cell, count, count_row)
    occupied = (row % 8 < count_col).astype(F32)
    occupied_row = (lane % 8 < count_row).astype(F32)
    masked = feat_ref[...] * occupied
    charges = contract(
        split_left(charge_ref[...]),
        split_right(jnp.concatenate([masked, masked], 0), 1),
        (((1,), (1,))),
    )
    sub = iota((8, 128), 0)
    tile = position_rows(pos_ref, lane)
    tile = jnp.where(sub == 3, occupied_row, tile)
    cell_x, cell_y, cell_z = lane // 32 % 2, lane // 16 % 2, lane // 8 % 2
    corner_x = 2 * lax.axis_index("gx")
    corner_y = 2 * lax.axis_index("gy")
    corner_z = 2 * lax.axis_index("gz")
    corner = jnp.where(
        sub == 0, cell_x + corner_x, jnp.where(sub == 1, cell_y + corner_y, cell_z + corner_z)
    )
    places = tile + corner.astype(F32)
    lane_low = lane < 64
    charges = jnp.where(lane_low, charges[0:8], charges[8:16])
    places = jnp.where(lane_low, places, swap_halves(pltpu.roll(places, 7, 0)))
    places = jnp.concatenate([places[0:1], places[2:3]], 0)
    pieces = [charges[2 * k : 2 * k + 2] for k in range(4)] + [places]
    for member in range(message_ref.shape[0]):
        for k in range(5):
            message_ref[member, k] = pieces[k]
    turned = jnp.concatenate(
        [jnp.zeros((32, 128), F32), tile, jnp.zeros((88, 128), F32)], 0
    ).T
    near = near_ref[...].astype(F32)
    slab_ref[0:64] = masked
    slab_ref[64:72] = tile
    slab_ref[72:104] = turned[0:32]
    slab_ref[72:104, 0:32] = near[0:32]
    rest_ref[...] = turned[32:64]
    rest_ref[:, 0:32] = near[32:64]


def stack_z_kernel(own_ref, rest_ref, in_x_ref, out_ref):
    out_ref[0:72] = own_ref[0:72]
    out_ref[72:144] = in_x_ref[0:72]
    out_ref[144:152] = rest_ref[0:8]
    out_ref[152:160] = rest_ref[16:24]
    out_ref[160:168] = in_x_ref[72:80]
    out_ref[168:176] = in_x_ref[88:96]


def stack_y_kernel(own_ref, rest_ref, in_x_ref, in_z_ref, out_ref):
    out_ref[0:72] = own_ref[0:72]
    out_ref[72:144] = in_x_ref[0:72]
    out_ref[144:288] = in_z_ref[0:144]
    out_ref[288:296] = rest_ref[8:16]
    out_ref[296:304] = in_x_ref[80:88]
    out_ref[304:312] = in_z_ref[144:152]
    out_ref[312:320] = in_z_ref[160:168]


def wave_numbers(member, shape, dim):
    index = iota(shape, dim) % 32
    number_y = (index // 8 + (member % 2) * 4 - KY // 2).astype(F32)
    number_z = (index % 8 - KZ // 2).astype(F32)
    number_x = (member // 2 - KX // 2).astype(F32)
    return number_x, number_y, number_z


def sine_cosine(turns):
    part = turns - jnp.floor(turns + 0.5)
    angle = part * (2.0 * math.pi)
    square = angle * angle
    sine = jnp.full_like(square, 1.0 / math.factorial(19) * -1.0)
    for power in range(17, 0, -2):
        sign = 1.0 if power // 2 % 2 == 0 else -1.0
        sine = sine * square + sign / math.factorial(power)
    cosine = jnp.full_like(square, -1.0 / math.factorial(18))
    for power in range(16, -1, -2):
        sign = 1.0 if power // 2 % 2 == 0 else -1.0
        cosine = cosine * square + sign / math.factorial(power)
    return sine * angle, cosine


def waves_kernel(grid, atoms_ref, message_ref, phase_ref, charge_ref):
    member = lax.axis_index("gy") * 4 + lax.axis_index("gz")
    low = iota((8, 128), 1) < 64
    upper, lower, places = [], [], []
    for pair in range(16):
        first, second = atoms_ref[20 * pair : 20 * pair + 8], atoms_ref[20 * pair + 10 : 20 * pair + 18]
        upper.append(jnp.where(low, first, swap_halves(second)))
        lower.append(jnp.where(low, swap_halves(first), second))
        first, second = (
            atoms_ref[20 * pair + 8 : 20 * pair + 10],
            atoms_ref[20 * pair + 18 : 20 * pair + 20],
        )
        places.append(
            jnp.concatenate(
                [
                    jnp.where(low[0:2], first, swap_halves(second)),
                    jnp.where(low[0:2], swap_halves(first), second),
                ],
                0,
            )
        )
    charges = jnp.concatenate(
        [jnp.concatenate(upper, 1), jnp.concatenate(lower, 1)], 0
    )
    places = jnp.concatenate(places, 1)
    row = iota((16, 1), 0)
    along_z = jnp.where(row < 8, (row - KZ // 2).astype(F32), 0.0)
    along_y = (row - 8 + (member % 2) * 4 - KY // 2).astype(F32)
    along_y = jnp.where((row >= 8) & (row < 12), along_y, 0.0)
    along_x = jnp.where(row == 12, (member // 2 - KX // 2).astype(F32), 0.0)
    turns = (
        along_x * (places[0:1] * (1.0 / grid[0]))
        + along_y * (places[2:3] * (1.0 / grid[1]))
        + along_z * (places[1:2] * (1.0 / grid[2]))
    )
    sine, cosine = sine_cosine(turns)
    sine_z, cosine_z = sine[0:8], cosine[0:8]
    sine_x, cosine_x = sine[12:13], cosine[12:13]
    flat_sine = sine_x * cosine[8:12] + cosine_x * sine[8:12]
    flat_cosine = cosine_x * cosine[8:12] - sine_x * sine[8:12]
    sines, cosines = [], []
    for k in range(4):
        sine_xy, cosine_xy = flat_sine[k : k + 1], flat_cosine[k : k + 1]
        sines.append(sine_xy * cosine_z + cosine_xy * sine_z)
        cosines.append(cosine_xy * cosine_z - sine_xy * sine_z)
    sine, cosine = jnp.concatenate(sines, 0), jnp.concatenate(cosines, 0)
    phases = jnp.concatenate([cosine, sine], 0)
    phase_ref[...] = phases
    charge_ref[...] = charges
    charge_stack = jnp.concatenate(split(charges), 0)
    phase_stack = jnp.concatenate(split(phases), 0)
    sums = contract(charge_stack, phase_stack, (((1,), (1,))))
    partial = sums[0:16] + sums[16:32]
    partial = partial + swap_halves(partial)
    partial = jnp.where(low, partial[0:8], partial[8:16])
    for other in range(message_ref.shape[0]):
        message_ref[other] = partial


def field_kernel(grid, scale, sums_ref, phase_ref, charge_ref, out_ref):
    at_y, at_z = lax.axis_index("gy"), lax.axis_index("gz")
    member = at_y * 4 + at_z
    total = sums_ref[0]
    for other in range(1, sums_ref.shape[0]):
        total = total + sums_ref[other]
    turned = swap_halves(total)
    low_lane = iota((8, 128), 1) < 64
    total = jnp.concatenate(
        [
            jnp.where(low_lane, total[0:8], turned[0:8]),
            jnp.where(low_lane, turned[0:8], total[0:8]),
        ],
        0,
    )
    two_pi = 2.0 * math.pi
    number_x, number_y, number_z = wave_numbers(member, (16, 128), 1)
    wave_x, wave_y, wave_z = (
        number_x * (two_pi / grid[0]),
        number_y * (two_pi / grid[1]),
        number_z * (two_pi / grid[2]),
    )
    length_sq = wave_x * wave_x + wave_y * wave_y + wave_z * wave_z
    total = total * (jnp.exp(-0.5 * length_sq) / (length_sq + 1.0))
    high = total.astype(BF16).astype(F32)
    low = total - high
    left = jnp.concatenate([high, low, high, jnp.zeros((80, 128), F32)], 0).T[0:64, 0:64]
    charge_high, charge_low = split(charge_ref[...])
    right = jnp.concatenate(
        [charge_high, charge_high, charge_low, jnp.zeros_like(charge_low)], 0
    )
    fields = contract(left.astype(BF16), right, (((1,), (0,))))
    cosine, sine = phase_ref[0:32], phase_ref[32:64]
    field_cos, field_sin = fields[0:32], fields[32:64]
    energy = (0.5 * scale) * jnp.sum(cosine * field_cos + sine * field_sin, 0, keepdims=True)
    turning = scale * (cosine * field_sin - sine * field_cos)
    number_x, number_y, number_z = wave_numbers(member, (32, 1), 0)
    pull_x = (number_x * (two_pi / grid[0])) * jnp.sum(turning, 0, keepdims=True)
    pull_y = jnp.sum(turning * (number_y * (two_pi / grid[1])), 0, keepdims=True)
    pull_z = jnp.sum(turning * (number_z * (two_pi / grid[2])), 0, keepdims=True)
    first = jnp.concatenate([energy, pull_y], 0)
    second = jnp.concatenate([pull_x, pull_z], 0)
    low = iota((2, 128), 1) < 64
    for pair in range(16):
        lanes = slice(128 * pair, 128 * pair + 128)
        left_part, right_part = first[:, lanes], second[:, lanes]
        out_ref[2 * pair] = jnp.where(low, left_part, swap_halves(right_part))
        out_ref[2 * pair + 1] = jnp.where(low, swap_halves(left_part), right_part)


def fold_kernel(parts_ref, kept_ref, came_ref, out_ref):
    at_y, at_z = lax.axis_index("gy"), lax.axis_index("gz")
    folded = kept_ref[...] + came_ref[...]
    turned = swap_halves(folded)
    low = iota((2, 128), 1) < 64
    out_ref[...] = parts_ref[...]
    for block in range(4):
        by, bz = block % 2, block // 2
        to = ((at_y + by) % 8) * 4 + (at_z + bz) % 4
        here, there = (folded, turned) if by == 0 else (turned, folded)
        row = 4 * bz
        piece = jnp.where(
            low,
            jnp.concatenate([here[row : row + 1], here[row + 2 : row + 3]], 0),
            jnp.concatenate([there[row + 1 : row + 2], there[row + 3 : row + 4]], 0),
        )
        out_ref[to] = out_ref[to] + piece


def short_kernel(
    own_ref, rest_ref, in_x_ref, in_z_ref, in_y_ref, extra_ref,
    radial_ref, vector_ref, mix_ref, species_ref, kept_ref, sent_ref,
):
    bases = [
        (own_ref, 0), (in_x_ref, 0), (in_y_ref, 0), (in_y_ref, 72),
        (in_z_ref, 0), (in_z_ref, 72), (in_y_ref, 144), (in_y_ref, 216),
    ]

    def local_row(x, y, z):
        return (x % 2 * 4 + y % 2 * 2 + z % 2) * 8

    def block_of(x, y, z):
        return z // 2 * 4 + y // 2 * 2 + x // 2

    def cell_tile(x, y, z):
        ref, at = bases[block_of(x, y, z)]
        at = at + local_row(x, y, z)
        return ref[at : at + 8]

    units = [(x, y, z) for z in (1, 2) for y in (1, 2) for x in (1, 2)]
    steps = [(dx, dy, dz) for dx in range(3) for dy in range(3) for dz in range(3)]
    centres = [
        rest_ref[24:32], in_x_ref[96:104], in_y_ref[288:296], in_y_ref[296:304],
        in_z_ref[152:160], in_z_ref[168:176], in_y_ref[304:312], in_y_ref[312:320],
    ]
    centres = jnp.concatenate(centres, 0)
    own = jnp.concatenate([cell_tile(*unit) for unit in units], 0)
    occupied = centres[:, 35:36]
    group = iota((8, 128), 1) // 8
    group_long = iota((64, 128), 1) // 8
    rows = [ref[at + 64 : at + 72] for ref, at in bases]
    columns = jnp.concatenate(rows + [jnp.zeros((64, 128), F32)], 0).T[0:64]
    copies = []
    for block in range(8):
        wide = jnp.where(group_long == block, columns, 0.0)
        for shift in (8, 16, 32, 64):
            wide = wide + pltpu.roll(wide, shift, 1)
        copies.append(wide)
    tiles = []
    for dx, dy, dz in steps:
        tile = jnp.zeros((8, 128), F32)
        for unit, (x, y, z) in enumerate(units):
            tx, ty, tz = x - 1 + dx, y - 1 + dy, z - 1 + dz
            row = local_row(tx, ty, tz)
            tile = jnp.where(group == unit, copies[block_of(tx, ty, tz)][row : row + 8], tile)
        tiles.append(tile)
    spots = jnp.concatenate(tiles + [jnp.zeros((40, 128), F32)], 0).T
    stencil = iota((1, 256), 1) // 8
    crossing = (stencil // 9 - 1, stencil // 3 % 3 - 1, stencil % 3 - 1)
    delta = []
    for a in range(3):
        spread = jnp.concatenate(
            [
                jnp.broadcast_to(spots[8 * unit + a : 8 * unit + a + 1], (8, 256))
                for unit in range(8)
            ],
            0,
        )
        delta.append(crossing[a].astype(F32) + spread - centres[:, 32 + a : 33 + a])
    dist_sq = delta[0] * delta[0] + delta[1] * delta[1] + delta[2] * delta[2]
    near = 1.0 - dist_sq * (1.0 / 16.0)
    envelope = near * near
    lane_f = iota((64, 256), 1).astype(F32)
    times = jnp.zeros((64, 256), F32)
    for entry in range(32):
        times = times + jnp.where(centres[:, entry : entry + 1] == lane_f, 1.0, 0.0)
    bases_m = []
    power = None
    for b in range(8):
        if b % 4 == 0:
            power = jnp.exp(dist_sq * (-(2.0 ** (b - 4))))
        else:
            power = power * power
        bases_m.append(power * times)
    norm = 1.0 / math.sqrt(32.0)
    windows = []
    sums = [[], [], [], []]
    for unit, (x, y, z) in enumerate(units):
        window = jnp.concatenate(
            [cell_tile(x - 1 + dx, y - 1 + dy, z - 1 + dz) for dx, dy, dz in steps]
            + [jnp.zeros((40, 128), F32)],
            0,
        )
        high, low = split(window)
        windows.append((high, low))
        at = slice(8 * unit, 8 * unit + 8)
        left = []
        for b in range(8):
            weight = bases_m[b][at] * envelope[at]
            left += [weight] + [weight * delta[a][at] for a in range(3)]
        left_high, left_low = split(jnp.concatenate(left, 0))
        made = contract(
            jnp.concatenate([left_high, left_low], 0),
            jnp.concatenate([high, low], 1),
            (((1,), (0,))),
        )
        made = made[0:256, 0:128] + made[0:256, 128:256] + made[256:512, 0:128]
        for part in range(4):
            weights = radial_ref if part == 0 else vector_ref
            total = made[8 * part : 8 * part + 8] * weights[0:1]
            for b in range(1, 8):
                row = 8 * (4 * b + part)
                total = total + made[row : row + 8] * weights[b : b + 1]
            sums[part].append(total)
    sums = [jnp.concatenate(part, 0) * norm for part in sums]
    product = sums[0] + sums[1] * sums[1] + sums[2] * sums[2] + sums[3] * sums[3]
    mixed = contract(split_left(product), split_right(mix_ref[...], 0), (((1,), (0,))))
    gate = 1.0 / (1.0 + jnp.exp(-mixed))
    out_weight = extra_ref[0:1]
    energy = jnp.sum((own + mixed * gate) * out_weight, 1, keepdims=True) * occupied
    slope = gate * (1.0 + mixed * (1.0 - gate)) * (out_weight * occupied)
    grad = contract(split_left(slope), split_right(mix_ref[...], 1), (((1,), (1,)))) * norm
    grads = [grad] + [2.0 * grad * sums[1 + a] for a in range(3)]
    sub = iota((8, 256), 0)
    column = iota((8, 128), 1)
    pushes, ends = [], {}
    for unit, spot in enumerate(units):
        at = slice(8 * unit, 8 * unit + 8)
        left = []
        for b in range(8):
            left.append(grads[0][at] * radial_ref[b : b + 1])
            left += [grads[1 + a][at] * vector_ref[b : b + 1] for a in range(3)]
        high, low = windows[unit]
        pulled = contract(
            split_left(jnp.concatenate(left, 0)),
            jnp.concatenate([high, high, low], 1),
            (((1,), (1,))),
        )
        linear = [jnp.zeros((8, 256), F32) for _ in range(3)]
        plain = jnp.zeros((8, 256), F32)
        decayed = jnp.zeros((8, 256), F32)
        here = [delta[a][at] for a in range(3)]
        for b in range(8):
            parts = [pulled[32 * b + 8 * part : 32 * b + 8 * part + 8] for part in range(4)]
            full = parts[0] + parts[1] * here[0] + parts[2] * here[1] + parts[3] * here[2]
            basis = bases_m[b][at]
            weighted = basis * full
            plain = plain + weighted
            decayed = decayed + weighted * (2.0 ** (b - 4))
            for a in range(3):
                linear[a] = linear[a] + basis * parts[1 + a]
        radial_slope = 2.0 * (near[at] * (-0.125) * plain - envelope[at] * decayed)
        gathered = jnp.zeros((8, 256), F32)
        end = jnp.where(column == 0, energy[at], 0.0)
        for a in range(3):
            push = envelope[at] * linear[a] + here[a] * radial_slope
            gathered = jnp.where(sub == 1 + a, jnp.sum(push, 0, keepdims=True), gathered)
            end = jnp.where(column == 1 + a, -jnp.sum(push, 1, keepdims=True), end)
        pushes.append(gathered)
        ends[spot] = end
    pushes = jnp.concatenate(pushes + [jnp.zeros((64, 256), F32)], 0).T
    folded = []
    for block in range(8):
        for local in range(8):
            x = block % 2 * 2 + local // 4
            y = block // 2 % 2 * 2 + local // 2 % 2
            z = block // 4 * 2 + local % 2
            total = ends.get((x, y, z), jnp.zeros((8, 128), F32))
            for unit, (ux, uy, uz) in enumerate(units):
                step = (x - ux + 1, y - uy + 1, z - uz + 1)
                if step in steps:
                    row = 8 * steps.index(step)
                    total = total + jnp.where(group == unit, pushes[row : row + 8], 0.0)
            folded.append(total)
    folded = jnp.concatenate(folded, 0).T
    rows = folded[0:8]
    for unit in range(1, 8):
        rows = rows + folded[8 * unit : 8 * unit + 8]
    rows = rows[0:4]
    kinds = [species_ref[x, y] for x in range(2) for y in range(2)]
    spread = (iota((8, 128), 1) % 8 == iota((8, 128), 0)).astype(F32)
    kinds = contract(jnp.concatenate(kinds, 0).astype(F32), spread, (((1,), (0,))))
    shift = jnp.zeros((8, 128), F32)
    for name in range(8):
        shift = jnp.where(kinds == float(name), extra_ref[1:2, name : name + 1], shift)
    mine = iota((8, 128), 1) // 8 == iota((8, 128), 0)
    shift = jnp.sum(jnp.where(mine, shift, 0.0), 0, keepdims=True) * own_ref[67:68]
    shift = jnp.where(iota((4, 128), 0) == 0, shift, 0.0)
    low = iota((4, 128), 1) < 64
    for half in range(2):
        first, second = (rows[:, 128 * k : 128 * k + 128] for k in (2 * half, 2 * half + 1))
        first = first + shift if half == 0 else first
        kept_ref[4 * half : 4 * half + 4] = jnp.where(low, first, swap_halves(second))
        sent_ref[4 * half : 4 * half + 4] = jnp.where(low, swap_halves(first), second)


def last_kernel(parts_ref, energy_ref, force_ref):
    total = parts_ref[0:8]
    for at in range(8, 64, 8):
        total = total + parts_ref[at : at + 8]
    total = total + pltpu.roll(total, 4, 0)
    total = total + pltpu.roll(total, 2, 0)
    turned = swap_halves(total)
    total = jnp.concatenate([total[0:1], turned[0:1], total[1:2], turned[1:2]], 0)
    for cell in range(8):
        x, y, z = cell // 4, cell // 2 % 2, cell % 2
        here = total if cell == 0 else pltpu.roll(total, 128 - 8 * cell, 1)
        energy_ref[x, y, z : z + 1] = here[0:1, 0:8]
        for d in range(3):
            force_ref[x, y, d, z : z + 1] = -here[1 + d : 2 + d, 0:8]


def call(kernel, out, *operands, micros=10, room=48):
    cost = pl.CostEstimate(flops=micros * 10**8, bytes_accessed=micros * 3 * 10**5, transcendentals=0)
    return pl.pallas_call(
        kernel,
        out_shape=[jax.ShapeDtypeStruct(shape, F32) for shape in out],
        compiler_params=pltpu.CompilerParams(vmem_limit_bytes=room * 1024 * 1024),
        cost_estimate=cost,
    )(*operands)


def moved(value, axes, *steps):
    counts = [lax.axis_size(axis) for axis in axes]
    pairs = []
    for source in range(math.prod(counts)):
        rest, target, stride = source, 0, 1
        for count, step in zip(counts[::-1], steps[::-1]):
            target += (rest + step) % count * stride
            rest, stride = rest // count, stride * count
        pairs.append((source, target))
    return lax.ppermute(value, axes, pairs)


def body(
    features, offsets, counts, species, neighbours,
    w_radial, w_vector, w_mix, w_out, w_charge, species_shift,
):
    cells_x, cells_y, cells_z, slots_cell, channels = features.shape
    grid = (
        cells_x * lax.axis_size("gx"),
        cells_y * lax.axis_size("gy"),
        cells_z * lax.axis_size("gz"),
    )
    scale = 1.0 / math.sqrt(grid[0] * grid[1] * grid[2] * slots_cell * MODES)
    held = (
        features.reshape(64, 128),
        jnp.transpose(offsets, (0, 1, 3, 2, 4)),
        counts,
        neighbours.reshape(64, 32),
        w_charge.T,
        w_out.reshape(1, 128),
        species_shift.reshape(1, 8),
    )
    slab, rest, extra, message = pl.pallas_call(
        pack_kernel,
        out_shape=[
            jax.ShapeDtypeStruct(shape, F32)
            for shape in [(104, 128), (32, 128), (8, 128), (32, 5, 2, 128)]
        ],
        in_specs=[pl.BlockSpec(memory_space=pl.ANY)] * len(held),
        scratch_shapes=[pltpu.VMEM(value.shape, value.dtype) for value in held]
        + [pltpu.SemaphoreType.DMA((len(held),))],
        compiler_params=pltpu.CompilerParams(vmem_limit_bytes=PACK_ROOM * 1024 * 1024),
    )(*held)
    in_x = moved(slab, ("gx",), -1)
    atoms = lax.all_to_all(message, ("gy", "gz"), 0, 0).reshape(320, 128)
    (to_z,) = call(stack_z_kernel, [(176, 128)], slab, rest, in_x, micros=STACK_Z_MICROS)
    in_z = moved(to_z, ("gz",), -1)
    (to_y,) = call(
        stack_y_kernel, [(320, 128)], slab, rest, in_x, in_z, micros=STACK_Y_MICROS
    )
    in_y = moved(to_y, ("gy",), -1)
    partial, phases, charges = call(
        functools.partial(waves_kernel, grid),
        [(16, 8, 128), (64, 2048), (16, 2048)],
        atoms,
        micros=WAVES_MICROS,
    )
    sums = lax.all_to_all(partial, "gx", 0, 0)
    kept, sent = call(
        short_kernel,
        [(8, 128), (8, 128)],
        slab, rest, in_x, in_z, in_y, extra,
        w_radial, w_vector, w_mix, species,
        micros=SHORT_MICROS,
    )
    came = moved(sent, ("gx",), 1)
    (parts,) = call(
        functools.partial(field_kernel, grid, scale),
        [(32, 2, 128)],
        sums, phases, charges,
        micros=FIELD_MICROS,
    )
    (parts,) = call(fold_kernel, [(32, 2, 128)], parts, kept, came)
    parts = lax.all_to_all(parts, ("gy", "gz"), 0, 0).reshape(64, 128)
    atom_energy, forces = call(last_kernel, [(2, 2, 2, 8), (2, 2, 3, 2, 8)], parts, room=LAST_ROOM)
    return (atom_energy, jnp.transpose(forces, (0, 1, 3, 2, 4)))


def solution(mesh):
    spread = P("gx", "gy", "gz")
    in_specs = (spread,) * 5 + (P(),) * 6
    return jax.shard_map(
        body, mesh=mesh, in_specs=in_specs, out_specs=(spread, spread), check_vma=False
    )
```
